32 devices in a mesh: lat: 4 (over x, core), lon: 8 (over z, y).
Axes of the slice: x: 2, y: 2, z: 4, core: 2. Of those that a mesh axis runs over, the one named last changes fastest.
Arguments:
- student: bfloat16 [2, 16, 256, 256], P(None, 'lat', 'lon'), may hold values from -6 to 6
- teacher: bfloat16 [2, 16, 256, 256], P(None, None, ('lon', 'lat')), may hold values from -6 to 6
- dw_weight: float32 [7, 7, 256], replicated, may hold values from -0.875 to 0.875
- norm_gain: float32 [256], replicated, may hold values from 0.1 to 1.9
- w_in: bfloat16 [256, 1024], replicated, may hold values from -0.375 to 0.375
- w_out: bfloat16 [1024, 256], replicated, may hold values from -0.1875 to 0.1875
- layer_scale: float32 [256], replicated, may hold values from 0.3 to 1.5
Outputs:
- grad_student: bfloat16 [2, 16, 256, 256], P(None, 'lat', 'lon')
- grad_w_in: float32 [256, 1024], replicated
- grad_w_out: float32 [1024, 256], replicated
- grad_dw: float32 [7, 7, 256], replicated
The draws below stay inside these ranges and needn't reach their ends.
All inputs are finite; a program needn't handle non-finite values.
Results may differ from the reference program's by a relative error of at most 0.0034.
The reference program's roundings to bfloat16 on the way (of `normed`, `hidden`, `out_grad`, `preact_grad` and `conv_grad`) count: a program that leaves them out, or rounds other values in their place, can miss the bound.
Values may be sent and summed in bfloat16 or wider, within the bound.
No kernel may reach another device: no remote copies, remote signals or barrier semaphores. Data moves between devices by JAX's collectives and lax.ppermute only.
A program may use at most 64 MiB of HBM per device.

```python
import math
import jax
import jax.numpy as jnp
from jax import lax

BATCH = 2
CHANNELS = 256
HIDDEN_SIZE = 1024
KERNEL = 7
NLAT = 16
NLON = 256
CELLS = 8192


def block_levels(stream_key, shape, cuts, least, top_value):
    factor_of = 1.0
    for position, shards_of in cuts:
        steps = jax.random.uniform(jax.random.fold_in(jax.random.fold_in(stream_key, 6), position), (shards_of,), jnp.float32, least / len(cuts), top_value / len(cuts))
        factor_of = factor_of * jnp.repeat(jnp.exp(steps), shape[position] // shards_of).reshape((-1,) + (1,) * (len(shape) - 1 - position))
    return factor_of


def noise(rng, extent, scale, most, cuts=(), held_as=jnp.bfloat16):
    values = jax.random.normal(rng, extent, jnp.float32) * scale
    if len(cuts) > 0:
        values = block_levels(rng, extent, cuts, -0.22, 0.18) * values
    return jnp.clip(values, min=-most, max=most).astype(held_as)


def setup_inputs(seed: int = 0) -> dict:
    key_of = jax.random.split(jax.random.key(seed), 8)
    student = noise(key_of[0], (BATCH, NLAT, NLON, CHANNELS), 1.0, 6.0, ((1, 4), (2, 8)))
    teacher = noise(key_of[1], (BATCH, NLAT, NLON, CHANNELS), 1.0, 6.0, ((2, 32),))
    dw_weight = noise(key_of[2], (KERNEL, KERNEL, CHANNELS), (KERNEL * KERNEL) ** -0.5, 0.875, (), jnp.float32)
    norm_gain = jnp.clip(1.0 + 0.18 * jax.random.normal(key_of[3], (CHANNELS,), jnp.float32), 0.1, 1.9)
    w_in = noise(key_of[4], (CHANNELS, HIDDEN_SIZE), CHANNELS ** -0.5, 0.375)
    w_out = noise(key_of[5], (HIDDEN_SIZE, CHANNELS), HIDDEN_SIZE ** -0.5, 0.1875)
    layer_scale = jnp.clip(jnp.exp(jax.random.uniform(key_of[6], (CHANNELS,), jnp.float32, math.log(0.3), math.log(1.5))), 0.3, 1.5)
    return dict(student=student, teacher=teacher, dw_weight=dw_weight, norm_gain=norm_gain, w_in=w_in, w_out=w_out, layer_scale=layer_scale)


slope_coef = 0.7978845608028654
cubic_coef = 0.044715
norm_eps = 1e-06

def gelu_tanh(values):
    tanh_arg = slope_coef * (values + cubic_coef * values * values * values)
    return 0.5 * values * (1.0 + jnp.tanh(tanh_arg))

def gelu_slope(values):
    tangent = jnp.tanh(slope_coef * (values + cubic_coef * values * values * values))
    return 0.5 * (1.0 + tangent) + 0.5 * values * (1.0 - tangent * tangent) * slope_coef * (1.0 + 3.0 * cubic_coef * values * values)

def forward_cells(smoothed, student_rows, norm_gain, w_in, w_out, layer_scale):
    average = lax.optimization_barrier(jnp.mean(smoothed, axis=-1, keepdims=True))
    centred = smoothed - average
    variance = lax.optimization_barrier(jnp.mean(centred * centred, axis=-1, keepdims=True))
    inv_std = lax.rsqrt(variance + norm_eps)
    unit_norm = centred * inv_std
    normed = (unit_norm * norm_gain).astype(jnp.bfloat16)
    preact = jnp.dot(normed, w_in, preferred_element_type=jnp.float32)
    hidden = gelu_tanh(preact).astype(jnp.bfloat16)
    mlp_out = jnp.dot(hidden, w_out, preferred_element_type=jnp.float32)
    output = student_rows.astype(jnp.float32) + layer_scale * mlp_out
    return (output, (normed, unit_norm, inv_std, preact, hidden))

def backward_cells(misfit, stored, norm_gain, w_in, w_out, layer_scale):
    normed, unit_norm, inv_std, preact, hidden = stored
    out_grad = (layer_scale * misfit).astype(jnp.bfloat16)
    part_out = lax.dot_general(hidden, out_grad, (((0,), (0,)), ((), ())), preferred_element_type=jnp.float32)
    hidden_grad = lax.dot_general(out_grad, w_out, (((1,), (1,)), ((), ())), preferred_element_type=jnp.float32)
    preact_grad = (hidden_grad * gelu_slope(preact)).astype(jnp.bfloat16)
    part_in = lax.dot_general(normed, preact_grad, (((0,), (0,)), ((), ())), preferred_element_type=jnp.float32)
    normed_grad = lax.dot_general(preact_grad, w_in, (((1,), (1,)), ((), ())), preferred_element_type=jnp.float32)
    unit_grad = normed_grad * norm_gain
    first_mean = lax.optimization_barrier(jnp.mean(unit_grad, axis=-1, keepdims=True))
    second_mean = lax.optimization_barrier(jnp.mean(unit_grad * unit_norm, axis=-1, keepdims=True))
    conv_grad = inv_std * (unit_grad - first_mean - unit_norm * second_mean)
    return (conv_grad.astype(jnp.bfloat16), part_in, part_out)

def extend_grid(field):
    half_kernel = KERNEL // 2
    lon_padded = jnp.concatenate([field[:, :, NLON - half_kernel:], field, field[:, :, :half_kernel]], axis=2)
    lon_padded = lon_padded.astype(jnp.float32)
    return jnp.pad(lon_padded, ((0, 0), (half_kernel, half_kernel), (0, 0), (0, 0)))

def reference(student, teacher, dw_weight, norm_gain, w_in, w_out, layer_scale):
    padded = extend_grid(student)
    smoothed = jnp.zeros((BATCH, NLAT, NLON, CHANNELS), jnp.float32)
    for row_off in range(KERNEL):
        for col_off in range(KERNEL):
            smoothed = smoothed + dw_weight[row_off, col_off] * padded[:, row_off:row_off + NLAT, col_off:col_off + NLON]

    def one_line(totals, pieces):
        smooth_line, student_line, teacher_line = pieces
        output, stored = forward_cells(smooth_line, student_line, norm_gain, w_in, w_out, layer_scale)
        misfit = output - teacher_line.astype(jnp.float32)
        conv_grad, part_in, part_out = backward_cells(misfit, stored, norm_gain, w_in, w_out, layer_scale)
        return ((totals[0] + part_in, totals[1] + part_out), (conv_grad, misfit))
    start_totals = (jnp.zeros((CHANNELS, HIDDEN_SIZE), jnp.float32), jnp.zeros((HIDDEN_SIZE, CHANNELS), jnp.float32))
    line_inputs = (smoothed.reshape(BATCH * NLAT, NLON, CHANNELS), student.reshape(BATCH * NLAT, NLON, CHANNELS), teacher.reshape(BATCH * NLAT, NLON, CHANNELS))
    (sum_in, sum_out), (conv_grad, misfit) = lax.scan(one_line, start_totals, line_inputs)
    conv_grad = conv_grad.reshape(BATCH, NLAT, NLON, CHANNELS)
    misfit = misfit.reshape(BATCH, NLAT, NLON, CHANNELS)
    padded_grad = extend_grid(conv_grad)
    conv_grad_f = conv_grad.astype(jnp.float32)
    back_conv = jnp.zeros((BATCH, NLAT, NLON, CHANNELS), jnp.float32)
    kernel_terms = []
    for row_off in range(KERNEL):
        for col_off in range(KERNEL):
            row_start = KERNEL - 1 - row_off
            col_start = KERNEL - 1 - col_off
            back_conv = back_conv + dw_weight[row_off, col_off] * padded_grad[:, row_start:row_start + NLAT, col_start:col_start + NLON]
            kernel_terms.append(lax.optimization_barrier(jnp.sum(padded[:, row_off:row_off + NLAT, col_off:col_off + NLON] * conv_grad_f, axis=(0, 1, 2))))
    grad_student = (misfit + back_conv).astype(jnp.bfloat16)
    grad_dw = jnp.stack(kernel_terms).reshape(KERNEL, KERNEL, CHANNELS) / CELLS
    return (grad_student, sum_in / CELLS, sum_out / CELLS, grad_dw)
```

```python
import jax
import jax.numpy as jnp
from jax import lax
from jax.sharding import PartitionSpec as P

slope_coef = 0.7978845608028654
cubic_coef = 0.044715
norm_eps = 1e-06


def with_halo(block, sides, width, periodic):
    for axis, dim in sides:
        count = lax.axis_size(axis)
        forward = [(i, i + 1) for i in range(count - 1)]
        if periodic:
            forward.append((count - 1, 0))
        backward = [(target, source) for source, target in forward]
        low = lax.ppermute(
            lax.slice_in_dim(block, block.shape[dim] - width, None, axis=dim), axis, forward
        )
        high = lax.ppermute(lax.slice_in_dim(block, 0, width, axis=dim), axis, backward)
        block = jnp.concatenate([low, block, high], axis=dim)
    return block


def gelu_tanh(values):
    tanh_arg = slope_coef * (values + cubic_coef * values * values * values)
    return 0.5 * values * (1.0 + jnp.tanh(tanh_arg))


def gelu_slope(values):
    tangent = jnp.tanh(slope_coef * (values + cubic_coef * values * values * values))
    return 0.5 * (1.0 + tangent) + 0.5 * values * (1.0 - tangent * tangent) * slope_coef * (
        1.0 + 3.0 * cubic_coef * values * values
    )


def apply_stencil(padded, dw_weight, tile_rows, tile_cols, flipped):
    kernel_size = dw_weight.shape[0]
    result = jnp.zeros((padded.shape[0], tile_rows, tile_cols, padded.shape[3]), jnp.float32)
    for row_off in range(kernel_size):
        for col_off in range(kernel_size):
            row_start = kernel_size - 1 - row_off if flipped else row_off
            col_start = kernel_size - 1 - col_off if flipped else col_off
            result = (
                result
                + dw_weight[row_off, col_off]
                * padded[:, row_start : row_start + tile_rows, col_start : col_start + tile_cols]
            )
    return result


def bits_of(axis):
    return [(axis, 1 << k) for k in range((lax.axis_size(axis) - 1).bit_length())]


def swap(value, axis, bit):
    return lax.ppermute(value, axis, [(i, i ^ bit) for i in range(lax.axis_size(axis))])


def rows_at(value, half, upper):
    return lax.dynamic_slice_in_dim(value, upper * half, half, axis=0)


def split_rows(value, counts):
    pieces, start = [], 0
    for count in counts:
        pieces.append(lax.slice_in_dim(value, start, start + count, axis=0))
        start += count
    return pieces


def sum_over_mesh(parts, divisor):
    lat_bits, lon_bits = bits_of("lat"), bits_of("lon")
    halving = lat_bits[:2] + lon_bits[:1]
    whole = lon_bits[1:] + lat_bits[2:]
    parts = list(parts)
    for axis, bit in halving:
        upper = (lax.axis_index(axis) & bit) // bit
        halves = [part.shape[0] // 2 for part in parts]
        sent = [rows_at(p, h, 1 - upper).astype(jnp.bfloat16) for p, h in zip(parts, halves)]
        got = swap(jnp.concatenate(sent, axis=0), axis, bit)
        parts = [
            rows_at(p, h, upper) + g.astype(jnp.float32)
            for p, h, g in zip(parts, halves, split_rows(got, halves))
        ]
    counts = [part.shape[0] for part in parts]
    total = jnp.concatenate(parts, axis=0)
    for axis, bit in whole:
        total = total + swap(total, axis, bit)
    parts = split_rows((total / divisor).astype(jnp.bfloat16), counts)
    for axis, bit in reversed(halving):
        upper = (lax.axis_index(axis) & bit) // bit
        counts = [part.shape[0] for part in parts]
        got = split_rows(swap(jnp.concatenate(parts, axis=0), axis, bit), counts)
        parts = [
            jnp.where(upper == 1, jnp.concatenate([g, p]), jnp.concatenate([p, g]))
            for p, g in zip(parts, got)
        ]
    return [part.astype(jnp.float32) for part in parts]


def local(student, teacher, dw_weight, norm_gain, w_in, w_out, layer_scale):
    batch_size, tile_rows, tile_cols, channel_count = student.shape
    kernel_size = dw_weight.shape[0]
    half_kernel = kernel_size // 2
    cell_total = batch_size * tile_rows * lax.axis_size("lat") * tile_cols * lax.axis_size("lon")
    lon_padded = with_halo(student, (("lon", 2),), half_kernel, True)
    padded_bf = with_halo(lon_padded, (("lat", 1),), half_kernel, False)
    padded = padded_bf.astype(jnp.float32)
    smoothed = apply_stencil(padded, dw_weight, tile_rows, tile_cols, False).reshape(
        -1, channel_count
    )
    average = jnp.mean(smoothed, axis=-1, keepdims=True)
    centred = smoothed - average
    variance = jnp.mean(centred * centred, axis=-1, keepdims=True)
    inv_std = lax.rsqrt(variance + norm_eps)
    unit_norm = centred * inv_std
    normed = (unit_norm * norm_gain).astype(jnp.bfloat16)
    preact = jnp.dot(normed, w_in, preferred_element_type=jnp.float32)
    hidden = gelu_tanh(preact).astype(jnp.bfloat16)
    mlp_out = jnp.dot(hidden, w_out, preferred_element_type=jnp.float32)
    output = student.reshape(-1, channel_count).astype(jnp.float32) + layer_scale * mlp_out
    target = lax.all_to_all(teacher, "lat", split_axis=1, concat_axis=2, tiled=True)
    misfit = output - target.reshape(-1, channel_count).astype(jnp.float32)
    out_grad = (layer_scale * misfit).astype(jnp.bfloat16)
    part_out = lax.dot_general(
        hidden, out_grad, (((0,), (0,)), ((), ())), preferred_element_type=jnp.float32
    )
    hidden_grad = lax.dot_general(
        out_grad, w_out, (((1,), (1,)), ((), ())), preferred_element_type=jnp.float32
    )
    preact_grad = (hidden_grad * gelu_slope(preact)).astype(jnp.bfloat16)
    part_in = lax.dot_general(
        normed, preact_grad, (((0,), (0,)), ((), ())), preferred_element_type=jnp.float32
    )
    normed_grad = lax.dot_general(
        preact_grad, w_in, (((1,), (1,)), ((), ())), preferred_element_type=jnp.float32
    )
    unit_grad = normed_grad * norm_gain
    first_mean = jnp.mean(unit_grad, axis=-1, keepdims=True)
    second_mean = jnp.mean(unit_grad * unit_norm, axis=-1, keepdims=True)
    conv_grad = (inv_std * (unit_grad - first_mean - unit_norm * second_mean)).astype(jnp.bfloat16)
    conv_grid = conv_grad.reshape(student.shape)
    grad_lon = with_halo(conv_grid, (("lon", 2),), half_kernel, True)
    padded_grad = with_halo(grad_lon, (("lat", 1),), half_kernel, False).astype(jnp.float32)
    back_conv = apply_stencil(padded_grad, dw_weight, tile_rows, tile_cols, True)
    grad_student = (misfit.reshape(student.shape) + back_conv).astype(jnp.bfloat16)
    conv_grad_f = conv_grid.astype(jnp.float32)
    kernel_terms = []
    for row_off in range(kernel_size):
        for col_off in range(kernel_size):
            kernel_terms.append(
                jnp.sum(
                    padded[:, row_off : row_off + tile_rows, col_off : col_off + tile_cols]
                    * conv_grad_f,
                    axis=(0, 1, 2),
                )
            )
    part_dw = jnp.stack(kernel_terms).reshape(kernel_size, kernel_size, channel_count)
    dw_rows = part_dw.reshape(-1, channel_count)
    hidden_size = part_in.shape[1]
    per_row = hidden_size // channel_count
    pad_rows = -dw_rows.shape[0] % (8 * per_row)
    dw_wide = jnp.pad(dw_rows, ((0, pad_rows), (0, 0))).reshape(-1, hidden_size)
    (sum_out,) = sum_over_mesh((part_out,), cell_total)
    sum_in, sum_dw = sum_over_mesh((part_in, dw_wide), cell_total)
    sum_dw = sum_dw.reshape(-1, channel_count)[: kernel_size * kernel_size]
    return (grad_student, sum_in, sum_out, sum_dw.reshape(dw_weight.shape))


def solution(mesh):
    placed = (
        P(None, "lat", "lon", None),
        P(None, None, ("lon", "lat"), None),
        P(),
        P(),
        P(),
        P(),
        P(),
    )
    return jax.shard_map(
        local,
        mesh=mesh,
        in_specs=placed,
        out_specs=(P(None, "lat", "lon", None), P(), P(), P()),
        check_vma=False,
    )
```

```python
import jax
import jax.numpy as jnp
from jax import lax
from jax.sharding import PartitionSpec as P

slope_coef = 0.7978845608028654
cubic_coef = 0.044715
norm_eps = 1e-06


def bits_of(axis):
    return [1 << k for k in range((lax.axis_size(axis) - 1).bit_length())]


def swap(value, axis, bit):
    return lax.ppermute(value, axis, [(i, i ^ bit) for i in range(lax.axis_size(axis))])


def with_halo(block, sides, width, periodic):
    for axis, dim in sides:
        count = lax.axis_size(axis)
        odd = lax.axis_index(axis) % 2
        inner = [(i, i ^ 1) for i in range(count)]
        outer = [(i, (i + 1) % count) for i in range(1, count, 2)]
        if not periodic:
            outer = [(i, j) for i, j in outer if j]
        outer = outer + [(j, i) for i, j in outer]
        low = lax.slice_in_dim(block, 0, width, axis=dim)
        high = lax.slice_in_dim(block, block.shape[dim] - width, None, axis=dim)
        from_outer = lax.ppermute(jnp.where(odd == 1, high, low), axis, outer)
        from_inner = lax.ppermute(jnp.where(odd == 1, low, high), axis, inner)
        before = jnp.where(odd == 1, from_inner, from_outer)
        after = jnp.where(odd == 1, from_outer, from_inner)
        block = jnp.concatenate([before, block, after], axis=dim)
    return block


def to_bands(teacher, axis):
    batch_size, rows, cols, channel_count = teacher.shape
    count = lax.axis_size(axis)
    band = rows // count
    state = teacher.reshape(batch_size, count, band, cols, channel_count)
    for bit in bits_of(axis):
        upper = (lax.axis_index(axis) // bit) % 2
        state = state.reshape(batch_size, -1, 2, band, state.shape[3], channel_count)
        mine = lax.dynamic_index_in_dim(state, upper, axis=2, keepdims=False)
        got = swap(lax.dynamic_index_in_dim(state, 1 - upper, axis=2, keepdims=False), axis, bit)
        state = jnp.where(
            upper == 1,
            jnp.concatenate([got, mine], axis=3),
            jnp.concatenate([mine, got], axis=3),
        )
    return state.reshape(batch_size, band, -1, channel_count)


def gelu_tanh(values):
    tanh_arg = slope_coef * (values + cubic_coef * values * values * values)
    return 0.5 * values * (1.0 + jnp.tanh(tanh_arg))


def gelu_slope(values):
    tangent = jnp.tanh(slope_coef * (values + cubic_coef * values * values * values))
    return 0.5 * (1.0 + tangent) + 0.5 * values * (1.0 - tangent * tangent) * slope_coef * (
        1.0 + 3.0 * cubic_coef * values * values
    )


def apply_stencil(padded, dw_weight, tile_rows, tile_cols, flipped):
    kernel_size = dw_weight.shape[0]
    result = jnp.zeros((padded.shape[0], tile_rows, tile_cols, padded.shape[3]), jnp.float32)
    for row_off in range(kernel_size):
        for col_off in range(kernel_size):
            row_start = kernel_size - 1 - row_off if flipped else row_off
            col_start = kernel_size - 1 - col_off if flipped else col_off
            result = (
                result
                + dw_weight[row_off, col_off]
                * padded[:, row_start : row_start + tile_rows, col_start : col_start + tile_cols]
            )
    return result


def rows_at(value, half, upper):
    return lax.dynamic_slice_in_dim(value, upper * half, half, axis=0)


def split_rows(value, counts):
    pieces, start = [], 0
    for count in counts:
        pieces.append(lax.slice_in_dim(value, start, start + count, axis=0))
        start += count
    return pieces


def sum_over_mesh(parts, divisor):
    lat_bits = [("lat", bit) for bit in bits_of("lat")]
    lon_bits = [("lon", bit) for bit in bits_of("lon")]
    halving = lat_bits[:2] + lon_bits[:1]
    whole = lon_bits[1:] + lat_bits[2:]
    parts = list(parts)
    for axis, bit in halving:
        upper = (lax.axis_index(axis) & bit) // bit
        halves = [part.shape[0] // 2 for part in parts]
        sent = [rows_at(p, h, 1 - upper).astype(jnp.bfloat16) for p, h in zip(parts, halves)]
        got = swap(jnp.concatenate(sent, axis=0), axis, bit)
        parts = [
            rows_at(p, h, upper) + g.astype(jnp.float32)
            for p, h, g in zip(parts, halves, split_rows(got, halves))
        ]
    counts = [part.shape[0] for part in parts]
    total = jnp.concatenate(parts, axis=0)
    for axis, bit in whole:
        total = total + swap(total, axis, bit)
    parts = split_rows((total / divisor).astype(jnp.bfloat16), counts)
    for axis, bit in reversed(halving):
        upper = (lax.axis_index(axis) & bit) // bit
        counts = [part.shape[0] for part in parts]
        got = split_rows(swap(jnp.concatenate(parts, axis=0), axis, bit), counts)
        parts = [
            jnp.where(upper == 1, jnp.concatenate([g, p]), jnp.concatenate([p, g]))
            for p, g in zip(parts, got)
        ]
    return [part.astype(jnp.float32) for part in parts]


def local(student, teacher, dw_weight, norm_gain, w_in, w_out, layer_scale):
    batch_size, tile_rows, tile_cols, channel_count = student.shape
    kernel_size = dw_weight.shape[0]
    half_kernel = kernel_size // 2
    cell_total = batch_size * tile_rows * lax.axis_size("lat") * tile_cols * lax.axis_size("lon")
    lon_padded = with_halo(student, (("lon", 2),), half_kernel, True)
    padded_bf = with_halo(lon_padded, (("lat", 1),), half_kernel, False)
    padded = padded_bf.astype(jnp.float32)
    smoothed = apply_stencil(padded, dw_weight, tile_rows, tile_cols, False).reshape(
        -1, channel_count
    )
    average = jnp.mean(smoothed, axis=-1, keepdims=True)
    centred = smoothed - average
    variance = jnp.mean(centred * centred, axis=-1, keepdims=True)
    inv_std = lax.rsqrt(variance + norm_eps)
    unit_norm = centred * inv_std
    normed = (unit_norm * norm_gain).astype(jnp.bfloat16)
    preact = jnp.dot(normed, w_in, preferred_element_type=jnp.float32)
    hidden = gelu_tanh(preact).astype(jnp.bfloat16)
    mlp_out = jnp.dot(hidden, w_out, preferred_element_type=jnp.float32)
    output = student.reshape(-1, channel_count).astype(jnp.float32) + layer_scale * mlp_out
    target = to_bands(teacher, "lat")
    misfit = output - target.reshape(-1, channel_count).astype(jnp.float32)
    out_grad = (layer_scale * misfit).astype(jnp.bfloat16)
    part_out = lax.dot_general(
        hidden, out_grad, (((0,), (0,)), ((), ())), preferred_element_type=jnp.float32
    )
    hidden_grad = lax.dot_general(
        out_grad, w_out, (((1,), (1,)), ((), ())), preferred_element_type=jnp.float32
    )
    preact_grad = (hidden_grad * gelu_slope(preact)).astype(jnp.bfloat16)
    part_in = lax.dot_general(
        normed, preact_grad, (((0,), (0,)), ((), ())), preferred_element_type=jnp.float32
    )
    normed_grad = lax.dot_general(
        preact_grad, w_in, (((1,), (1,)), ((), ())), preferred_element_type=jnp.float32
    )
    unit_grad = normed_grad * norm_gain
    first_mean = jnp.mean(unit_grad, axis=-1, keepdims=True)
    second_mean = jnp.mean(unit_grad * unit_norm, axis=-1, keepdims=True)
    conv_grad = (inv_std * (unit_grad - first_mean - unit_norm * second_mean)).astype(jnp.bfloat16)
    conv_grid = conv_grad.reshape(student.shape)
    grad_lon = with_halo(conv_grid, (("lon", 2),), half_kernel, True)
    padded_grad = with_halo(grad_lon, (("lat", 1),), half_kernel, False).astype(jnp.float32)
    back_conv = apply_stencil(padded_grad, dw_weight, tile_rows, tile_cols, True)
    grad_student = (misfit.reshape(student.shape) + back_conv).astype(jnp.bfloat16)
    conv_grad_f = conv_grid.astype(jnp.float32)
    kernel_terms = []
    for row_off in range(kernel_size):
        for col_off in range(kernel_size):
            kernel_terms.append(
                jnp.sum(
                    padded[:, row_off : row_off + tile_rows, col_off : col_off + tile_cols]
                    * conv_grad_f,
                    axis=(0, 1, 2),
                )
            )
    part_dw = jnp.stack(kernel_terms).reshape(kernel_size, kernel_size, channel_count)
    dw_rows = part_dw.reshape(-1, channel_count)
    hidden_size = part_in.shape[1]
    per_row = hidden_size // channel_count
    pad_rows = -dw_rows.shape[0] % (8 * per_row)
    dw_wide = jnp.pad(dw_rows, ((0, pad_rows), (0, 0))).reshape(-1, hidden_size)
    (sum_out,) = sum_over_mesh((part_out,), cell_total)
    sum_in, sum_dw = sum_over_mesh((part_in, dw_wide), cell_total)
    sum_dw = sum_dw.reshape(-1, channel_count)[: kernel_size * kernel_size]
    return (grad_student, sum_in, sum_out, sum_dw.reshape(dw_weight.shape))


def solution(mesh):
    placed = (
        P(None, "lat", "lon", None),
        P(None, None, ("lon", "lat"), None),
        P(),
        P(),
        P(),
        P(),
        P(),
    )
    return jax.shard_map(
        local,
        mesh=mesh,
        in_specs=placed,
        out_specs=(P(None, "lat", "lon", None), P(), P(), P()),
        check_vma=False,
    )
```

```python
import jax
import jax.numpy as jnp
from jax import lax
from jax.sharding import PartitionSpec as P

slope_coef = 0.7978845608028654
cubic_coef = 0.044715
norm_eps = 1e-06


def bits_of(axis):
    return [1 << k for k in range((lax.axis_size(axis) - 1).bit_length())]


def swap(value, axis, bit):
    return lax.ppermute(value, axis, [(i, i ^ bit) for i in range(lax.axis_size(axis))])


def edges(block, axis, dim, width):
    low = lax.slice_in_dim(block, 0, width, axis=dim)
    high = lax.slice_in_dim(block, block.shape[dim] - width, None, axis=dim)
    odd = lax.axis_index(axis) % 2 == 1
    return jnp.where(odd, low, high), jnp.where(odd, high, low)


def swap_outer(edge, axis, periodic):
    count = lax.axis_size(axis)
    pairs = [(i, (i + 1) % count) for i in range(1, count, 2)]
    if not periodic:
        pairs = [(i, j) for i, j in pairs if j]
    return lax.ppermute(edge, axis, pairs + [(j, i) for i, j in pairs])


def with_edges(block, from_inner, from_outer, axis, dim):
    odd = lax.axis_index(axis) % 2 == 1
    before = jnp.where(odd, from_inner, from_outer)
    after = jnp.where(odd, from_outer, from_inner)
    return jnp.concatenate([before, block, after], axis=dim)


def with_halo(block, axis, dim, width, periodic):
    to_inner, to_outer = edges(block, axis, dim, width)
    from_outer = swap_outer(to_outer, axis, periodic)
    from_inner = swap(to_inner, axis, 1)
    return with_edges(block, from_inner, from_outer, axis, dim)


def to_bands(teacher, axis):
    batch_size, rows, cols, channel_count = teacher.shape
    count = lax.axis_size(axis)
    band = rows // count
    state = teacher.reshape(batch_size, count, band, cols, channel_count)
    for bit in bits_of(axis):
        upper = (lax.axis_index(axis) // bit) % 2
        state = state.reshape(batch_size, -1, 2, band, state.shape[3], channel_count)
        mine = lax.dynamic_index_in_dim(state, upper, axis=2, keepdims=False)
        got = swap(lax.dynamic_index_in_dim(state, 1 - upper, axis=2, keepdims=False), axis, bit)
        state = jnp.where(
            upper == 1,
            jnp.concatenate([got, mine], axis=3),
            jnp.concatenate([mine, got], axis=3),
        )
    return state.reshape(batch_size, band, -1, channel_count)


def gelu_tanh(values):
    tanh_arg = slope_coef * (values + cubic_coef * values * values * values)
    return 0.5 * values * (1.0 + jnp.tanh(tanh_arg))


def gelu_slope(values):
    tangent = jnp.tanh(slope_coef * (values + cubic_coef * values * values * values))
    return 0.5 * (1.0 + tangent) + 0.5 * values * (1.0 - tangent * tangent) * slope_coef * (
        1.0 + 3.0 * cubic_coef * values * values
    )


def apply_stencil(padded, dw_weight, tile_rows, tile_cols, flipped):
    kernel_size = dw_weight.shape[0]
    result = jnp.zeros((padded.shape[0], tile_rows, tile_cols, padded.shape[3]), jnp.float32)
    for row_off in range(kernel_size):
        for col_off in range(kernel_size):
            row_start = kernel_size - 1 - row_off if flipped else row_off
            col_start = kernel_size - 1 - col_off if flipped else col_off
            result = (
                result
                + dw_weight[row_off, col_off]
                * padded[:, row_start : row_start + tile_rows, col_start : col_start + tile_cols]
            )
    return result


def half_of(value, upper):
    count = value.shape[0] // 2
    return lax.dynamic_slice_in_dim(value, upper * count, count, axis=0)


def total_of(terms):
    total = terms[0].astype(jnp.float32)
    for term in terms[1:]:
        total = total + term.astype(jnp.float32)
    return total


def flat_rows(block):
    return block.reshape(-1, block.shape[-1])


def after(value, other):
    return lax.optimization_barrier((value, other))[0]


def exchange(parts, axis, bit, halved, sent_as, rider=None):
    upper = (lax.axis_index(axis) // bit) % 2
    if halved:
        give = [total_of([half_of(t, 1 - upper) for t in terms]) for terms in parts]
        keep = [total_of([half_of(t, upper) for t in terms]) for terms in parts]
    else:
        give = keep = [total_of(terms) for terms in parts]
    give = [value.astype(sent_as) for value in give]
    if not halved:
        keep = [value.astype(jnp.float32) for value in give]
    counts = [value.shape[0] for value in give]
    if rider is not None:
        give = give + [flat_rows(rider).astype(sent_as)]
        counts = counts + [give[-1].shape[0]]
    sent = jnp.concatenate(give, axis=0) if len(give) > 1 else give[0]
    got = swap(sent, axis, bit)
    got = split_rows(got, counts) if len(give) > 1 else [got]
    parts = [[k, g] for k, g in zip(keep, got)]
    ridden = None if rider is None else got[-1].astype(rider.dtype).reshape(rider.shape)
    return parts, ridden, sent


def split_rows(value, counts):
    pieces, start = [], 0
    for count in counts:
        pieces.append(lax.slice_in_dim(value, start, start + count, axis=0))
        start += count
    return pieces


def gather_halves(chunks, axis, bit):
    upper = (lax.axis_index(axis) // bit) % 2
    got = swap(chunks, axis, bit)
    return jnp.where(
        upper == 1, jnp.concatenate([got, chunks]), jnp.concatenate([chunks, got])
    )


def carried(axis, bit):
    index = lax.axis_index(axis)
    lower = index % bit // 2
    return lower == jnp.where(index % 2 == 0, 0, bit // 2 - 1)


def sum_stages():
    lat_bits, lon_bits = bits_of("lat"), bits_of("lon")
    lat_stages = [("lat", bit) for bit in lat_bits[1:]]
    lon_stages = [("lon", bit) for bit in lon_bits]
    return lat_stages, lon_stages, [lat_stages[0], lon_stages[0]]


def sum_over_mesh(lead, trail, divisor, block, inner, outer, width):
    lat_stages, lon_stages, halved = sum_stages()
    last = (lat_stages + lon_stages)[-1]
    for stages, dim, periodic in ((lat_stages, 1, False), (lon_stages, 2, True)):
        for axis, bit in stages:
            rider = jnp.stack(edges(block, axis, dim, width)) if bit == 1 else outer
            is_halved = (axis, bit) in halved
            sent_as = jnp.bfloat16 if is_halved or (axis, bit) == last else jnp.float32
            lead, _, _ = exchange(lead, axis, bit, is_halved, sent_as)
            trail, got, sent = exchange(trail, axis, bit, is_halved, sent_as, rider)
            lead = after(lead, sent)
            if bit == 1:
                inner, outer = got[0], got[1]
            else:
                outer = jnp.where(carried(axis, bit), got, outer)
        if not periodic:
            index = lax.axis_index(axis)
            at_end = (index == 0) | (index == lax.axis_size(axis) - 1)
            outer = jnp.where(at_end, jnp.zeros_like(outer), outer)
        block = with_edges(block, inner, outer, axis, dim)
    lead = [(total_of(terms) / divisor).astype(jnp.bfloat16) for terms in lead]
    trail = [(total_of(terms) / divisor).astype(jnp.bfloat16) for terms in trail]
    return lead, trail, block


def gather_sums(lead, trail):
    for axis, bit in sum_stages()[2][::-1] + [("lat", 1)]:
        lead = gather_halves(lead, axis, bit)
        trail = gather_halves(trail, axis, bit)
    return lead, trail


def columns_half(value, upper):
    count = value.shape[1] // 2
    return lax.dynamic_slice_in_dim(value, upper * count, count, axis=1)


def cell_products(left, right):
    return lax.dot_general(
        left, right, (((0,), (0,)), ((), ())), preferred_element_type=jnp.float32
    )


def local(student, teacher, dw_weight, norm_gain, w_in, w_out, layer_scale):
    batch_size, tile_rows, tile_cols, channel_count = student.shape
    kernel_size = dw_weight.shape[0]
    half_kernel = kernel_size // 2
    cell_total = batch_size * tile_rows * lax.axis_size("lat") * tile_cols * lax.axis_size("lon")
    lon_padded = with_halo(student, "lon", 2, half_kernel, True)
    lon_padded, teacher = lax.optimization_barrier((lon_padded, teacher))
    padded_bf = with_halo(lon_padded, "lat", 1, half_kernel, False)
    padded = padded_bf.astype(jnp.float32)
    smoothed = apply_stencil(padded, dw_weight, tile_rows, tile_cols, False).reshape(
        -1, channel_count
    )
    average = jnp.mean(smoothed, axis=-1, keepdims=True)
    centred = smoothed - average
    variance = jnp.mean(centred * centred, axis=-1, keepdims=True)
    inv_std = lax.rsqrt(variance + norm_eps)
    unit_norm = centred * inv_std
    normed = (unit_norm * norm_gain).astype(jnp.bfloat16)
    preact = jnp.dot(normed, w_in, preferred_element_type=jnp.float32)
    hidden = gelu_tanh(preact).astype(jnp.bfloat16)
    mlp_out = jnp.dot(hidden, w_out, preferred_element_type=jnp.float32)
    output = student.reshape(-1, channel_count).astype(jnp.float32) + layer_scale * mlp_out
    target = to_bands(teacher, "lat")
    misfit = output - target.reshape(-1, channel_count).astype(jnp.float32)
    out_grad = (layer_scale * misfit).astype(jnp.bfloat16)
    upper = lax.axis_index("lat") % 2
    got_out = swap(
        cell_products(columns_half(hidden, 1 - upper), out_grad).astype(jnp.bfloat16), "lat", 1
    )
    kept_out = cell_products(columns_half(hidden, upper), out_grad)
    hidden_grad = lax.dot_general(
        out_grad, w_out, (((1,), (1,)), ((), ())), preferred_element_type=jnp.float32
    )
    preact_grad = (hidden_grad * gelu_slope(preact)).astype(jnp.bfloat16)
    got_in = swap(
        cell_products(columns_half(preact_grad, 1 - upper), normed).astype(jnp.bfloat16), "lat", 1
    )
    kept_in = cell_products(columns_half(preact_grad, upper), normed)
    normed_grad = lax.dot_general(
        preact_grad, w_in, (((1,), (1,)), ((), ())), preferred_element_type=jnp.float32
    )
    unit_grad = normed_grad * norm_gain
    first_mean = jnp.mean(unit_grad, axis=-1, keepdims=True)
    second_mean = jnp.mean(unit_grad * unit_norm, axis=-1, keepdims=True)
    conv_grad = (inv_std * (unit_grad - first_mean - unit_norm * second_mean)).astype(jnp.bfloat16)
    conv_grid = conv_grad.reshape(student.shape)
    inner, outer = swap(jnp.stack(edges(conv_grid, "lat", 1, half_kernel)), "lat", 1)
    conv_grad_f = conv_grid.astype(jnp.float32)
    kernel_terms = []
    for row_off in range(kernel_size):
        for col_off in range(kernel_size):
            kernel_terms.append(
                jnp.sum(
                    padded[:, row_off : row_off + tile_rows, col_off : col_off + tile_cols]
                    * conv_grad_f,
                    axis=(0, 1, 2),
                )
            )
    part_dw = jnp.stack(kernel_terms)
    tap_count = kernel_size * kernel_size
    part_dw = jnp.pad(part_dw, ((0, -tap_count % 64), (0, 0)))
    got_dw = swap(half_of(part_dw, 1 - upper).astype(jnp.bfloat16), "lat", 1)
    (out_chunk,), (in_chunk, dw_chunk), padded_grad = sum_over_mesh(
        [[kept_out, got_out]],
        [[kept_in, got_in], [half_of(part_dw, upper), got_dw]],
        cell_total,
        conv_grid,
        inner,
        outer,
        half_kernel,
    )
    back_conv = apply_stencil(
        padded_grad.astype(jnp.float32), dw_weight, tile_rows, tile_cols, True
    )
    grad_student = (misfit.reshape(student.shape) + back_conv).astype(jnp.bfloat16)
    hidden_rows = in_chunk.shape[0]
    mixed = jnp.concatenate([in_chunk.T, dw_chunk.reshape(-1, hidden_rows)])
    out_chunks, in_chunks = gather_sums(out_chunk[None], mixed[None])
    sum_out = out_chunks.astype(jnp.float32).reshape(w_out.shape)
    sum_in = jnp.swapaxes(in_chunks[:, :channel_count], 0, 1).astype(jnp.float32)
    sum_dw = in_chunks[:, channel_count:].astype(jnp.float32).reshape(-1, channel_count)
    return (
        grad_student,
        sum_in.reshape(w_in.shape),
        sum_out,
        sum_dw[:tap_count].reshape(dw_weight.shape),
    )


def solution(mesh):
    placed = (
        P(None, "lat", "lon", None),
        P(None, None, ("lon", "lat"), None),
        P(),
        P(),
        P(),
        P(),
        P(),
    )
    return jax.shard_map(
        local,
        mesh=mesh,
        in_specs=placed,
        out_specs=(P(None, "lat", "lon", None), P(), P(), P()),
        check_vma=False,
    )
```

```python
import jax
import jax.numpy as jnp
from jax import lax
from jax.experimental import pallas as pl
from jax.experimental.pallas import tpu as pltpu
from jax.sharding import PartitionSpec as P

slope_coef = 0.7978845608028654
cubic_coef = 0.044715
norm_eps = 1e-06


def bits_of(axis):
    return [1 << k for k in range((lax.axis_size(axis) - 1).bit_length())]


def swap(value, axis, bit):
    return lax.ppermute(value, axis, [(i, i ^ bit) for i in range(lax.axis_size(axis))])


def edges(block, axis, dim, width):
    low = lax.slice_in_dim(block, 0, width, axis=dim)
    high = lax.slice_in_dim(block, block.shape[dim] - width, None, axis=dim)
    odd = lax.axis_index(axis) % 2 == 1
    return jnp.where(odd, low, high), jnp.where(odd, high, low)


def swap_outer(edge, axis, periodic):
    count = lax.axis_size(axis)
    pairs = [(i, (i + 1) % count) for i in range(1, count, 2)]
    if not periodic:
        pairs = [(i, j) for i, j in pairs if j]
    return lax.ppermute(edge, axis, pairs + [(j, i) for i, j in pairs])


def with_edges(block, from_inner, from_outer, axis, dim):
    odd = lax.axis_index(axis) % 2 == 1
    before = jnp.where(odd, from_inner, from_outer)
    after = jnp.where(odd, from_outer, from_inner)
    return jnp.concatenate([before, block, after], axis=dim)


def with_halo(block, axis, dim, width, periodic):
    to_inner, to_outer = edges(block, axis, dim, width)
    from_outer = swap_outer(to_outer, axis, periodic)
    from_inner = swap(to_inner, axis, 1)
    return with_edges(block, from_inner, from_outer, axis, dim)


def to_bands(teacher, axis):
    batch_size, rows, cols, channel_count = teacher.shape
    count = lax.axis_size(axis)
    band = rows // count
    state = teacher.reshape(batch_size, count, band, cols, channel_count)
    for bit in bits_of(axis):
        upper = (lax.axis_index(axis) // bit) % 2
        state = state.reshape(batch_size, -1, 2, band, state.shape[3], channel_count)
        mine = lax.dynamic_index_in_dim(state, upper, axis=2, keepdims=False)
        got = swap(lax.dynamic_index_in_dim(state, 1 - upper, axis=2, keepdims=False), axis, bit)
        state = jnp.where(
            upper == 1,
            jnp.concatenate([got, mine], axis=3),
            jnp.concatenate([mine, got], axis=3),
        )
    return state.reshape(batch_size, band, -1, channel_count)


def gelu_tanh(values):
    tanh_arg = slope_coef * (values + cubic_coef * values * values * values)
    return 0.5 * values * (1.0 + jnp.tanh(tanh_arg))


def gelu_slope(values):
    tangent = jnp.tanh(slope_coef * (values + cubic_coef * values * values * values))
    return 0.5 * (1.0 + tangent) + 0.5 * values * (1.0 - tangent * tangent) * slope_coef * (
        1.0 + 3.0 * cubic_coef * values * values
    )


def half_of(value, upper):
    count = value.shape[0] // 2
    return lax.dynamic_slice_in_dim(value, upper * count, count, axis=0)


def total_of(terms):
    total = terms[0].astype(jnp.float32)
    for term in terms[1:]:
        total = total + term.astype(jnp.float32)
    return total


def flat_rows(block):
    return block.reshape(-1, block.shape[-1])


def after(value, other):
    return lax.optimization_barrier((value, other))[0]


def exchange(parts, axis, bit, halved, sent_as, rider=None):
    upper = (lax.axis_index(axis) // bit) % 2
    if halved:
        give = [total_of([half_of(t, 1 - upper) for t in terms]) for terms in parts]
        keep = [total_of([half_of(t, upper) for t in terms]) for terms in parts]
    else:
        give = keep = [total_of(terms) for terms in parts]
    give = [value.astype(sent_as) for value in give]
    if not halved:
        keep = [value.astype(jnp.float32) for value in give]
    counts = [value.shape[0] for value in give]
    if rider is not None:
        give = give + [flat_rows(rider).astype(sent_as)]
        counts = counts + [give[-1].shape[0]]
    sent = jnp.concatenate(give, axis=0) if len(give) > 1 else give[0]
    got = swap(sent, axis, bit)
    got = split_rows(got, counts) if len(give) > 1 else [got]
    parts = [[k, g] for k, g in zip(keep, got)]
    ridden = None if rider is None else got[-1].astype(rider.dtype).reshape(rider.shape)
    return parts, ridden, sent


def split_rows(value, counts):
    pieces, start = [], 0
    for count in counts:
        pieces.append(lax.slice_in_dim(value, start, start + count, axis=0))
        start += count
    return pieces


def gather_halves(chunks, axis, bit):
    upper = (lax.axis_index(axis) // bit) % 2
    got = swap(chunks, axis, bit)
    return jnp.where(
        upper == 1, jnp.concatenate([got, chunks]), jnp.concatenate([chunks, got])
    )


def carried(axis, bit):
    index = lax.axis_index(axis)
    lower = index % bit // 2
    return lower == jnp.where(index % 2 == 0, 0, bit // 2 - 1)


def sum_stages():
    lat_bits, lon_bits = bits_of("lat"), bits_of("lon")
    lat_stages = [("lat", bit) for bit in lat_bits[1:]]
    lon_stages = [("lon", bit) for bit in lon_bits]
    return lat_stages, lon_stages, [lat_stages[0], lon_stages[0]]


def sum_over_mesh(lead, trail, divisor, block, inner, outer, width):
    lat_stages, lon_stages, halved = sum_stages()
    last = (lat_stages + lon_stages)[-1]
    for stages, dim, periodic in ((lat_stages, 1, False), (lon_stages, 2, True)):
        for axis, bit in stages:
            rider = jnp.stack(edges(block, axis, dim, width)) if bit == 1 else outer
            is_halved = (axis, bit) in halved
            sent_as = jnp.bfloat16 if is_halved or (axis, bit) == last else jnp.float32
            lead, _, _ = exchange(lead, axis, bit, is_halved, sent_as)
            trail, got, sent = exchange(trail, axis, bit, is_halved, sent_as, rider)
            lead = after(lead, sent)
            if bit == 1:
                inner, outer = got[0], got[1]
            else:
                outer = jnp.where(carried(axis, bit), got, outer)
        if not periodic:
            index = lax.axis_index(axis)
            at_end = (index == 0) | (index == lax.axis_size(axis) - 1)
            outer = jnp.where(at_end, jnp.zeros_like(outer), outer)
        block = with_edges(block, inner, outer, axis, dim)
    lead = [(total_of(terms) / divisor).astype(jnp.bfloat16) for terms in lead]
    trail = [(total_of(terms) / divisor).astype(jnp.bfloat16) for terms in trail]
    return lead, trail, block


def gather_sums(lead, trail):
    for axis, bit in sum_stages()[2][::-1]:
        lead = gather_halves(lead, axis, bit)
        trail = gather_halves(trail, axis, bit)
    return lead, trail


def columns_half(value, upper):
    count = value.shape[1] // 2
    return lax.dynamic_slice_in_dim(value, upper * count, count, axis=1)


def cell_products(left, right):
    return lax.dot_general(
        left, right, (((0,), (0,)), ((), ())), preferred_element_type=jnp.float32
    )


lane_count = 128


def spread(padded_ref, wide):
    batch_size, rows, cols, channel_count = padded_ref.shape
    for group in range(channel_count // lane_count):
        lanes = slice(group * lane_count, (group + 1) * lane_count)
        for b in range(batch_size):
            wide[group, b, :, :cols, :] = padded_ref[b, :, :, lanes].astype(jnp.float32)


def stencil(wide, weights, group, b, tile_rows, tile_cols, flipped):
    kernel_size = weights.shape[1]
    rows = [None] * tile_rows
    for q in range(kernel_size):
        for r in range(tile_rows + kernel_size - 1):
            shifted = wide[group, b, r, q : q + tile_cols, :]
            for i in range(max(0, r - kernel_size + 1), min(tile_rows, r + 1)):
                p = r - i
                tap = (kernel_size - 1 - p, kernel_size - 1 - q) if flipped else (p, q)
                term = weights[group, tap[0], pl.ds(tap[1], 1), :] * shifted
                rows[i] = term if rows[i] is None else rows[i] + term
    return rows


def conv_norm_kernel(padded_ref, weights_ref, gain_ref, normed_ref, unit_ref, inv_ref, wide, smooth):
    batch_size, pad_rows, pad_cols, channel_count = padded_ref.shape
    kernel_size = weights_ref.shape[1]
    tile_rows, tile_cols = pad_rows - kernel_size + 1, pad_cols - kernel_size + 1
    spread(padded_ref, wide)

    def one(step, _):
        group, b = step // batch_size, step % batch_size
        rows = stencil(wide, weights_ref, group, b, tile_rows, tile_cols, False)
        for i, row in enumerate(rows):
            smooth[group, pl.ds((b * tile_rows + i) * tile_cols, tile_cols), :] = row
        return 0

    lax.fori_loop(0, wide.shape[0] * batch_size, one, 0)
    groups = range(wide.shape[0])
    cells = smooth.shape[1]
    block = 32

    def norm(step, _):
        at = pl.ds(pl.multiple_of(step * block, block), block)
        values = jnp.concatenate([smooth[g, at, :] for g in groups], axis=1)
        average = jnp.mean(values, axis=-1, keepdims=True)
        centred = values - average
        variance = jnp.mean(centred * centred, axis=-1, keepdims=True)
        inv_std = lax.rsqrt(variance + norm_eps)
        unit = centred * inv_std
        unit_ref[at, :] = unit
        inv_ref[at, :] = inv_std
        normed_ref[at, :] = (unit * gain_ref[...]).astype(jnp.bfloat16)
        return 0

    lax.fori_loop(0, cells // block, norm, 0, unroll=True)


def lane_groups(weights):
    groups = weights.shape[-1] // lane_count
    return jnp.moveaxis(weights.reshape(weights.shape[:2] + (groups, lane_count)), 2, 0)


def round_up(value, unit):
    return -(-value // unit) * unit


def conv_norm(padded, weights, gain):
    batch_size, pad_rows, pad_cols, channel_count = padded.shape
    kernel_size = weights.shape[0]
    cells = batch_size * (pad_rows - kernel_size + 1) * (pad_cols - kernel_size + 1)
    groups = channel_count // lane_count
    return pl.pallas_call(
        conv_norm_kernel,
        out_shape=(
            jax.ShapeDtypeStruct((cells, channel_count), jnp.bfloat16),
            jax.ShapeDtypeStruct((cells, channel_count), jnp.float32),
            jax.ShapeDtypeStruct((cells, 1), jnp.float32),
        ),
        scratch_shapes=[
            pltpu.VMEM((groups, batch_size, pad_rows, round_up(pad_cols, 8), lane_count), jnp.float32),
            pltpu.VMEM((groups, cells, lane_count), jnp.float32),
        ],
        compiler_params=pltpu.CompilerParams(vmem_limit_bytes=16 << 20),
        cost_estimate=pl.CostEstimate(flops=2 * 49 * cells * channel_count, bytes_accessed=1 << 20, transcendentals=0),
        name="conv_norm",
    )(padded, lane_groups(weights), gain.reshape(1, -1))


def conv_back_kernel(padded_ref, weights_ref, misfit_ref, out_ref, wide):
    batch_size, tile_rows, tile_cols, channel_count = out_ref.shape
    spread(padded_ref, wide)
    for group in range(wide.shape[0]):
        lanes = slice(group * lane_count, (group + 1) * lane_count)

        def one(b, _):
            rows = stencil(wide, weights_ref, group, b, tile_rows, tile_cols, True)
            for i, row in enumerate(rows):
                out_ref[b, i, :, lanes] = (misfit_ref[b, i, :, lanes] + row).astype(out_ref.dtype)
            return 0

        lax.fori_loop(0, batch_size, one, 0)


def conv_back(padded, weights, misfit):
    batch_size, pad_rows, pad_cols, channel_count = padded.shape
    groups = channel_count // lane_count
    return pl.pallas_call(
        conv_back_kernel,
        out_shape=jax.ShapeDtypeStruct(misfit.shape, jnp.bfloat16),
        scratch_shapes=[
            pltpu.VMEM((groups, batch_size, pad_rows, round_up(pad_cols, 8), lane_count), jnp.float32),
        ],
        compiler_params=pltpu.CompilerParams(vmem_limit_bytes=16 << 20),
        cost_estimate=pl.CostEstimate(flops=2 * 49 * misfit.size, bytes_accessed=1 << 20, transcendentals=0),
        name="conv_back",
    )(padded, lane_groups(weights), misfit)


def tap_sums_kernel(padded_ref, grad_ref, out_ref, wide, partial):
    batch_size, tile_rows, tile_cols, channel_count = grad_ref.shape
    kernel_size = padded_ref.shape[1] - tile_rows + 1
    spread(padded_ref, wide)
    out_ref[...] = jnp.zeros_like(out_ref)
    for group in range(wide.shape[0]):
        lanes = slice(group * lane_count, (group + 1) * lane_count)

        def one(b, _):
            grads = [grad_ref[b, i, :, lanes].astype(jnp.float32) for i in range(tile_rows)]
            for q in range(kernel_size):
                sums = [None] * kernel_size
                for r in range(tile_rows + kernel_size - 1):
                    shifted = wide[group, b, r, q : q + tile_cols, :]
                    for i in range(max(0, r - kernel_size + 1), min(tile_rows, r + 1)):
                        product = shifted * grads[i]
                        term = product.reshape(tile_cols // 8, 8, lane_count).sum(axis=0)
                        p = r - i
                        sums[p] = term if sums[p] is None else sums[p] + term
                for p in range(kernel_size):
                    at = pl.ds((p * kernel_size + q) * 8, 8)
                    partial[group, b, at, :] = sums[p]
            return 0

        lax.fori_loop(0, batch_size, one, 0)
        taps = kernel_size * kernel_size
        total = partial[group, 0]
        for b in range(1, batch_size):
            total = total + partial[group, b]
        out_ref[:taps, lanes] = total.reshape(taps, 8, lane_count).sum(axis=1)


def tap_sums(padded, grads, row_count):
    batch_size, pad_rows, pad_cols, channel_count = padded.shape
    kernel_size = pad_rows - grads.shape[1] + 1
    groups = channel_count // lane_count
    return pl.pallas_call(
        tap_sums_kernel,
        out_shape=jax.ShapeDtypeStruct((row_count, channel_count), jnp.float32),
        scratch_shapes=[
            pltpu.VMEM((groups, batch_size, pad_rows, round_up(pad_cols, 8), lane_count), jnp.float32),
            pltpu.VMEM((groups, batch_size, kernel_size * kernel_size * 8, lane_count), jnp.float32),
        ],
        compiler_params=pltpu.CompilerParams(vmem_limit_bytes=16 << 20),
        cost_estimate=pl.CostEstimate(flops=2 * 49 * grads.size, bytes_accessed=1 << 20, transcendentals=0),
        name="tap_sums",
    )(padded, grads)


def assemble_kernel(side_ref, out_mine, out_got, in_mine, in_got, out_ref, in_ref, taps_ref):
    half = pl.program_id(0)
    own = half == side_ref[0]
    count, rows, _ = out_mine.shape
    channel_count = in_ref.shape[0]

    def write(out_chunks, in_chunks):
        for k in range(count):
            out_ref[k * rows : (k + 1) * rows, :] = out_chunks[k].astype(jnp.float32)
            in_ref[:, k * rows : (k + 1) * rows] = in_chunks[k, :channel_count].astype(jnp.float32)

    @pl.when(own)
    def _():
        write(out_mine, in_mine)

    @pl.when(jnp.logical_not(own))
    def _():
        write(out_got, in_got)

    @pl.when(half == 0)
    def _():
        first = side_ref[0] == 0
        tail = slice(channel_count, in_mine.shape[1])
        mine, got = in_mine[:, tail].astype(jnp.float32), in_got[:, tail].astype(jnp.float32)
        halves = [jnp.where(first, mine, got), jnp.where(first, got, mine)]
        rows_of = (channel_count // in_mine.shape[2], mine.shape[1])
        step = rows_of[1] // rows_of[0]
        pieces = []
        for chunks in halves:
            for k in range(count):
                groups = [chunks[k, n * step : (n + 1) * step] for n in range(rows_of[0])]
                pieces.append(jnp.concatenate(groups, axis=1))
        taps = jnp.concatenate(pieces, axis=0)
        width = taps_ref.shape[1]
        for p in range(taps_ref.shape[0]):
            taps_ref[p] = taps[p * width : (p + 1) * width]


def assemble(side, out_mine, out_got, in_mine, in_got, channel_count, kernel_size):
    count, rows, _ = out_mine.shape
    whole = lambda value: pl.BlockSpec(value.shape, lambda i: (0,) * value.ndim)
    operands = (out_mine, out_got, in_mine, in_got)
    return pl.pallas_call(
        assemble_kernel,
        grid=(2,),
        in_specs=[pl.BlockSpec(memory_space=pltpu.SMEM)] + [whole(v) for v in operands],
        out_specs=(
            pl.BlockSpec((count * rows, channel_count), lambda i: (i, 0)),
            pl.BlockSpec((channel_count, count * rows), lambda i: (0, i)),
            pl.BlockSpec((kernel_size, kernel_size, channel_count), lambda i: (0, 0, 0)),
        ),
        out_shape=(
            jax.ShapeDtypeStruct((2 * count * rows, channel_count), jnp.float32),
            jax.ShapeDtypeStruct((channel_count, 2 * count * rows), jnp.float32),
            jax.ShapeDtypeStruct((kernel_size, kernel_size, channel_count), jnp.float32),
        ),
        compiler_params=pltpu.CompilerParams(vmem_limit_bytes=16 << 20),
        cost_estimate=pl.CostEstimate(flops=0, bytes_accessed=3 << 20, transcendentals=0),
        name="assemble",
    )(side, *operands)


def local(student, teacher, dw_weight, norm_gain, w_in, w_out, layer_scale):
    batch_size, tile_rows, tile_cols, channel_count = student.shape
    kernel_size = dw_weight.shape[0]
    half_kernel = kernel_size // 2
    cell_total = batch_size * tile_rows * lax.axis_size("lat") * tile_cols * lax.axis_size("lon")
    lon_padded = with_halo(student, "lon", 2, half_kernel, True)
    lon_padded, teacher = lax.optimization_barrier((lon_padded, teacher))
    padded_bf = with_halo(lon_padded, "lat", 1, half_kernel, False)
    normed, unit_norm, inv_std = conv_norm(padded_bf, dw_weight, norm_gain)
    preact = jnp.dot(normed, w_in, preferred_element_type=jnp.float32)
    hidden = gelu_tanh(preact).astype(jnp.bfloat16)
    mlp_out = jnp.dot(hidden, w_out, preferred_element_type=jnp.float32)
    output = student.reshape(-1, channel_count).astype(jnp.float32) + layer_scale * mlp_out
    target = to_bands(teacher, "lat")
    misfit = output - target.reshape(-1, channel_count).astype(jnp.float32)
    out_grad = (layer_scale * misfit).astype(jnp.bfloat16)
    upper = lax.axis_index("lat") % 2
    got_out = swap(
        cell_products(columns_half(hidden, 1 - upper), out_grad).astype(jnp.bfloat16), "lat", 1
    )
    kept_out = cell_products(columns_half(hidden, upper), out_grad)
    hidden_grad = lax.dot_general(
        out_grad, w_out, (((1,), (1,)), ((), ())), preferred_element_type=jnp.float32
    )
    preact_grad = (hidden_grad * gelu_slope(preact)).astype(jnp.bfloat16)
    got_in = swap(
        cell_products(columns_half(preact_grad, 1 - upper), normed).astype(jnp.bfloat16), "lat", 1
    )
    kept_in = cell_products(columns_half(preact_grad, upper), normed)
    normed_grad = lax.dot_general(
        preact_grad, w_in, (((1,), (1,)), ((), ())), preferred_element_type=jnp.float32
    )
    unit_grad = normed_grad * norm_gain
    first_mean = jnp.mean(unit_grad, axis=-1, keepdims=True)
    second_mean = jnp.mean(unit_grad * unit_norm, axis=-1, keepdims=True)
    conv_grad = (inv_std * (unit_grad - first_mean - unit_norm * second_mean)).astype(jnp.bfloat16)
    conv_grid = conv_grad.reshape(student.shape)
    inner, outer = swap(jnp.stack(edges(conv_grid, "lat", 1, half_kernel)), "lat", 1)
    tap_count = kernel_size * kernel_size
    part_dw = tap_sums(padded_bf, conv_grid, round_up(tap_count, 64))
    got_dw = swap(half_of(part_dw, 1 - upper).astype(jnp.bfloat16), "lat", 1)
    (out_chunk,), (in_chunk, dw_chunk), padded_grad = sum_over_mesh(
        [[kept_out, got_out]],
        [[kept_in, got_in], [half_of(part_dw, upper), got_dw]],
        cell_total,
        conv_grid,
        inner,
        outer,
        half_kernel,
    )
    grad_student = conv_back(padded_grad, dw_weight, misfit.reshape(student.shape))
    hidden_rows = in_chunk.shape[0]
    dw_groups = [dw_chunk[:, k : k + hidden_rows] for k in range(0, channel_count, hidden_rows)]
    mixed = jnp.concatenate([in_chunk.T] + dw_groups)
    out_chunks, in_chunks = gather_sums(out_chunk[None], mixed[None])
    sum_out, sum_in, sum_dw = assemble(
        upper.astype(jnp.int32).reshape(1),
        out_chunks,
        swap(out_chunks, "lat", 1),
        in_chunks,
        swap(in_chunks, "lat", 1),
        channel_count,
        kernel_size,
    )
    return (grad_student, sum_in, sum_out, sum_dw)


def solution(mesh):
    placed = (
        P(None, "lat", "lon", None),
        P(None, None, ("lon", "lat"), None),
        P(),
        P(),
        P(),
        P(),
        P(),
    )
    return jax.shard_map(
        local,
        mesh=mesh,
        in_specs=placed,
        out_specs=(P(None, "lat", "lon", None), P(), P(), P()),
        check_vma=False,
    )
```

```python
import jax
import jax.numpy as jnp
from jax import lax
from jax.experimental import pallas as pl
from jax.experimental.pallas import tpu as pltpu
from jax.sharding import PartitionSpec as P

slope_coef = 0.7978845608028654
cubic_coef = 0.044715
norm_eps = 1e-06


def bits_of(axis):
    return [1 << k for k in range((lax.axis_size(axis) - 1).bit_length())]


def swap(value, axis, bit):
    return lax.ppermute(value, axis, [(i, i ^ bit) for i in range(lax.axis_size(axis))])


def edges(block, axis, dim, width):
    low = lax.slice_in_dim(block, 0, width, axis=dim)
    high = lax.slice_in_dim(block, block.shape[dim] - width, None, axis=dim)
    odd = lax.axis_index(axis) % 2 == 1
    return jnp.where(odd, low, high), jnp.where(odd, high, low)


def swap_outer(edge, axis, periodic):
    count = lax.axis_size(axis)
    pairs = [(i, (i + 1) % count) for i in range(1, count, 2)]
    if not periodic:
        pairs = [(i, j) for i, j in pairs if j]
    return lax.ppermute(edge, axis, pairs + [(j, i) for i, j in pairs])


def with_edges(block, from_inner, from_outer, axis, dim):
    odd = lax.axis_index(axis) % 2 == 1
    before = jnp.where(odd, from_inner, from_outer)
    after = jnp.where(odd, from_outer, from_inner)
    return jnp.concatenate([before, block, after], axis=dim)


def with_halo(block, axis, dim, width, periodic):
    to_inner, to_outer = edges(block, axis, dim, width)
    from_outer = swap_outer(to_outer, axis, periodic)
    from_inner = swap(to_inner, axis, 1)
    return with_edges(block, from_inner, from_outer, axis, dim)


def to_bands(teacher, axis):
    batch_size, rows, cols, channel_count = teacher.shape
    count = lax.axis_size(axis)
    band = rows // count
    state = teacher.reshape(batch_size, count, band, cols, channel_count)
    for bit in bits_of(axis):
        upper = (lax.axis_index(axis) // bit) % 2
        state = state.reshape(batch_size, -1, 2, band, state.shape[3], channel_count)
        mine = lax.dynamic_index_in_dim(state, upper, axis=2, keepdims=False)
        got = swap(lax.dynamic_index_in_dim(state, 1 - upper, axis=2, keepdims=False), axis, bit)
        state = jnp.where(
            upper == 1,
            jnp.concatenate([got, mine], axis=3),
            jnp.concatenate([mine, got], axis=3),
        )
    return state.reshape(batch_size, band, -1, channel_count)


def half_of(value, upper):
    count = value.shape[0] // 2
    return lax.dynamic_slice_in_dim(value, upper * count, count, axis=0)


def total_of(terms):
    total = terms[0].astype(jnp.float32)
    for term in terms[1:]:
        total = total + term.astype(jnp.float32)
    return total


def flat_rows(block):
    return block.reshape(-1, block.shape[-1])


def after(value, other):
    return lax.optimization_barrier((value, other))[0]


def exchange(parts, axis, bit, halved, sent_as, rider=None):
    upper = (lax.axis_index(axis) // bit) % 2
    if halved:
        give = [total_of([half_of(t, 1 - upper) for t in terms]) for terms in parts]
        keep = [total_of([half_of(t, upper) for t in terms]) for terms in parts]
    else:
        give = keep = [total_of(terms) for terms in parts]
    give = [value.astype(sent_as) for value in give]
    if not halved:
        keep = [value.astype(jnp.float32) for value in give]
    counts = [value.shape[0] for value in give]
    if rider is not None:
        give = give + [flat_rows(rider).astype(sent_as)]
        counts = counts + [give[-1].shape[0]]
    sent = jnp.concatenate(give, axis=0) if len(give) > 1 else give[0]
    got = swap(sent, axis, bit)
    got = split_rows(got, counts) if len(give) > 1 else [got]
    parts = [[k, g] for k, g in zip(keep, got)]
    ridden = None if rider is None else got[-1].astype(rider.dtype).reshape(rider.shape)
    return parts, ridden, sent


def split_rows(value, counts):
    pieces, start = [], 0
    for count in counts:
        pieces.append(lax.slice_in_dim(value, start, start + count, axis=0))
        start += count
    return pieces


def gather_halves(chunks, axis, bit):
    upper = (lax.axis_index(axis) // bit) % 2
    got = swap(chunks, axis, bit)
    return jnp.where(
        upper == 1, jnp.concatenate([got, chunks]), jnp.concatenate([chunks, got])
    )


def carried(axis, bit):
    index = lax.axis_index(axis)
    lower = index % bit // 2
    return lower == jnp.where(index % 2 == 0, 0, bit // 2 - 1)


def sum_stages():
    lat_stages = [("lat", bit) for bit in bits_of("lat")[1:]]
    lon_stages = [("lon", bit) for bit in bits_of("lon")]
    trail = lat_stages + lon_stages
    lead = lon_stages[1:3] + lat_stages + lon_stages[:1] + lon_stages[3:]
    return (lead, lead[:2]), (trail, [lat_stages[0], lon_stages[0]])


def sent_type(stage, stages, halved):
    return jnp.bfloat16 if stage in halved or stage == stages[-1] else jnp.float32


def sum_over_mesh(lead, trail, divisor, block, inner, outer, width):
    (lead_stages, lead_halved), (stages, halved) = sum_stages()
    dim_of = {"lat": 1, "lon": 2}
    for k, (axis, bit) in enumerate(stages):
        dim = dim_of[axis]
        stage = lead_stages[k]
        lead, _, _ = exchange(
            lead, *stage, stage in lead_halved, sent_type(stage, lead_stages, lead_halved)
        )
        rider = jnp.stack(edges(block, axis, dim, width)) if bit == 1 else outer
        trail, got, sent = exchange(
            trail, axis, bit, (axis, bit) in halved, sent_type((axis, bit), stages, halved), rider
        )
        lead = after(lead, sent)
        if bit == 1:
            inner, outer = got[0], got[1]
        else:
            outer = jnp.where(carried(axis, bit), got, outer)
        if k + 1 == len(stages) or stages[k + 1][0] != axis:
            if axis == "lat":
                index = lax.axis_index(axis)
                at_end = (index == 0) | (index == lax.axis_size(axis) - 1)
                outer = jnp.where(at_end, jnp.zeros_like(outer), outer)
            block = with_edges(block, inner, outer, axis, dim)
    lead = [(total_of(terms) / divisor).astype(jnp.bfloat16) for terms in lead]
    trail = [(total_of(terms) / divisor).astype(jnp.bfloat16) for terms in trail]
    return lead, trail, block


def gather_sums(lead, trail):
    (_, lead_halved), (_, halved) = sum_stages()
    for lead_stage, stage in zip(lead_halved[::-1], halved[::-1]):
        lead = gather_halves(lead, *lead_stage)
        trail = gather_halves(trail, *stage)
    return lead, trail


lane_count = 128
kernel_side = 7
gain_row = kernel_side * kernel_side
scale_row = gain_row + 1


def spread(padded_ref, wide):
    batch_size, rows, cols, channel_count = padded_ref.shape
    for group in range(channel_count // lane_count):
        lanes = slice(group * lane_count, (group + 1) * lane_count)
        for b in range(batch_size):
            wide[group, b, :, :cols, :] = padded_ref[b, :, :, lanes].astype(jnp.float32)


def stencil(wide, params, group, b, tile_rows, tile_cols, flipped):
    kernel_size = wide.shape[2] - tile_rows + 1
    lanes = slice(group * lane_count, (group + 1) * lane_count)
    rows = [None] * tile_rows
    for q in range(kernel_size):
        for r in range(tile_rows + kernel_size - 1):
            shifted = wide[group, b, r, q : q + tile_cols, :]
            for i in range(max(0, r - kernel_size + 1), min(tile_rows, r + 1)):
                p = r - i
                tap = (kernel_size - 1 - p, kernel_size - 1 - q) if flipped else (p, q)
                term = params[pl.ds(tap[0] * kernel_size + tap[1], 1), lanes] * shifted
                rows[i] = term if rows[i] is None else rows[i] + term
    return rows


def conv_norm_kernel(padded_ref, params_ref, normed_ref, unit_ref, inv_ref, wide, smooth):
    batch_size, pad_rows, pad_cols, channel_count = padded_ref.shape
    cells = smooth.shape[1]
    tile_rows = pad_rows - kernel_side + 1
    tile_cols = pad_cols - kernel_side + 1
    spread(padded_ref, wide)
    for group in range(wide.shape[0]):

        def one(b, _):
            rows = stencil(wide, params_ref, group, b, tile_rows, tile_cols, False)
            for i, row in enumerate(rows):
                smooth[group, pl.ds((b * tile_rows + i) * tile_cols, tile_cols), :] = row
            return 0

        lax.fori_loop(0, batch_size, one, 0)
    gain = params_ref[gain_row : gain_row + 1, :]
    block = 32

    def norm(step, _):
        at = pl.ds(pl.multiple_of(step * block, block), block)
        values = jnp.concatenate([smooth[g, at, :] for g in range(wide.shape[0])], axis=1)
        average = jnp.mean(values, axis=-1, keepdims=True)
        centred = values - average
        variance = jnp.mean(centred * centred, axis=-1, keepdims=True)
        inv_std = lax.rsqrt(variance + norm_eps)
        unit = centred * inv_std
        unit_ref[at, :] = unit
        inv_ref[at, :] = inv_std
        normed_ref[at, :] = (unit * gain).astype(jnp.bfloat16)
        return 0

    lax.fori_loop(0, cells // block, norm, 0, unroll=True)


def round_up(value, unit):
    return -(-value // unit) * unit


def conv_norm(padded, params):
    batch_size, pad_rows, pad_cols, channel_count = padded.shape
    cells = batch_size * (pad_rows - kernel_side + 1) * (pad_cols - kernel_side + 1)
    groups = channel_count // lane_count
    return pl.pallas_call(
        conv_norm_kernel,
        out_shape=(
            jax.ShapeDtypeStruct((cells, channel_count), jnp.bfloat16),
            jax.ShapeDtypeStruct((cells, channel_count), jnp.float32),
            jax.ShapeDtypeStruct((cells, 1), jnp.float32),
        ),
        scratch_shapes=[
            pltpu.VMEM((groups, batch_size, pad_rows, round_up(pad_cols, 8), lane_count), jnp.float32),
            pltpu.VMEM((groups, cells, lane_count), jnp.float32),
        ],
        compiler_params=pltpu.CompilerParams(vmem_limit_bytes=16 << 20),
        cost_estimate=pl.CostEstimate(flops=2 * 49 * cells * channel_count, bytes_accessed=1 << 20, transcendentals=0),
        name="conv_norm",
    )(padded, params)


def conv_back_kernel(padded_ref, params_ref, misfit_ref, out_ref, wide):
    batch_size, tile_rows, tile_cols, channel_count = out_ref.shape
    spread(padded_ref, wide)
    for group in range(wide.shape[0]):
        lanes = slice(group * lane_count, (group + 1) * lane_count)

        def one(b, _):
            rows = stencil(wide, params_ref, group, b, tile_rows, tile_cols, True)
            for i, row in enumerate(rows):
                out_ref[b, i, :, lanes] = (misfit_ref[b, i, :, lanes] + row).astype(out_ref.dtype)
            return 0

        lax.fori_loop(0, batch_size, one, 0)


def conv_back(padded, params, misfit):
    batch_size, pad_rows, pad_cols, channel_count = padded.shape
    groups = channel_count // lane_count
    return pl.pallas_call(
        conv_back_kernel,
        out_shape=jax.ShapeDtypeStruct(misfit.shape, jnp.bfloat16),
        scratch_shapes=[
            pltpu.VMEM((groups, batch_size, pad_rows, round_up(pad_cols, 8), lane_count), jnp.float32),
        ],
        compiler_params=pltpu.CompilerParams(vmem_limit_bytes=16 << 20),
        cost_estimate=pl.CostEstimate(flops=2 * 49 * misfit.size, bytes_accessed=1 << 20, transcendentals=0),
        name="conv_back",
    )(padded, params, misfit)


def tap_sums_kernel(padded_ref, grad_ref, out_ref, wide, partial):
    batch_size, tile_rows, tile_cols, channel_count = grad_ref.shape
    kernel_size = padded_ref.shape[1] - tile_rows + 1
    spread(padded_ref, wide)
    out_ref[...] = jnp.zeros_like(out_ref)
    for group in range(wide.shape[0]):
        lanes = slice(group * lane_count, (group + 1) * lane_count)

        def one(b, _):
            grads = [grad_ref[b, i, :, lanes].astype(jnp.float32) for i in range(tile_rows)]
            for q in range(kernel_size):
                sums = [None] * kernel_size
                for r in range(tile_rows + kernel_size - 1):
                    shifted = wide[group, b, r, q : q + tile_cols, :]
                    for i in range(max(0, r - kernel_size + 1), min(tile_rows, r + 1)):
                        product = shifted * grads[i]
                        term = product.reshape(tile_cols // 8, 8, lane_count).sum(axis=0)
                        p = r - i
                        sums[p] = term if sums[p] is None else sums[p] + term
                for p in range(kernel_size):
                    at = pl.ds((p * kernel_size + q) * 8, 8)
                    partial[group, b, at, :] = sums[p]
            return 0

        lax.fori_loop(0, batch_size, one, 0)
        taps = kernel_size * kernel_size
        total = partial[group, 0]
        for b in range(1, batch_size):
            total = total + partial[group, b]
        out_ref[:taps, lanes] = total.reshape(taps, 8, lane_count).sum(axis=1)


def tap_sums(padded, grads, row_count):
    batch_size, pad_rows, pad_cols, channel_count = padded.shape
    kernel_size = pad_rows - grads.shape[1] + 1
    groups = channel_count // lane_count
    return pl.pallas_call(
        tap_sums_kernel,
        out_shape=jax.ShapeDtypeStruct((row_count, channel_count), jnp.float32),
        scratch_shapes=[
            pltpu.VMEM((groups, batch_size, pad_rows, round_up(pad_cols, 8), lane_count), jnp.float32),
            pltpu.VMEM((groups, batch_size, kernel_size * kernel_size * 8, lane_count), jnp.float32),
        ],
        compiler_params=pltpu.CompilerParams(vmem_limit_bytes=16 << 20),
        cost_estimate=pl.CostEstimate(flops=2 * 49 * grads.size, bytes_accessed=1 << 20, transcendentals=0),
        name="tap_sums",
    )(padded, grads)


def assemble_kernel(side_ref, out_mine, out_got, in_mine, in_got, out_ref, in_ref, taps_ref):
    half = pl.program_id(0)
    own = half == side_ref[0]
    count, rows, _ = out_mine.shape
    channel_count = in_ref.shape[0]

    def write(out_chunks, in_chunks):
        for k in range(count):
            out_ref[k * rows : (k + 1) * rows, :] = out_chunks[k].astype(jnp.float32)
            in_ref[:, k * rows : (k + 1) * rows] = in_chunks[k, :channel_count].astype(jnp.float32)

    @pl.when(own)
    def _():
        write(out_mine, in_mine)

    @pl.when(jnp.logical_not(own))
    def _():
        write(out_got, in_got)

    @pl.when(half == 0)
    def _():
        tail = slice(channel_count, in_mine.shape[1])
        chunks = in_mine[:, tail].astype(jnp.float32) + in_got[:, tail].astype(jnp.float32)
        groups = channel_count // in_mine.shape[2]
        step = chunks.shape[1] // groups
        pieces = [
            jnp.concatenate([chunks[k, n * step : (n + 1) * step] for n in range(groups)], axis=1)
            for k in range(count)
        ]
        taps = jnp.concatenate(pieces, axis=0)
        width = taps_ref.shape[1]
        for p in range(taps_ref.shape[0]):
            taps_ref[p] = taps[p * width : (p + 1) * width]


def assemble(side, out_mine, out_got, in_mine, in_got, channel_count, kernel_size):
    count, rows, _ = out_mine.shape
    whole = lambda value: pl.BlockSpec(value.shape, lambda i: (0,) * value.ndim)
    operands = (out_mine, out_got, in_mine, in_got)
    return pl.pallas_call(
        assemble_kernel,
        grid=(2,),
        in_specs=[pl.BlockSpec(memory_space=pltpu.SMEM)] + [whole(v) for v in operands],
        out_specs=(
            pl.BlockSpec((count * rows, channel_count), lambda i: (i, 0)),
            pl.BlockSpec((channel_count, count * rows), lambda i: (0, i)),
            pl.BlockSpec((kernel_size, kernel_size, channel_count), lambda i: (0, 0, 0)),
        ),
        out_shape=(
            jax.ShapeDtypeStruct((2 * count * rows, channel_count), jnp.float32),
            jax.ShapeDtypeStruct((channel_count, 2 * count * rows), jnp.float32),
            jax.ShapeDtypeStruct((kernel_size, kernel_size, channel_count), jnp.float32),
        ),
        compiler_params=pltpu.CompilerParams(vmem_limit_bytes=16 << 20),
        cost_estimate=pl.CostEstimate(flops=0, bytes_accessed=3 << 20, transcendentals=0),
        name="assemble",
    )(side, *operands)


def product(left, right, left_dim, right_dim):
    return lax.dot_general(
        left, right, (((left_dim,), (right_dim,)), ((), ())), preferred_element_type=jnp.float32
    )


def half_columns(ref, half):
    count = ref.shape[1] // 2
    return ref[:, pl.ds(pl.multiple_of(half * count, count), count)]


def forward_kernel(
    side_ref, normed_ref, student_ref, target_ref, w_in_ref, w_out_ref, params_ref,
    slope_ref, misfit_ref, out_grad_ref, sent_ref, kept_ref, hidden,
):
    cells, hidden_size = slope_ref.shape
    scale = params_ref[scale_row : scale_row + 1, :]
    slope_ref[...] = product(normed_ref[...], w_in_ref[...], 1, 0)
    rows, cols = 16, min(512, hidden_size)

    def gelu(step, _):
        at = pl.ds(pl.multiple_of(step * rows, rows), rows)
        for k in range(0, hidden_size, cols):
            values = slope_ref[at, k : k + cols]
            squares = values * values
            tangent = jnp.tanh(slope_coef * (values + cubic_coef * (squares * values)))
            gate = 0.5 * (1.0 + tangent)
            hidden[at, k : k + cols] = (values * gate).astype(jnp.bfloat16)
            bend = (1.0 - tangent * tangent) * (slope_coef + 3.0 * slope_coef * cubic_coef * squares)
            slope_ref[at, k : k + cols] = gate + 0.5 * values * bend
        return 0

    lax.fori_loop(0, cells // rows, gelu, 0, unroll=2)
    mlp_out = product(hidden[...], w_out_ref[...], 1, 0)
    misfit = student_ref[...].astype(jnp.float32) + scale * mlp_out
    misfit = misfit - target_ref[...].astype(jnp.float32)
    misfit_ref[...] = misfit
    out_grad_ref[...] = (scale * misfit).astype(jnp.bfloat16)
    side = side_ref[0]
    sent_ref[...] = product(half_columns(hidden, 1 - side), out_grad_ref[...], 0, 0).astype(
        jnp.bfloat16
    )
    kept_ref[...] = product(half_columns(hidden, side), out_grad_ref[...], 0, 0)


def vmem_specs(count):
    return [pl.BlockSpec(memory_space=pltpu.VMEM)] * count


def forward(side, normed, student, target, w_in, w_out, params):
    cells, channel_count = normed.shape
    hidden_size = w_in.shape[1]
    shape = jax.ShapeDtypeStruct
    return pl.pallas_call(
        forward_kernel,
        in_specs=[pl.BlockSpec(memory_space=pltpu.SMEM)] + vmem_specs(6),
        out_specs=vmem_specs(5),
        out_shape=(
            shape((cells, hidden_size), jnp.float32),
            shape((cells, channel_count), jnp.float32),
            shape((cells, channel_count), jnp.bfloat16),
            shape((hidden_size // 2, channel_count), jnp.bfloat16),
            shape((hidden_size // 2, channel_count), jnp.float32),
        ),
        scratch_shapes=[pltpu.VMEM((cells, hidden_size), jnp.bfloat16)],
        compiler_params=pltpu.CompilerParams(vmem_limit_bytes=16 << 20),
        cost_estimate=pl.CostEstimate(
            flops=6 * cells * channel_count * hidden_size,
            bytes_accessed=4 << 20,
            transcendentals=cells * hidden_size,
        ),
        name="forward",
    )(side, normed, student, target, w_in, w_out, params)


def backward_kernel(
    side_ref, slope_ref, out_grad_ref, normed_ref, unit_ref, inv_ref, w_in_ref, w_out_ref, params_ref,
    conv_grad_ref, sent_ref, kept_ref, hidden_grad, preact_grad,
):
    cells, hidden_size = slope_ref.shape
    hidden_grad[...] = product(out_grad_ref[...], w_out_ref[...], 1, 1)
    rows = 16

    def scale_by_slope(step, _):
        at = pl.ds(pl.multiple_of(step * rows, rows), rows)
        preact_grad[at, :] = (hidden_grad[at, :] * slope_ref[at, :]).astype(jnp.bfloat16)
        return 0

    lax.fori_loop(0, cells // rows, scale_by_slope, 0, unroll=2)
    unit_grad = product(preact_grad[...], w_in_ref[...], 1, 1) * params_ref[gain_row : gain_row + 1, :]
    unit = unit_ref[...]
    first_mean = jnp.mean(unit_grad, axis=-1, keepdims=True)
    second_mean = jnp.mean(unit_grad * unit, axis=-1, keepdims=True)
    conv_grad_ref[...] = (inv_ref[...] * (unit_grad - first_mean - unit * second_mean)).astype(
        jnp.bfloat16
    )
    side = side_ref[0]
    sent_ref[...] = product(half_columns(preact_grad, 1 - side), normed_ref[...], 0, 0).astype(
        jnp.bfloat16
    )
    kept_ref[...] = product(half_columns(preact_grad, side), normed_ref[...], 0, 0)


def backward(side, slope, out_grad, normed, unit_norm, inv_std, w_in, w_out, params):
    cells, channel_count = normed.shape
    hidden_size = w_in.shape[1]
    shape = jax.ShapeDtypeStruct
    return pl.pallas_call(
        backward_kernel,
        in_specs=[pl.BlockSpec(memory_space=pltpu.SMEM)] + vmem_specs(8),
        out_specs=vmem_specs(3),
        out_shape=(
            shape((cells, channel_count), jnp.bfloat16),
            shape((hidden_size // 2, channel_count), jnp.bfloat16),
            shape((hidden_size // 2, channel_count), jnp.float32),
        ),
        scratch_shapes=[
            pltpu.VMEM((cells, hidden_size), jnp.float32),
            pltpu.VMEM((cells, hidden_size), jnp.bfloat16),
        ],
        compiler_params=pltpu.CompilerParams(vmem_limit_bytes=16 << 20),
        cost_estimate=pl.CostEstimate(
            flops=6 * cells * channel_count * hidden_size, bytes_accessed=4 << 20, transcendentals=0
        ),
        name="backward",
    )(side, slope, out_grad, normed, unit_norm, inv_std, w_in, w_out, params)


def local(student, teacher, dw_weight, norm_gain, w_in, w_out, layer_scale):
    batch_size, tile_rows, tile_cols, channel_count = student.shape
    half_kernel = kernel_side // 2
    cell_total = batch_size * tile_rows * lax.axis_size("lat") * tile_cols * lax.axis_size("lon")
    tap_count = kernel_side * kernel_side
    params = jnp.concatenate(
        [dw_weight.reshape(tap_count, channel_count), norm_gain[None], layer_scale[None]]
    )
    to_inner, to_outer = edges(student, "lon", 2, half_kernel)
    from_outer = swap_outer(to_outer, "lon", True)
    from_inner = swap(to_inner, "lon", 1)
    teacher, params = after((teacher, params), (to_inner, to_outer))
    lon_padded = with_edges(student, from_inner, from_outer, "lon", 2)
    lon_padded = after(lon_padded, params)
    padded_bf = with_halo(lon_padded, "lat", 1, half_kernel, False)
    normed, unit_norm, inv_std = conv_norm(padded_bf, params)
    target = to_bands(teacher, "lat")
    upper = lax.axis_index("lat") % 2
    side = upper.astype(jnp.int32).reshape(1)
    rows = lambda block: block.reshape(-1, channel_count)
    slope, misfit, out_grad, sent, kept_out = forward(
        side, normed, rows(student), rows(target), w_in, w_out, params
    )
    got_out = swap(sent, "lat", 1)
    conv_grad, sent, kept_in = backward(
        side, slope, out_grad, normed, unit_norm, inv_std, w_in, w_out, params
    )
    got_in = swap(sent, "lat", 1)
    conv_grid = conv_grad.reshape(student.shape)
    inner, outer = [swap(edge, "lat", 1) for edge in edges(conv_grid, "lat", 1, half_kernel)]
    part_dw = tap_sums(padded_bf, conv_grid, round_up(tap_count, 64))
    (out_chunk,), (in_chunk, dw_chunk), padded_grad = sum_over_mesh(
        [[kept_out, got_out]],
        [[kept_in, got_in], [part_dw]],
        cell_total,
        conv_grid,
        inner,
        outer,
        half_kernel,
    )
    grad_student = conv_back(padded_grad, params, misfit.reshape(student.shape))
    hidden_rows = in_chunk.shape[0]
    dw_groups = [dw_chunk[:, k : k + hidden_rows] for k in range(0, channel_count, hidden_rows)]
    mixed = jnp.concatenate([in_chunk.T] + dw_groups)
    out_chunks, in_chunks = gather_sums(out_chunk[None], mixed[None])
    in_chunks = after(in_chunks, grad_student)
    sum_out, sum_in, sum_dw = assemble(
        side,
        out_chunks,
        swap(out_chunks, "lat", 1),
        in_chunks,
        swap(in_chunks, "lat", 1),
        channel_count,
        kernel_side,
    )
    return (grad_student, sum_in, sum_out, sum_dw)


def solution(mesh):
    placed = (
        P(None, "lat", "lon", None),
        P(None, None, ("lon", "lat"), None),
        P(),
        P(),
        P(),
        P(),
        P(),
    )
    return jax.shard_map(
        local,
        mesh=mesh,
        in_specs=placed,
        out_specs=(P(None, "lat", "lon", None), P(), P(), P()),
        check_vma=False,
    )
```

```python
import functools

import jax
import jax.numpy as jnp
from jax import lax
from jax.experimental import pallas as pl
from jax.experimental.pallas import tpu as pltpu
from jax.sharding import PartitionSpec as P

slope_coef = 0.7978845608028654
cubic_coef = 0.044715
norm_eps = 1e-06


def bits_of(axis):
    return [1 << k for k in range((lax.axis_size(axis) - 1).bit_length())]


def swap(value, axis, bit):
    return lax.ppermute(value, axis, [(i, i ^ bit) for i in range(lax.axis_size(axis))])


def edges(block, axis, dim, width):
    low = lax.slice_in_dim(block, 0, width, axis=dim)
    high = lax.slice_in_dim(block, block.shape[dim] - width, None, axis=dim)
    odd = lax.axis_index(axis) % 2 == 1
    return jnp.where(odd, low, high), jnp.where(odd, high, low)


def swap_outer(edge, axis, periodic):
    count = lax.axis_size(axis)
    pairs = [(i, (i + 1) % count) for i in range(1, count, 2)]
    got = lax.ppermute(edge, axis, pairs + [(j, i) for i, j in pairs])
    return got if periodic else inside(got, axis)


def inside(edge, axis):
    index = lax.axis_index(axis)
    at_end = (index == 0) | (index == lax.axis_size(axis) - 1)
    return jnp.where(at_end, jnp.zeros_like(edge), edge)


def with_edges(block, from_inner, from_outer, axis, dim):
    odd = lax.axis_index(axis) % 2 == 1
    before = jnp.where(odd, from_inner, from_outer)
    after = jnp.where(odd, from_outer, from_inner)
    return jnp.concatenate([before, block, after], axis=dim)


def with_halo(block, axis, dim, width, periodic):
    to_inner, to_outer = edges(block, axis, dim, width)
    from_outer = swap_outer(to_outer, axis, periodic)
    from_inner = swap(to_inner, axis, 1)
    return with_edges(block, from_inner, from_outer, axis, dim)


def to_bands(teacher, axis):
    batch_size, rows, cols, channel_count = teacher.shape
    band = rows // lax.axis_size(axis)
    state = teacher.reshape(batch_size, -1, band, 1, cols, channel_count)
    for bit in bits_of(axis)[::-1]:
        upper = (lax.axis_index(axis) // bit) % 2
        state = state.reshape(batch_size, 2, -1, *state.shape[2:])
        mine = lax.dynamic_index_in_dim(state, upper, axis=1, keepdims=False)
        got = swap(lax.dynamic_index_in_dim(state, 1 - upper, axis=1, keepdims=False), axis, bit)
        state = jnp.where(
            upper == 1, jnp.stack([got, mine], axis=4), jnp.stack([mine, got], axis=4)
        )
        state = state.reshape(batch_size, -1, band, 2 * state.shape[3], cols, channel_count)
    return state.reshape(batch_size, band, -1, channel_count)


def half_of(value, upper):
    count = value.shape[0] // 2
    return lax.dynamic_slice_in_dim(value, upper * count, count, axis=0)


def total_of(terms):
    total = terms[0].astype(jnp.float32)
    for term in terms[1:]:
        total = total + term.astype(jnp.float32)
    return total


def flat_rows(block):
    return block.reshape(-1, block.shape[-1])


def after(value, other):
    return lax.optimization_barrier((value, other))[0]


def exchange(parts, axis, bit, halved, sent_as, rider=None):
    upper = (lax.axis_index(axis) // bit) % 2
    if halved:
        give = [total_of([half_of(t, 1 - upper) for t in terms]) for terms in parts]
        keep = [total_of([half_of(t, upper) for t in terms]) for terms in parts]
    else:
        give = keep = [total_of(terms) for terms in parts]
    give = [value.astype(sent_as) for value in give]
    if not halved:
        keep = [value.astype(jnp.float32) for value in give]
    counts = [value.shape[0] for value in give]
    if rider is not None:
        give = give + [flat_rows(rider).astype(sent_as)]
        counts = counts + [give[-1].shape[0]]
    sent = jnp.concatenate(give, axis=0) if len(give) > 1 else give[0]
    raw = swap(sent, axis, bit)
    got = split_rows(raw, counts) if len(give) > 1 else [raw]
    parts = [[k, g] for k, g in zip(keep, got)]
    ridden = None if rider is None else got[-1].astype(rider.dtype).reshape(rider.shape)
    return parts, ridden, sent, raw


def split_rows(value, counts):
    pieces, start = [], 0
    for count in counts:
        pieces.append(lax.slice_in_dim(value, start, start + count, axis=0))
        start += count
    return pieces


def in_order(chunks, got, axis, bit):
    upper = (lax.axis_index(axis) // bit) % 2
    return jnp.where(
        upper == 1, jnp.concatenate([got, chunks]), jnp.concatenate([chunks, got])
    )


def gather_halves(chunks, axis, bit):
    return in_order(chunks, swap(chunks, axis, bit), axis, bit)


def join_kernel(place_ref, mine, got, _, out_ref):
    count = mine.shape[0]
    place = place_ref[0]
    out_ref[pl.ds(place * count, count)] = mine[...]
    out_ref[pl.ds((1 - place) * count, count)] = got[...]


def join(place, mine, got, earlier):
    shape = (2 * mine.shape[0],) + mine.shape[1:]
    return pl.pallas_call(
        join_kernel,
        in_specs=[pl.BlockSpec(memory_space=pltpu.SMEM)]
        + vmem_specs(2)
        + [pl.BlockSpec(memory_space=pl.ANY)],
        out_specs=pl.BlockSpec(memory_space=pltpu.VMEM),
        out_shape=jax.ShapeDtypeStruct(shape, mine.dtype),
        compiler_params=pltpu.CompilerParams(vmem_limit_bytes=4 << 20),
        cost_estimate=pl.CostEstimate(flops=0, bytes_accessed=1 << 18, transcendentals=0),
        name="join",
    )(place, mine, got, earlier)


def carried(axis, bit):
    index = lax.axis_index(axis)
    lower = index % bit // 2
    return lower == jnp.where(index % 2 == 0, 0, bit // 2 - 1)


def sum_stages():
    lat_stages = [("lat", bit) for bit in bits_of("lat")[1:]]
    lon_stages = [("lon", bit) for bit in bits_of("lon")]
    trail = lat_stages + lon_stages
    lead = lon_stages[1:3] + lat_stages + lon_stages[:1] + lon_stages[3:]
    return (lead, lead[:2]), (trail, [lat_stages[0], lon_stages[0]])


def sent_type(stage, stages, halved):
    return jnp.bfloat16 if stage in halved or stage == stages[-1] else jnp.float32


def finish_columns_kernel(divisor, main_ref, taps_ref, got_ref, out_ref):
    rows, channel_count = main_ref.shape
    tap_rows = taps_ref.shape[0]
    main = main_ref[...] + got_ref[:rows].astype(jnp.float32)
    out_ref[0, :channel_count] = (main / divisor).T.astype(jnp.bfloat16)
    taps = taps_ref[...] + got_ref[rows : rows + tap_rows].astype(jnp.float32)
    taps = (taps / divisor).astype(jnp.bfloat16)
    for k in range(channel_count // rows):
        at = channel_count + k * tap_rows
        out_ref[0, at : at + tap_rows] = taps[:, k * rows : (k + 1) * rows]


def finish_columns(main, taps, got, divisor):
    rows, channel_count = main.shape
    height = channel_count + channel_count // rows * taps.shape[0]
    return pl.pallas_call(
        functools.partial(finish_columns_kernel, float(divisor)),
        out_shape=jax.ShapeDtypeStruct((1, height, rows), jnp.bfloat16),
        in_specs=vmem_specs(3),
        out_specs=pl.BlockSpec(memory_space=pltpu.VMEM),
        compiler_params=pltpu.CompilerParams(vmem_limit_bytes=4 << 20),
        cost_estimate=pl.CostEstimate(flops=main.size, bytes_accessed=1 << 18, transcendentals=0),
        name="finish_columns",
    )(main, taps, got)


def sum_over_mesh(lead, trail, divisor, block, inner, outer, width):
    (lead_stages, lead_halved), (stages, halved) = sum_stages()
    dim_of = {"lat": 1, "lon": 2}
    for k, (axis, bit) in enumerate(stages):
        dim = dim_of[axis]
        stage = lead_stages[k]
        lead, _, _, _ = exchange(
            lead, *stage, stage in lead_halved, sent_type(stage, lead_stages, lead_halved)
        )
        rider = jnp.stack(edges(block, axis, dim, width)) if bit == 1 else outer
        trail, got, sent, raw = exchange(
            trail, axis, bit, (axis, bit) in halved, sent_type((axis, bit), stages, halved), rider
        )
        lead = after(lead, sent)
        if bit == 1:
            inner, outer = got[0], got[1]
        else:
            outer = jnp.where(carried(axis, bit), got, outer)
        if k + 1 == len(stages) or stages[k + 1][0] != axis:
            if axis == "lat":
                outer = inside(outer, axis)
            block = with_edges(block, inner, outer, axis, dim)
    lead = [(total_of(terms) / divisor).astype(jnp.bfloat16) for terms in lead]
    return lead, finish_columns(trail[0][0], trail[1][0], raw, divisor), block


lane_count = 128
kernel_side = 7
gain_row = kernel_side * kernel_side
scale_row = gain_row + 1


def spread(padded_ref, wide):
    batch_size, rows, cols, channel_count = padded_ref.shape
    for group in range(channel_count // lane_count):
        lanes = slice(group * lane_count, (group + 1) * lane_count)
        for b in range(batch_size):
            wide[group, b, :, :cols, :] = padded_ref[b, :, :, lanes].astype(jnp.float32)


def stencil(wide, params, group, b, tile_rows, tile_cols, flipped):
    kernel_size = wide.shape[2] - tile_rows + 1
    lanes = slice(group * lane_count, (group + 1) * lane_count)
    rows = [None] * tile_rows
    for q in range(kernel_size):
        for r in range(tile_rows + kernel_size - 1):
            shifted = wide[group, b, r, q : q + tile_cols, :]
            for i in range(max(0, r - kernel_size + 1), min(tile_rows, r + 1)):
                p = r - i
                tap = (kernel_size - 1 - p, kernel_size - 1 - q) if flipped else (p, q)
                term = params[pl.ds(tap[0] * kernel_size + tap[1], 1), lanes] * shifted
                rows[i] = term if rows[i] is None else rows[i] + term
    return rows


def conv_norm_kernel(padded_ref, params_ref, normed_ref, unit_ref, inv_ref, wide, smooth):
    batch_size, pad_rows, pad_cols, channel_count = padded_ref.shape
    cells = smooth.shape[1]
    tile_rows = pad_rows - kernel_side + 1
    tile_cols = pad_cols - kernel_side + 1
    spread(padded_ref, wide)
    for group in range(wide.shape[0]):

        def one(b, _):
            rows = stencil(wide, params_ref, group, b, tile_rows, tile_cols, False)
            for i, row in enumerate(rows):
                smooth[group, pl.ds((b * tile_rows + i) * tile_cols, tile_cols), :] = row
            return 0

        lax.fori_loop(0, batch_size, one, 0)
    gain = params_ref[gain_row : gain_row + 1, :]
    block = 32

    def norm(step, _):
        at = pl.ds(pl.multiple_of(step * block, block), block)
        values = jnp.concatenate([smooth[g, at, :] for g in range(wide.shape[0])], axis=1)
        average = jnp.mean(values, axis=-1, keepdims=True)
        centred = values - average
        variance = jnp.mean(centred * centred, axis=-1, keepdims=True)
        inv_std = lax.rsqrt(variance + norm_eps)
        unit = centred * inv_std
        unit_ref[at, :] = unit
        inv_ref[at, :] = inv_std
        normed_ref[at, :] = (unit * gain).astype(jnp.bfloat16)
        return 0

    lax.fori_loop(0, cells // block, norm, 0, unroll=True)


def round_up(value, unit):
    return -(-value // unit) * unit


def conv_norm(padded, params):
    batch_size, pad_rows, pad_cols, channel_count = padded.shape
    cells = batch_size * (pad_rows - kernel_side + 1) * (pad_cols - kernel_side + 1)
    groups = channel_count // lane_count
    return pl.pallas_call(
        conv_norm_kernel,
        out_shape=(
            jax.ShapeDtypeStruct((cells, channel_count), jnp.bfloat16),
            jax.ShapeDtypeStruct((cells, channel_count), jnp.float32),
            jax.ShapeDtypeStruct((cells, 1), jnp.float32),
        ),
        scratch_shapes=[
            pltpu.VMEM((groups, batch_size, pad_rows, round_up(pad_cols, 8), lane_count), jnp.float32),
            pltpu.VMEM((groups, cells, lane_count), jnp.float32),
        ],
        compiler_params=pltpu.CompilerParams(vmem_limit_bytes=6 << 20),
        cost_estimate=pl.CostEstimate(flops=2 * 49 * cells * channel_count, bytes_accessed=1 << 20, transcendentals=0),
        name="conv_norm",
    )(padded, params)


def conv_back_kernel(padded_ref, params_ref, misfit_ref, _, out_ref, mark_ref, wide):
    mark_ref[...] = jnp.zeros_like(mark_ref)
    batch_size, tile_rows, tile_cols, channel_count = out_ref.shape
    spread(padded_ref, wide)
    for group in range(wide.shape[0]):
        lanes = slice(group * lane_count, (group + 1) * lane_count)

        def one(b, _):
            rows = stencil(wide, params_ref, group, b, tile_rows, tile_cols, True)
            for i, row in enumerate(rows):
                out_ref[b, i, :, lanes] = (misfit_ref[b, i, :, lanes] + row).astype(out_ref.dtype)
            return 0

        lax.fori_loop(0, batch_size, one, 0)


def conv_back(padded, params, misfit, earlier):
    batch_size, pad_rows, pad_cols, channel_count = padded.shape
    groups = channel_count // lane_count
    return pl.pallas_call(
        conv_back_kernel,
        out_shape=(jax.ShapeDtypeStruct(misfit.shape, jnp.bfloat16), mark_shape),
        in_specs=vmem_specs(3) + [pl.BlockSpec(memory_space=pl.ANY)],
        out_specs=vmem_specs(2),
        scratch_shapes=[
            pltpu.VMEM((groups, batch_size, pad_rows, round_up(pad_cols, 8), lane_count), jnp.float32),
        ],
        compiler_params=pltpu.CompilerParams(vmem_limit_bytes=6 << 20),
        cost_estimate=pl.CostEstimate(flops=2 * 49 * misfit.size, bytes_accessed=1 << 20, transcendentals=0),
        name="conv_back",
    )(padded, params, misfit, earlier)


def tap_sums_kernel(padded_ref, grad_ref, out_ref, wide, partial):
    batch_size, tile_rows, tile_cols, channel_count = grad_ref.shape
    kernel_size = padded_ref.shape[1] - tile_rows + 1
    spread(padded_ref, wide)
    out_ref[...] = jnp.zeros_like(out_ref)
    for group in range(wide.shape[0]):
        lanes = slice(group * lane_count, (group + 1) * lane_count)

        def one(b, _):
            grads = [grad_ref[b, i, :, lanes].astype(jnp.float32) for i in range(tile_rows)]
            for q in range(kernel_size):
                sums = [None] * kernel_size
                for r in range(tile_rows + kernel_size - 1):
                    shifted = wide[group, b, r, q : q + tile_cols, :]
                    for i in range(max(0, r - kernel_size + 1), min(tile_rows, r + 1)):
                        product = shifted * grads[i]
                        term = product.reshape(tile_cols // 8, 8, lane_count).sum(axis=0)
                        p = r - i
                        sums[p] = term if sums[p] is None else sums[p] + term
                for p in range(kernel_size):
                    at = pl.ds((p * kernel_size + q) * 8, 8)
                    partial[group, b, at, :] = sums[p]
            return 0

        lax.fori_loop(0, batch_size, one, 0)
        taps = kernel_size * kernel_size
        total = partial[group, 0]
        for b in range(1, batch_size):
            total = total + partial[group, b]
        out_ref[:taps, lanes] = total.reshape(taps, 8, lane_count).sum(axis=1)


def tap_sums(padded, grads, row_count):
    batch_size, pad_rows, pad_cols, channel_count = padded.shape
    kernel_size = pad_rows - grads.shape[1] + 1
    groups = channel_count // lane_count
    return pl.pallas_call(
        tap_sums_kernel,
        out_shape=jax.ShapeDtypeStruct((row_count, channel_count), jnp.float32),
        scratch_shapes=[
            pltpu.VMEM((groups, batch_size, pad_rows, round_up(pad_cols, 8), lane_count), jnp.float32),
            pltpu.VMEM((groups, batch_size, kernel_size * kernel_size * 8, lane_count), jnp.float32),
        ],
        compiler_params=pltpu.CompilerParams(vmem_limit_bytes=6 << 20),
        cost_estimate=pl.CostEstimate(flops=2 * 49 * grads.size, bytes_accessed=1 << 20, transcendentals=0),
        name="tap_sums",
    )(padded, grads)


def assemble_rows_kernel(side_ref, mine, got, _, out_ref, mark_ref):
    mark_ref[...] = jnp.zeros_like(mark_ref)
    own = pl.program_id(0) == side_ref[0]
    count, rows, _ = mine.shape
    for k in range(count):
        chunk = jnp.where(own, mine[k].astype(jnp.float32), got[k].astype(jnp.float32))
        out_ref[k * rows : (k + 1) * rows, :] = chunk


def assemble_columns_kernel(side_ref, mine, got, out_ref, taps_ref):
    half = pl.program_id(0)
    own = half == side_ref[0]
    count, _, cols = mine.shape
    channel_count = out_ref.shape[0]
    for k in range(count):
        chunk = jnp.where(
            own,
            mine[k, :channel_count].astype(jnp.float32),
            got[k, :channel_count].astype(jnp.float32),
        )
        out_ref[:, k * cols : (k + 1) * cols] = chunk

    @pl.when(half == 0)
    def _():
        tail = slice(channel_count, mine.shape[1])
        chunks = mine[:, tail].astype(jnp.float32) + got[:, tail].astype(jnp.float32)
        groups = channel_count // cols
        step = chunks.shape[1] // groups
        pieces = [
            jnp.concatenate([chunks[k, n * step : (n + 1) * step] for n in range(groups)], axis=1)
            for k in range(count)
        ]
        taps = jnp.concatenate(pieces, axis=0)
        width = taps_ref.shape[1]
        for p in range(taps_ref.shape[0]):
            taps_ref[p] = taps[p * width : (p + 1) * width]


mark_shape = jax.ShapeDtypeStruct((8, 128), jnp.float32)


def whole_block(value):
    return pl.BlockSpec(value.shape, lambda i: (0,) * len(value.shape))


def assemble_rows(side, mine, got, earlier):
    count, rows, cols = mine.shape
    return pl.pallas_call(
        assemble_rows_kernel,
        grid=(2,),
        in_specs=[pl.BlockSpec(memory_space=pltpu.SMEM), whole_block(mine), whole_block(got)]
        + [pl.BlockSpec(memory_space=pl.ANY)],
        out_specs=(pl.BlockSpec((count * rows, cols), lambda i: (i, 0)), whole_block(mark_shape)),
        out_shape=(jax.ShapeDtypeStruct((2 * count * rows, cols), jnp.float32), mark_shape),
        compiler_params=pltpu.CompilerParams(vmem_limit_bytes=6 << 20),
        cost_estimate=pl.CostEstimate(flops=0, bytes_accessed=3 << 19, transcendentals=0),
        name="assemble_rows",
    )(side, mine, got, earlier)


def assemble_columns(side, mine, got, channel_count):
    count, _, cols = mine.shape
    return pl.pallas_call(
        assemble_columns_kernel,
        grid=(2,),
        in_specs=[pl.BlockSpec(memory_space=pltpu.SMEM), whole_block(mine), whole_block(got)],
        out_specs=(
            pl.BlockSpec((channel_count, count * cols), lambda i: (0, i)),
            pl.BlockSpec((kernel_side, kernel_side, channel_count), lambda i: (0, 0, 0)),
        ),
        out_shape=(
            jax.ShapeDtypeStruct((channel_count, 2 * count * cols), jnp.float32),
            jax.ShapeDtypeStruct((kernel_side, kernel_side, channel_count), jnp.float32),
        ),
        compiler_params=pltpu.CompilerParams(vmem_limit_bytes=6 << 20),
        cost_estimate=pl.CostEstimate(flops=0, bytes_accessed=3 << 19, transcendentals=0),
        name="assemble_columns",
    )(side, mine, got)


def product(left, right, left_dim, right_dim):
    return lax.dot_general(
        left, right, (((left_dim,), (right_dim,)), ((), ())), preferred_element_type=jnp.float32
    )


def half_columns(ref, half):
    count = ref.shape[1] // 2
    return ref[:, pl.ds(pl.multiple_of(half * count, count), count)]


def forward_kernel(
    side_ref, normed_ref, student_ref, target_ref, w_in_ref, w_out_ref, params_ref,
    slope_ref, misfit_ref, out_grad_ref, sent_ref, kept_ref, hidden,
):
    cells, hidden_size = slope_ref.shape
    scale = params_ref[scale_row : scale_row + 1, :]
    slope_ref[...] = product(normed_ref[...], w_in_ref[...], 1, 0)
    rows, cols = 16, min(512, hidden_size)

    def gelu(step, _):
        at = pl.ds(pl.multiple_of(step * rows, rows), rows)
        for k in range(0, hidden_size, cols):
            values = slope_ref[at, k : k + cols]
            squares = values * values
            tangent = jnp.tanh(slope_coef * (values + cubic_coef * (squares * values)))
            gate = 0.5 * (1.0 + tangent)
            hidden[at, k : k + cols] = (values * gate).astype(jnp.bfloat16)
            bend = (1.0 - tangent * tangent) * (slope_coef + 3.0 * slope_coef * cubic_coef * squares)
            slope_ref[at, k : k + cols] = gate + 0.5 * values * bend
        return 0

    lax.fori_loop(0, cells // rows, gelu, 0, unroll=2)
    mlp_out = product(hidden[...], w_out_ref[...], 1, 0)
    misfit = student_ref[...].astype(jnp.float32) + scale * mlp_out
    misfit = misfit - target_ref[...].astype(jnp.float32)
    misfit_ref[...] = misfit
    out_grad_ref[...] = (scale * misfit).astype(jnp.bfloat16)
    side = side_ref[0]
    sent_ref[...] = product(half_columns(hidden, 1 - side), out_grad_ref[...], 0, 0).astype(
        jnp.bfloat16
    )
    kept_ref[...] = product(half_columns(hidden, side), out_grad_ref[...], 0, 0)


def vmem_specs(count):
    return [pl.BlockSpec(memory_space=pltpu.VMEM)] * count


def forward(side, normed, student, target, w_in, w_out, params):
    cells, channel_count = normed.shape
    hidden_size = w_in.shape[1]
    shape = jax.ShapeDtypeStruct
    return pl.pallas_call(
        forward_kernel,
        in_specs=[pl.BlockSpec(memory_space=pltpu.SMEM)] + vmem_specs(6),
        out_specs=vmem_specs(5),
        out_shape=(
            shape((cells, hidden_size), jnp.float32),
            shape((cells, channel_count), jnp.float32),
            shape((cells, channel_count), jnp.bfloat16),
            shape((hidden_size // 2, channel_count), jnp.bfloat16),
            shape((hidden_size // 2, channel_count), jnp.float32),
        ),
        scratch_shapes=[pltpu.VMEM((cells, hidden_size), jnp.bfloat16)],
        compiler_params=pltpu.CompilerParams(vmem_limit_bytes=6 << 20),
        cost_estimate=pl.CostEstimate(
            flops=6 * cells * channel_count * hidden_size,
            bytes_accessed=4 << 20,
            transcendentals=cells * hidden_size,
        ),
        name="forward",
    )(side, normed, student, target, w_in, w_out, params)


def backward_kernel(
    side_ref, slope_ref, out_grad_ref, normed_ref, unit_ref, inv_ref, w_in_ref, w_out_ref, params_ref,
    conv_grad_ref, sent_ref, kept_ref, hidden_grad, preact_grad,
):
    cells, hidden_size = slope_ref.shape
    hidden_grad[...] = product(out_grad_ref[...], w_out_ref[...], 1, 1)
    rows = 16

    def scale_by_slope(step, _):
        at = pl.ds(pl.multiple_of(step * rows, rows), rows)
        preact_grad[at, :] = (hidden_grad[at, :] * slope_ref[at, :]).astype(jnp.bfloat16)
        return 0

    lax.fori_loop(0, cells // rows, scale_by_slope, 0, unroll=2)
    unit_grad = product(preact_grad[...], w_in_ref[...], 1, 1) * params_ref[gain_row : gain_row + 1, :]
    unit = unit_ref[...]
    first_mean = jnp.mean(unit_grad, axis=-1, keepdims=True)
    second_mean = jnp.mean(unit_grad * unit, axis=-1, keepdims=True)
    conv_grad_ref[...] = (inv_ref[...] * (unit_grad - first_mean - unit * second_mean)).astype(
        jnp.bfloat16
    )
    side = side_ref[0]
    sent_ref[...] = product(half_columns(preact_grad, 1 - side), normed_ref[...], 0, 0).astype(
        jnp.bfloat16
    )
    kept_ref[...] = product(half_columns(preact_grad, side), normed_ref[...], 0, 0)


def backward(side, slope, out_grad, normed, unit_norm, inv_std, w_in, w_out, params):
    cells, channel_count = normed.shape
    hidden_size = w_in.shape[1]
    shape = jax.ShapeDtypeStruct
    return pl.pallas_call(
        backward_kernel,
        in_specs=[pl.BlockSpec(memory_space=pltpu.SMEM)] + vmem_specs(8),
        out_specs=vmem_specs(3),
        out_shape=(
            shape((cells, channel_count), jnp.bfloat16),
            shape((hidden_size // 2, channel_count), jnp.bfloat16),
            shape((hidden_size // 2, channel_count), jnp.float32),
        ),
        scratch_shapes=[
            pltpu.VMEM((cells, hidden_size), jnp.float32),
            pltpu.VMEM((cells, hidden_size), jnp.bfloat16),
        ],
        compiler_params=pltpu.CompilerParams(vmem_limit_bytes=6 << 20),
        cost_estimate=pl.CostEstimate(
            flops=6 * cells * channel_count * hidden_size, bytes_accessed=4 << 20, transcendentals=0
        ),
        name="backward",
    )(side, slope, out_grad, normed, unit_norm, inv_std, w_in, w_out, params)


def local(student, teacher, dw_weight, norm_gain, w_in, w_out, layer_scale):
    batch_size, tile_rows, tile_cols, channel_count = student.shape
    half_kernel = kernel_side // 2
    cell_total = batch_size * tile_rows * lax.axis_size("lat") * tile_cols * lax.axis_size("lon")
    tap_count = kernel_side * kernel_side
    params = jnp.concatenate(
        [dw_weight.reshape(tap_count, channel_count), norm_gain[None], layer_scale[None]]
    )
    to_inner, to_outer = edges(student, "lon", 2, half_kernel)
    from_outer = swap_outer(to_outer, "lon", True)
    from_inner = swap(to_inner, "lon", 1)
    teacher, params = after((teacher, params), (to_inner, to_outer))
    lon_padded = with_edges(student, from_inner, from_outer, "lon", 2)
    lon_padded = after(lon_padded, params)
    padded_bf = with_halo(lon_padded, "lat", 1, half_kernel, False)
    normed, unit_norm, inv_std = conv_norm(padded_bf, params)
    target = to_bands(teacher, "lat")
    upper = lax.axis_index("lat") % 2
    side = upper.astype(jnp.int32).reshape(1)
    rows = lambda block: block.reshape(-1, channel_count)
    slope, misfit, out_grad, sent, kept_out = forward(
        side, normed, rows(student), rows(target), w_in, w_out, params
    )
    got_out = swap(sent, "lat", 1)
    conv_grad, sent, kept_in = backward(
        side, slope, out_grad, normed, unit_norm, inv_std, w_in, w_out, params
    )
    got_in = swap(sent, "lat", 1)
    conv_grid = conv_grad.reshape(student.shape)
    inner, outer = [swap(edge, "lat", 1) for edge in edges(conv_grid, "lat", 1, half_kernel)]
    part_dw = tap_sums(padded_bf, conv_grid, round_up(tap_count, 64))
    (out_chunk,), in_chunk, padded_grad = sum_over_mesh(
        [[kept_out, got_out]],
        [[kept_in, got_in], [part_dw]],
        cell_total,
        conv_grid,
        inner,
        outer,
        half_kernel,
    )
    out_chunks, in_chunks = out_chunk[None], in_chunk
    (_, out_halved), (_, in_halved) = sum_stages()
    for out_stage, in_stage in zip(out_halved[::-1], in_halved[::-1]):
        out_chunks = gather_halves(out_chunks, *out_stage)
        in_mine, in_got = in_chunks, swap(in_chunks, *in_stage)
        if in_stage != in_halved[0]:
            in_chunks = in_order(in_mine, in_got, *in_stage)
    grad_student, mark = conv_back(padded_grad, params, misfit.reshape(student.shape), out_chunks)
    sum_out, mark = assemble_rows(side, out_chunks, swap(out_chunks, "lat", 1), mark)
    axis, bit = in_halved[0]
    place = ((lax.axis_index(axis) // bit) % 2).astype(jnp.int32).reshape(1)
    in_chunks = join(place, in_mine, in_got, mark)
    sum_in, sum_dw = assemble_columns(side, in_chunks, swap(in_chunks, "lat", 1), channel_count)
    return (grad_student, sum_in, sum_out, sum_dw)


def solution(mesh):
    placed = (
        P(None, "lat", "lon", None),
        P(None, None, ("lon", "lat"), None),
        P(),
        P(),
        P(),
        P(),
        P(),
    )
    return jax.shard_map(
        local,
        mesh=mesh,
        in_specs=placed,
        out_specs=(P(None, "lat", "lon", None), P(), P(), P()),
        check_vma=False,
    )
```

```python
import functools

import jax
import jax.numpy as jnp
from jax import lax
from jax.experimental import pallas as pl
from jax.experimental.pallas import tpu as pltpu
from jax.sharding import PartitionSpec as P

slope_coef = 0.7978845608028654
cubic_coef = 0.044715
norm_eps = 1e-06


def bits_of(axis):
    return [1 << k for k in range((lax.axis_size(axis) - 1).bit_length())]


def swap(value, axis, bit):
    return lax.ppermute(value, axis, [(i, i ^ bit) for i in range(lax.axis_size(axis))])


def edges(block, axis, dim, width):
    low = lax.slice_in_dim(block, 0, width, axis=dim)
    high = lax.slice_in_dim(block, block.shape[dim] - width, None, axis=dim)
    odd = lax.axis_index(axis) % 2 == 1
    return jnp.where(odd, low, high), jnp.where(odd, high, low)


def swap_outer(edge, axis, periodic):
    count = lax.axis_size(axis)
    pairs = [(i, (i + 1) % count) for i in range(1, count, 2)]
    got = lax.ppermute(edge, axis, pairs + [(j, i) for i, j in pairs])
    return got if periodic else inside(got, axis)


def inside(edge, axis):
    index = lax.axis_index(axis)
    at_end = (index == 0) | (index == lax.axis_size(axis) - 1)
    return jnp.where(at_end, jnp.zeros_like(edge), edge)


def with_edges(block, from_inner, from_outer, axis, dim):
    odd = lax.axis_index(axis) % 2 == 1
    before = jnp.where(odd, from_inner, from_outer)
    after = jnp.where(odd, from_outer, from_inner)
    return jnp.concatenate([before, block, after], axis=dim)


def with_halo(block, axis, dim, width, periodic):
    to_inner, to_outer = edges(block, axis, dim, width)
    from_outer = swap_outer(to_outer, axis, periodic)
    from_inner = swap(to_inner, axis, 1)
    return with_edges(block, from_inner, from_outer, axis, dim)


def to_bands(teacher, axis):
    batch_size, rows, cols, channel_count = teacher.shape
    band = rows // lax.axis_size(axis)
    state = teacher.reshape(batch_size, -1, band, 1, cols, channel_count)
    for bit in bits_of(axis)[::-1]:
        upper = (lax.axis_index(axis) // bit) % 2
        state = state.reshape(batch_size, 2, -1, *state.shape[2:])
        mine = lax.dynamic_index_in_dim(state, upper, axis=1, keepdims=False)
        got = swap(lax.dynamic_index_in_dim(state, 1 - upper, axis=1, keepdims=False), axis, bit)
        state = jnp.where(
            upper == 1, jnp.stack([got, mine], axis=4), jnp.stack([mine, got], axis=4)
        )
        state = state.reshape(batch_size, -1, band, 2 * state.shape[3], cols, channel_count)
    return state.reshape(batch_size, band, -1, channel_count)


def half_of(value, upper):
    count = value.shape[0] // 2
    return lax.dynamic_slice_in_dim(value, upper * count, count, axis=0)


def total_of(terms):
    total = terms[0].astype(jnp.float32)
    for term in terms[1:]:
        total = total + term.astype(jnp.float32)
    return total


def flat_rows(block):
    return block.reshape(-1, block.shape[-1])


def after(value, other):
    return lax.optimization_barrier((value, other))[0]


def exchange(parts, axis, bit, halved, sent_as, rider=None):
    upper = (lax.axis_index(axis) // bit) % 2
    if halved:
        give = [total_of([half_of(t, 1 - upper) for t in terms]) for terms in parts]
        keep = [total_of([half_of(t, upper) for t in terms]) for terms in parts]
    else:
        give = keep = [total_of(terms) for terms in parts]
    give = [value.astype(sent_as) for value in give]
    if not halved:
        keep = [value.astype(jnp.float32) for value in give]
    counts = [value.shape[0] for value in give]
    if rider is not None:
        give = give + [flat_rows(rider).astype(sent_as)]
        counts = counts + [give[-1].shape[0]]
    sent = jnp.concatenate(give, axis=0) if len(give) > 1 else give[0]
    raw = swap(sent, axis, bit)
    got = split_rows(raw, counts) if len(give) > 1 else [raw]
    parts = [[k, g] for k, g in zip(keep, got)]
    ridden = None if rider is None else got[-1].astype(rider.dtype).reshape(rider.shape)
    return parts, ridden, sent, raw


def split_rows(value, counts):
    pieces, start = [], 0
    for count in counts:
        pieces.append(lax.slice_in_dim(value, start, start + count, axis=0))
        start += count
    return pieces


def in_order(chunks, got, axis, bit):
    upper = (lax.axis_index(axis) // bit) % 2
    return jnp.where(
        upper == 1, jnp.concatenate([got, chunks]), jnp.concatenate([chunks, got])
    )


def gather_halves(chunks, axis, bit):
    return in_order(chunks, swap(chunks, axis, bit), axis, bit)


def join_kernel(place_ref, mine, got, _, out_ref):
    count = mine.shape[0]
    place = place_ref[0]
    out_ref[pl.ds(place * count, count)] = mine[...]
    out_ref[pl.ds((1 - place) * count, count)] = got[...]


def join(place, mine, got, earlier):
    shape = (2 * mine.shape[0],) + mine.shape[1:]
    return pl.pallas_call(
        join_kernel,
        in_specs=[pl.BlockSpec(memory_space=pltpu.SMEM)]
        + vmem_specs(2)
        + [pl.BlockSpec(memory_space=pl.ANY)],
        out_specs=pl.BlockSpec(memory_space=pltpu.VMEM),
        out_shape=jax.ShapeDtypeStruct(shape, mine.dtype),
        compiler_params=pltpu.CompilerParams(vmem_limit_bytes=4 << 20),
        cost_estimate=pl.CostEstimate(flops=0, bytes_accessed=1 << 18, transcendentals=0),
        name="join",
    )(place, mine, got, earlier)


def carried(axis, bit):
    index = lax.axis_index(axis)
    lower = index % bit // 2
    return lower == jnp.where(index % 2 == 0, 0, bit // 2 - 1)


def sum_stages():
    lat_stages = [("lat", bit) for bit in bits_of("lat")[1:]]
    lon_stages = [("lon", bit) for bit in bits_of("lon")]
    trail = lat_stages + lon_stages
    lead = lon_stages[1:3] + lat_stages + lon_stages[:1] + lon_stages[3:]
    return (lead, lead[:2]), (trail, [lat_stages[0], lon_stages[0]])


def sent_type(stage, stages, halved):
    return jnp.bfloat16 if stage in halved or stage == stages[-1] else jnp.float32


def finish_columns_kernel(divisor, main_ref, taps_ref, got_ref, out_ref):
    rows, channel_count = main_ref.shape
    tap_rows = taps_ref.shape[0]
    main = main_ref[...] + got_ref[:rows].astype(jnp.float32)
    out_ref[0, :channel_count] = (main / divisor).T.astype(jnp.bfloat16)
    taps = taps_ref[...] + got_ref[rows : rows + tap_rows].astype(jnp.float32)
    taps = (taps / divisor).astype(jnp.bfloat16)
    for k in range(channel_count // rows):
        at = channel_count + k * tap_rows
        out_ref[0, at : at + tap_rows] = taps[:, k * rows : (k + 1) * rows]


def finish_columns(main, taps, got, divisor):
    rows, channel_count = main.shape
    height = channel_count + channel_count // rows * taps.shape[0]
    return pl.pallas_call(
        functools.partial(finish_columns_kernel, float(divisor)),
        out_shape=jax.ShapeDtypeStruct((1, height, rows), jnp.bfloat16),
        in_specs=vmem_specs(3),
        out_specs=pl.BlockSpec(memory_space=pltpu.VMEM),
        compiler_params=pltpu.CompilerParams(vmem_limit_bytes=4 << 20),
        cost_estimate=pl.CostEstimate(flops=main.size, bytes_accessed=1 << 18, transcendentals=0),
        name="finish_columns",
    )(main, taps, got)


def sum_over_mesh(lead, trail, divisor, block, inner, outer, width):
    (lead_stages, lead_halved), (stages, halved) = sum_stages()
    dim_of = {"lat": 1, "lon": 2}
    for k, (axis, bit) in enumerate(stages):
        dim = dim_of[axis]
        stage = lead_stages[k]
        lead, _, _, _ = exchange(
            lead, *stage, stage in lead_halved, sent_type(stage, lead_stages, lead_halved)
        )
        rider = jnp.stack(edges(block, axis, dim, width)) if bit == 1 else outer
        trail, got, sent, raw = exchange(
            trail, axis, bit, (axis, bit) in halved, sent_type((axis, bit), stages, halved), rider
        )
        lead = after(lead, sent)
        if bit == 1:
            inner, outer = got[0], got[1]
        else:
            outer = jnp.where(carried(axis, bit), got, outer)
        if k + 1 == len(stages) or stages[k + 1][0] != axis:
            if axis == "lat":
                outer = inside(outer, axis)
            block = with_edges(block, inner, outer, axis, dim)
    lead = [(total_of(terms) / divisor).astype(jnp.bfloat16) for terms in lead]
    return lead, finish_columns(trail[0][0], trail[1][0], raw, divisor), block


lane_count = 128
kernel_side = 7
gain_row = kernel_side * kernel_side
scale_row = gain_row + 1


def spread(padded_ref, wide):
    batch_size, rows, cols, channel_count = padded_ref.shape
    for group in range(channel_count // lane_count):
        lanes = slice(group * lane_count, (group + 1) * lane_count)
        for b in range(batch_size):
            wide[group, b, :, :cols, :] = padded_ref[b, :, :, lanes].astype(jnp.float32)


def stencil(wide, params, group, b, tile_rows, tile_cols, flipped):
    kernel_size = wide.shape[2] - tile_rows + 1
    lanes = slice(group * lane_count, (group + 1) * lane_count)
    rows = [None] * tile_rows
    for q in range(kernel_size):
        for r in range(tile_rows + kernel_size - 1):
            shifted = wide[group, b, r, q : q + tile_cols, :]
            for i in range(max(0, r - kernel_size + 1), min(tile_rows, r + 1)):
                p = r - i
                tap = (kernel_size - 1 - p, kernel_size - 1 - q) if flipped else (p, q)
                term = params[pl.ds(tap[0] * kernel_size + tap[1], 1), lanes] * shifted
                rows[i] = term if rows[i] is None else rows[i] + term
    return rows


def conv_norm_kernel(padded_ref, params_ref, normed_ref, unit_ref, inv_ref, wide, smooth):
    batch_size, pad_rows, pad_cols, channel_count = padded_ref.shape
    cells = smooth.shape[1]
    tile_rows = pad_rows - kernel_side + 1
    tile_cols = pad_cols - kernel_side + 1
    spread(padded_ref, wide)
    for group in range(wide.shape[0]):

        def one(b, _):
            rows = stencil(wide, params_ref, group, b, tile_rows, tile_cols, False)
            for i, row in enumerate(rows):
                smooth[group, pl.ds((b * tile_rows + i) * tile_cols, tile_cols), :] = row
            return 0

        for b in range(batch_size):
            one(b, 0)
    gain = params_ref[gain_row : gain_row + 1, :]
    block = 32

    def norm(step, _):
        at = pl.ds(pl.multiple_of(step * block, block), block)
        values = jnp.concatenate([smooth[g, at, :] for g in range(wide.shape[0])], axis=1)
        average = jnp.mean(values, axis=-1, keepdims=True)
        centred = values - average
        variance = jnp.mean(centred * centred, axis=-1, keepdims=True)
        inv_std = lax.rsqrt(variance + norm_eps)
        unit = centred * inv_std
        unit_ref[at, :] = unit
        inv_ref[at, :] = inv_std
        normed_ref[at, :] = (unit * gain).astype(jnp.bfloat16)
        return 0

    lax.fori_loop(0, cells // block, norm, 0, unroll=True)


def round_up(value, unit):
    return -(-value // unit) * unit


def conv_norm(padded, params):
    batch_size, pad_rows, pad_cols, channel_count = padded.shape
    cells = batch_size * (pad_rows - kernel_side + 1) * (pad_cols - kernel_side + 1)
    groups = channel_count // lane_count
    return pl.pallas_call(
        conv_norm_kernel,
        out_shape=(
            jax.ShapeDtypeStruct((cells, channel_count), jnp.bfloat16),
            jax.ShapeDtypeStruct((cells, channel_count), jnp.float32),
            jax.ShapeDtypeStruct((cells, 1), jnp.float32),
        ),
        scratch_shapes=[
            pltpu.VMEM((groups, batch_size, pad_rows, round_up(pad_cols, 8), lane_count), jnp.float32),
            pltpu.VMEM((groups, cells, lane_count), jnp.float32),
        ],
        compiler_params=pltpu.CompilerParams(vmem_limit_bytes=6 << 20),
        cost_estimate=pl.CostEstimate(flops=2 * 49 * cells * channel_count, bytes_accessed=1 << 20, transcendentals=0),
        name="conv_norm",
    )(padded, params)


def conv_back_kernel(padded_ref, params_ref, misfit_ref, _, out_ref, mark_ref, wide):
    mark_ref[...] = jnp.zeros_like(mark_ref)
    batch_size, tile_rows, tile_cols, channel_count = out_ref.shape
    spread(padded_ref, wide)
    for group in range(wide.shape[0]):
        lanes = slice(group * lane_count, (group + 1) * lane_count)

        def one(b, _):
            rows = stencil(wide, params_ref, group, b, tile_rows, tile_cols, True)
            for i, row in enumerate(rows):
                out_ref[b, i, :, lanes] = (misfit_ref[b, i, :, lanes] + row).astype(out_ref.dtype)
            return 0

        for b in range(batch_size):
            one(b, 0)


def conv_back(padded, params, misfit, earlier):
    batch_size, pad_rows, pad_cols, channel_count = padded.shape
    groups = channel_count // lane_count
    return pl.pallas_call(
        conv_back_kernel,
        out_shape=(jax.ShapeDtypeStruct(misfit.shape, jnp.bfloat16), mark_shape),
        in_specs=vmem_specs(3) + [pl.BlockSpec(memory_space=pl.ANY)],
        out_specs=vmem_specs(2),
        scratch_shapes=[
            pltpu.VMEM((groups, batch_size, pad_rows, round_up(pad_cols, 8), lane_count), jnp.float32),
        ],
        compiler_params=pltpu.CompilerParams(vmem_limit_bytes=6 << 20),
        cost_estimate=pl.CostEstimate(flops=2 * 49 * misfit.size, bytes_accessed=1 << 20, transcendentals=0),
        name="conv_back",
    )(padded, params, misfit, earlier)


def tap_sums_kernel(padded_ref, grad_ref, out_ref, wide, partial):
    batch_size, tile_rows, tile_cols, channel_count = grad_ref.shape
    kernel_size = padded_ref.shape[1] - tile_rows + 1
    spread(padded_ref, wide)
    out_ref[...] = jnp.zeros_like(out_ref)
    for group in range(wide.shape[0]):
        lanes = slice(group * lane_count, (group + 1) * lane_count)

        def one(b, _):
            grads = [grad_ref[b, i, :, lanes].astype(jnp.float32) for i in range(tile_rows)]
            for q in range(kernel_size):
                sums = [None] * kernel_size
                for r in range(tile_rows + kernel_size - 1):
                    shifted = wide[group, b, r, q : q + tile_cols, :]
                    for i in range(max(0, r - kernel_size + 1), min(tile_rows, r + 1)):
                        product = shifted * grads[i]
                        term = product.reshape(tile_cols // 8, 8, lane_count).sum(axis=0)
                        p = r - i
                        sums[p] = term if sums[p] is None else sums[p] + term
                for p in range(kernel_size):
                    at = pl.ds((p * kernel_size + q) * 8, 8)
                    partial[group, b, at, :] = sums[p]
            return 0

        for b in range(batch_size):
            one(b, 0)
        taps = kernel_size * kernel_size
        total = partial[group, 0]
        for b in range(1, batch_size):
            total = total + partial[group, b]
        out_ref[:taps, lanes] = total.reshape(taps, 8, lane_count).sum(axis=1)


def tap_sums(padded, grads, row_count):
    batch_size, pad_rows, pad_cols, channel_count = padded.shape
    kernel_size = pad_rows - grads.shape[1] + 1
    groups = channel_count // lane_count
    return pl.pallas_call(
        tap_sums_kernel,
        out_shape=jax.ShapeDtypeStruct((row_count, channel_count), jnp.float32),
        scratch_shapes=[
            pltpu.VMEM((groups, batch_size, pad_rows, round_up(pad_cols, 8), lane_count), jnp.float32),
            pltpu.VMEM((groups, batch_size, kernel_size * kernel_size * 8, lane_count), jnp.float32),
        ],
        compiler_params=pltpu.CompilerParams(vmem_limit_bytes=6 << 20),
        cost_estimate=pl.CostEstimate(flops=2 * 49 * grads.size, bytes_accessed=1 << 20, transcendentals=0),
        name="tap_sums",
    )(padded, grads)


def assemble_rows_kernel(side_ref, mine, got, _, out_ref, mark_ref):
    mark_ref[...] = jnp.zeros_like(mark_ref)
    own = pl.program_id(0) == side_ref[0]
    count, rows, _ = mine.shape
    for k in range(count):
        chunk = jnp.where(own, mine[k].astype(jnp.float32), got[k].astype(jnp.float32))
        out_ref[k * rows : (k + 1) * rows, :] = chunk


def assemble_columns_kernel(side_ref, mine, got, out_ref, taps_ref):
    half = pl.program_id(0)
    own = half == side_ref[0]
    count, _, cols = mine.shape
    channel_count = out_ref.shape[0]
    for k in range(count):
        chunk = jnp.where(
            own,
            mine[k, :channel_count].astype(jnp.float32),
            got[k, :channel_count].astype(jnp.float32),
        )
        out_ref[:, k * cols : (k + 1) * cols] = chunk

    @pl.when(half == 0)
    def _():
        tail = slice(channel_count, mine.shape[1])
        chunks = mine[:, tail].astype(jnp.float32) + got[:, tail].astype(jnp.float32)
        groups = channel_count // cols
        step = chunks.shape[1] // groups
        pieces = [
            jnp.concatenate([chunks[k, n * step : (n + 1) * step] for n in range(groups)], axis=1)
            for k in range(count)
        ]
        taps = jnp.concatenate(pieces, axis=0)
        width = taps_ref.shape[1]
        for p in range(taps_ref.shape[0]):
            taps_ref[p] = taps[p * width : (p + 1) * width]


mark_shape = jax.ShapeDtypeStruct((8, 128), jnp.float32)


def whole_block(value):
    return pl.BlockSpec(value.shape, lambda i: (0,) * len(value.shape))


def assemble_rows(side, mine, got, earlier):
    count, rows, cols = mine.shape
    return pl.pallas_call(
        assemble_rows_kernel,
        grid=(2,),
        in_specs=[pl.BlockSpec(memory_space=pltpu.SMEM), whole_block(mine), whole_block(got)]
        + [pl.BlockSpec(memory_space=pl.ANY)],
        out_specs=(pl.BlockSpec((count * rows, cols), lambda i: (i, 0)), whole_block(mark_shape)),
        out_shape=(jax.ShapeDtypeStruct((2 * count * rows, cols), jnp.float32), mark_shape),
        compiler_params=pltpu.CompilerParams(vmem_limit_bytes=6 << 20),
        cost_estimate=pl.CostEstimate(flops=0, bytes_accessed=3 << 19, transcendentals=0),
        name="assemble_rows",
    )(side, mine, got, earlier)


def assemble_columns(side, mine, got, channel_count):
    count, _, cols = mine.shape
    return pl.pallas_call(
        assemble_columns_kernel,
        grid=(2,),
        in_specs=[pl.BlockSpec(memory_space=pltpu.SMEM), whole_block(mine), whole_block(got)],
        out_specs=(
            pl.BlockSpec((channel_count, count * cols), lambda i: (0, i)),
            pl.BlockSpec((kernel_side, kernel_side, channel_count), lambda i: (0, 0, 0)),
        ),
        out_shape=(
            jax.ShapeDtypeStruct((channel_count, 2 * count * cols), jnp.float32),
            jax.ShapeDtypeStruct((kernel_side, kernel_side, channel_count), jnp.float32),
        ),
        compiler_params=pltpu.CompilerParams(vmem_limit_bytes=6 << 20),
        cost_estimate=pl.CostEstimate(flops=0, bytes_accessed=3 << 19, transcendentals=0),
        name="assemble_columns",
    )(side, mine, got)


block_cols = 256


def product(left, right, left_dim, right_dim):
    return lax.dot_general(
        left, right, (((left_dim,), (right_dim,)), ((), ())), preferred_element_type=jnp.float32
    )


def half_columns(ref, half):
    count = ref.shape[1] // 2
    return ref[:, pl.ds(pl.multiple_of(half * count, count), count)]


def forward_kernel(
    side_ref, normed_ref, student_ref, target_ref, w_in_ref, w_out_ref, params_ref,
    slope_ref, misfit_ref, out_grad_ref, sent_ref, kept_ref, hidden,
):
    cells, hidden_size = slope_ref.shape
    scale = params_ref[scale_row : scale_row + 1, :]
    rows = 16
    mlp_out = None
    for k in range(0, hidden_size, block_cols):
        cols = slice(k, k + block_cols)
        slope_ref[:, cols] = product(normed_ref[...], w_in_ref[:, cols], 1, 0)
        for r in range(0, cells, rows):
            at = slice(r, r + rows)
            values = slope_ref[at, cols]
            squares = values * values
            tangent = jnp.tanh(values * (slope_coef + slope_coef * cubic_coef * squares))
            gate = 0.5 + 0.5 * tangent
            bend = (0.5 - 0.5 * (tangent * tangent)) * (
                slope_coef + 3.0 * slope_coef * cubic_coef * squares
            )
            hidden[at, cols] = (values * gate).astype(jnp.bfloat16)
            slope_ref[at, cols] = gate + values * bend
        part = product(hidden[:, cols], w_out_ref[cols, :], 1, 0)
        mlp_out = part if mlp_out is None else mlp_out + part
    misfit = student_ref[...].astype(jnp.float32) + scale * mlp_out
    misfit = misfit - target_ref[...].astype(jnp.float32)
    misfit_ref[...] = misfit
    out_grad_ref[...] = (scale * misfit).astype(jnp.bfloat16)
    side = side_ref[0]
    sent_ref[...] = product(half_columns(hidden, 1 - side), out_grad_ref[...], 0, 0).astype(
        jnp.bfloat16
    )
    kept_ref[...] = product(half_columns(hidden, side), out_grad_ref[...], 0, 0)


def vmem_specs(count):
    return [pl.BlockSpec(memory_space=pltpu.VMEM)] * count


def forward(side, normed, student, target, w_in, w_out, params):
    cells, channel_count = normed.shape
    hidden_size = w_in.shape[1]
    shape = jax.ShapeDtypeStruct
    return pl.pallas_call(
        forward_kernel,
        in_specs=[pl.BlockSpec(memory_space=pltpu.SMEM)] + vmem_specs(6),
        out_specs=vmem_specs(5),
        out_shape=(
            shape((cells, hidden_size), jnp.float32),
            shape((cells, channel_count), jnp.float32),
            shape((cells, channel_count), jnp.bfloat16),
            shape((hidden_size // 2, channel_count), jnp.bfloat16),
            shape((hidden_size // 2, channel_count), jnp.float32),
        ),
        scratch_shapes=[pltpu.VMEM((cells, hidden_size), jnp.bfloat16)],
        compiler_params=pltpu.CompilerParams(vmem_limit_bytes=6 << 20),
        cost_estimate=pl.CostEstimate(
            flops=6 * cells * channel_count * hidden_size,
            bytes_accessed=4 << 20,
            transcendentals=cells * hidden_size,
        ),
        name="forward",
    )(side, normed, student, target, w_in, w_out, params)


def backward_kernel(
    side_ref, slope_ref, out_grad_ref, normed_ref, unit_ref, inv_ref, w_in_ref, w_out_ref, params_ref,
    conv_grad_ref, sent_ref, kept_ref, preact_grad,
):
    cells, hidden_size = slope_ref.shape
    normed_grad = None
    for k in range(0, hidden_size, block_cols):
        cols = slice(k, k + block_cols)
        hidden_grad = product(out_grad_ref[...], w_out_ref[cols, :], 1, 1)
        preact_grad[:, cols] = (hidden_grad * slope_ref[:, cols]).astype(jnp.bfloat16)
        part = product(preact_grad[:, cols], w_in_ref[:, cols], 1, 1)
        normed_grad = part if normed_grad is None else normed_grad + part
    unit_grad = normed_grad * params_ref[gain_row : gain_row + 1, :]
    unit = unit_ref[...]
    first_mean = jnp.mean(unit_grad, axis=-1, keepdims=True)
    second_mean = jnp.mean(unit_grad * unit, axis=-1, keepdims=True)
    conv_grad_ref[...] = (inv_ref[...] * (unit_grad - first_mean - unit * second_mean)).astype(
        jnp.bfloat16
    )
    side = side_ref[0]
    sent_ref[...] = product(half_columns(preact_grad, 1 - side), normed_ref[...], 0, 0).astype(
        jnp.bfloat16
    )
    kept_ref[...] = product(half_columns(preact_grad, side), normed_ref[...], 0, 0)


def backward(side, slope, out_grad, normed, unit_norm, inv_std, w_in, w_out, params):
    cells, channel_count = normed.shape
    hidden_size = w_in.shape[1]
    shape = jax.ShapeDtypeStruct
    return pl.pallas_call(
        backward_kernel,
        in_specs=[pl.BlockSpec(memory_space=pltpu.SMEM)] + vmem_specs(8),
        out_specs=vmem_specs(3),
        out_shape=(
            shape((cells, channel_count), jnp.bfloat16),
            shape((hidden_size // 2, channel_count), jnp.bfloat16),
            shape((hidden_size // 2, channel_count), jnp.float32),
        ),
        scratch_shapes=[pltpu.VMEM((cells, hidden_size), jnp.bfloat16)],
        compiler_params=pltpu.CompilerParams(vmem_limit_bytes=6 << 20),
        cost_estimate=pl.CostEstimate(
            flops=6 * cells * channel_count * hidden_size, bytes_accessed=4 << 20, transcendentals=0
        ),
        name="backward",
    )(side, slope, out_grad, normed, unit_norm, inv_std, w_in, w_out, params)


def local(student, teacher, dw_weight, norm_gain, w_in, w_out, layer_scale):
    batch_size, tile_rows, tile_cols, channel_count = student.shape
    half_kernel = kernel_side // 2
    cell_total = batch_size * tile_rows * lax.axis_size("lat") * tile_cols * lax.axis_size("lon")
    tap_count = kernel_side * kernel_side
    params = jnp.concatenate(
        [dw_weight.reshape(tap_count, channel_count), norm_gain[None], layer_scale[None]]
    )
    to_inner, to_outer = edges(student, "lon", 2, half_kernel)
    from_outer = swap_outer(to_outer, "lon", True)
    from_inner = swap(to_inner, "lon", 1)
    teacher, params = after((teacher, params), (to_inner, to_outer))
    lon_padded = with_edges(student, from_inner, from_outer, "lon", 2)
    lon_padded = after(lon_padded, params)
    padded_bf = with_halo(lon_padded, "lat", 1, half_kernel, False)
    normed, unit_norm, inv_std = conv_norm(padded_bf, params)
    target = to_bands(teacher, "lat")
    upper = lax.axis_index("lat") % 2
    side = upper.astype(jnp.int32).reshape(1)
    rows = lambda block: block.reshape(-1, channel_count)
    slope, misfit, out_grad, sent, kept_out = forward(
        side, normed, rows(student), rows(target), w_in, w_out, params
    )
    got_out = swap(sent, "lat", 1)
    conv_grad, sent, kept_in = backward(
        side, slope, out_grad, normed, unit_norm, inv_std, w_in, w_out, params
    )
    got_in = swap(sent, "lat", 1)
    conv_grid = conv_grad.reshape(student.shape)
    inner, outer = [swap(edge, "lat", 1) for edge in edges(conv_grid, "lat", 1, half_kernel)]
    part_dw = tap_sums(padded_bf, conv_grid, round_up(tap_count, 64))
    (out_chunk,), in_chunk, padded_grad = sum_over_mesh(
        [[kept_out, got_out]],
        [[kept_in, got_in], [part_dw]],
        cell_total,
        conv_grid,
        inner,
        outer,
        half_kernel,
    )
    out_chunks, in_chunks = out_chunk[None], in_chunk
    (_, out_halved), (_, in_halved) = sum_stages()
    for out_stage, in_stage in zip(out_halved[::-1], in_halved[::-1]):
        out_chunks = gather_halves(out_chunks, *out_stage)
        in_mine, in_got = in_chunks, swap(in_chunks, *in_stage)
        if in_stage != in_halved[0]:
            in_chunks = in_order(in_mine, in_got, *in_stage)
    grad_student, mark = conv_back(padded_grad, params, misfit.reshape(student.shape), out_chunks)
    sum_out, mark = assemble_rows(side, out_chunks, swap(out_chunks, "lat", 1), mark)
    axis, bit = in_halved[0]
    place = ((lax.axis_index(axis) // bit) % 2).astype(jnp.int32).reshape(1)
    in_chunks = join(place, in_mine, in_got, mark)
    sum_in, sum_dw = assemble_columns(side, in_chunks, swap(in_chunks, "lat", 1), channel_count)
    return (grad_student, sum_in, sum_out, sum_dw)


def solution(mesh):
    placed = (
        P(None, "lat", "lon", None),
        P(None, None, ("lon", "lat"), None),
        P(),
        P(),
        P(),
        P(),
        P(),
    )
    return jax.shard_map(
        local,
        mesh=mesh,
        in_specs=placed,
        out_specs=(P(None, "lat", "lon", None), P(), P(), P()),
        check_vma=False,
    )
```

```python
import functools

import jax
import jax.numpy as jnp
from jax import lax
from jax.experimental import pallas as pl
from jax.experimental.pallas import tpu as pltpu
from jax.sharding import PartitionSpec as P

slope_coef = 0.7978845608028654
cubic_coef = 0.044715
norm_eps = 1e-06


def bits_of(axis):
    return [1 << k for k in range((lax.axis_size(axis) - 1).bit_length())]


def swap(value, axis, bit):
    return lax.ppermute(value, axis, [(i, i ^ bit) for i in range(lax.axis_size(axis))])


def edges(block, axis, dim, width):
    low = lax.slice_in_dim(block, 0, width, axis=dim)
    high = lax.slice_in_dim(block, block.shape[dim] - width, None, axis=dim)
    odd = lax.axis_index(axis) % 2 == 1
    return jnp.where(odd, low, high), jnp.where(odd, high, low)


def swap_outer(edge, axis, periodic):
    count = lax.axis_size(axis)
    pairs = [(i, (i + 1) % count) for i in range(1, count, 2)]
    got = lax.ppermute(edge, axis, pairs + [(j, i) for i, j in pairs])
    return got if periodic else inside(got, axis)


def inside(edge, axis):
    index = lax.axis_index(axis)
    at_end = (index == 0) | (index == lax.axis_size(axis) - 1)
    return jnp.where(at_end, jnp.zeros_like(edge), edge)


def with_edges(block, from_inner, from_outer, axis, dim):
    odd = lax.axis_index(axis) % 2 == 1
    before = jnp.where(odd, from_inner, from_outer)
    after = jnp.where(odd, from_outer, from_inner)
    return jnp.concatenate([before, block, after], axis=dim)


def with_halo(block, axis, dim, width, periodic):
    to_inner, to_outer = edges(block, axis, dim, width)
    from_outer = swap_outer(to_outer, axis, periodic)
    from_inner = swap(to_inner, axis, 1)
    return with_edges(block, from_inner, from_outer, axis, dim)


def to_bands(teacher, axis):
    batch_size, rows, cols, channel_count = teacher.shape
    band = rows // lax.axis_size(axis)
    state = teacher.reshape(batch_size, -1, band, 1, cols, channel_count)
    for bit in bits_of(axis)[::-1]:
        upper = (lax.axis_index(axis) // bit) % 2
        state = state.reshape(batch_size, 2, -1, *state.shape[2:])
        mine = lax.dynamic_index_in_dim(state, upper, axis=1, keepdims=False)
        got = swap(lax.dynamic_index_in_dim(state, 1 - upper, axis=1, keepdims=False), axis, bit)
        state = jnp.where(
            upper == 1, jnp.stack([got, mine], axis=4), jnp.stack([mine, got], axis=4)
        )
        state = state.reshape(batch_size, -1, band, 2 * state.shape[3], cols, channel_count)
    return state.reshape(batch_size, band, -1, channel_count)


def half_of(value, upper):
    count = value.shape[0] // 2
    return lax.dynamic_slice_in_dim(value, upper * count, count, axis=0)


def total_of(terms):
    total = terms[0].astype(jnp.float32)
    for term in terms[1:]:
        total = total + term.astype(jnp.float32)
    return total


def flat_rows(block):
    return block.reshape(-1, block.shape[-1])


def after(value, other):
    return lax.optimization_barrier((value, other))[0]


def exchange(parts, axis, bit, halved, sent_as, rider=None):
    upper = (lax.axis_index(axis) // bit) % 2
    if halved:
        give = [total_of([half_of(t, 1 - upper) for t in terms]) for terms in parts]
        keep = [total_of([half_of(t, upper) for t in terms]) for terms in parts]
    else:
        give = keep = [total_of(terms) for terms in parts]
    give = [value.astype(sent_as) for value in give]
    if not halved:
        keep = [value.astype(jnp.float32) for value in give]
    counts = [value.shape[0] for value in give]
    if rider is not None:
        give = give + [flat_rows(rider).astype(sent_as)]
        counts = counts + [give[-1].shape[0]]
    sent = jnp.concatenate(give, axis=0) if len(give) > 1 else give[0]
    raw = swap(sent, axis, bit)
    got = split_rows(raw, counts) if len(give) > 1 else [raw]
    parts = [[k, g] for k, g in zip(keep, got)]
    ridden = None if rider is None else got[-1].astype(rider.dtype).reshape(rider.shape)
    return parts, ridden, sent, raw


def split_rows(value, counts):
    pieces, start = [], 0
    for count in counts:
        pieces.append(lax.slice_in_dim(value, start, start + count, axis=0))
        start += count
    return pieces


def in_order(chunks, got, axis, bit):
    upper = (lax.axis_index(axis) // bit) % 2
    return jnp.where(
        upper == 1, jnp.concatenate([got, chunks]), jnp.concatenate([chunks, got])
    )


def gather_halves(chunks, axis, bit):
    return in_order(chunks, swap(chunks, axis, bit), axis, bit)


def join_kernel(place_ref, mine, got, _, out_ref):
    count = mine.shape[0]
    place = place_ref[0]
    out_ref[pl.ds(place * count, count)] = mine[...]
    out_ref[pl.ds((1 - place) * count, count)] = got[...]


def join(place, mine, got, earlier):
    shape = (2 * mine.shape[0],) + mine.shape[1:]
    return pl.pallas_call(
        join_kernel,
        in_specs=[pl.BlockSpec(memory_space=pltpu.SMEM)]
        + vmem_specs(2)
        + [pl.BlockSpec(memory_space=pl.ANY)],
        out_specs=pl.BlockSpec(memory_space=pltpu.VMEM),
        out_shape=jax.ShapeDtypeStruct(shape, mine.dtype),
        compiler_params=pltpu.CompilerParams(vmem_limit_bytes=4 << 20),
        cost_estimate=pl.CostEstimate(flops=0, bytes_accessed=1 << 18, transcendentals=0),
        name="join",
    )(place, mine, got, earlier)


def carried(axis, bit):
    index = lax.axis_index(axis)
    lower = index % bit // 2
    return lower == jnp.where(index % 2 == 0, 0, bit // 2 - 1)


def sum_stages():
    lat_stages = [("lat", bit) for bit in bits_of("lat")[1:]]
    lon_stages = [("lon", bit) for bit in bits_of("lon")]
    trail = lat_stages + lon_stages
    lead = lon_stages[1:3] + lat_stages + lon_stages[:1] + lon_stages[3:]
    return (lead, lead[:2]), (trail, [lat_stages[0], lon_stages[0]])


def sent_type(stage, stages, halved):
    return jnp.bfloat16 if stage in halved or stage == stages[-1] else jnp.float32


def finish_columns_kernel(divisor, main_ref, taps_ref, got_ref, out_ref):
    rows, channel_count = main_ref.shape
    tap_rows = taps_ref.shape[0]
    main = main_ref[...] + got_ref[:rows].astype(jnp.float32)
    out_ref[0, :channel_count] = (main / divisor).T.astype(jnp.bfloat16)
    taps = taps_ref[...] + got_ref[rows : rows + tap_rows].astype(jnp.float32)
    taps = (taps / divisor).astype(jnp.bfloat16)
    for k in range(channel_count // rows):
        at = channel_count + k * tap_rows
        out_ref[0, at : at + tap_rows] = taps[:, k * rows : (k + 1) * rows]


def finish_columns(main, taps, got, divisor):
    rows, channel_count = main.shape
    height = channel_count + channel_count // rows * taps.shape[0]
    return pl.pallas_call(
        functools.partial(finish_columns_kernel, float(divisor)),
        out_shape=jax.ShapeDtypeStruct((1, height, rows), jnp.bfloat16),
        in_specs=vmem_specs(3),
        out_specs=pl.BlockSpec(memory_space=pltpu.VMEM),
        compiler_params=pltpu.CompilerParams(vmem_limit_bytes=4 << 20),
        cost_estimate=pl.CostEstimate(flops=main.size, bytes_accessed=1 << 18, transcendentals=0),
        name="finish_columns",
    )(main, taps, got)


def sum_over_mesh(lead, trail, divisor, block, inner, outer, width):
    (lead_stages, lead_halved), (stages, halved) = sum_stages()
    dim_of = {"lat": 1, "lon": 2}
    for k, (axis, bit) in enumerate(stages):
        dim = dim_of[axis]
        stage = lead_stages[k]
        lead, _, _, _ = exchange(
            lead, *stage, stage in lead_halved, sent_type(stage, lead_stages, lead_halved)
        )
        rider = jnp.stack(edges(block, axis, dim, width)) if bit == 1 else outer
        trail, got, sent, raw = exchange(
            trail, axis, bit, (axis, bit) in halved, sent_type((axis, bit), stages, halved), rider
        )
        lead = after(lead, sent)
        if bit == 1:
            inner, outer = got[0], got[1]
        else:
            outer = jnp.where(carried(axis, bit), got, outer)
        if k + 1 == len(stages) or stages[k + 1][0] != axis:
            if axis == "lat":
                outer = inside(outer, axis)
            block = with_edges(block, inner, outer, axis, dim)
    lead = [(total_of(terms) / divisor).astype(jnp.bfloat16) for terms in lead]
    return lead, finish_columns(trail[0][0], trail[1][0], raw, divisor), block


lane_count = 128
kernel_side = 7
gain_row = kernel_side * kernel_side
scale_row = gain_row + 1


def spread(padded_ref, wide):
    batch_size, rows, cols, channel_count = padded_ref.shape
    for group in range(channel_count // lane_count):
        lanes = slice(group * lane_count, (group + 1) * lane_count)
        for b in range(batch_size):
            wide[group, b, :, :cols, :] = padded_ref[b, :, :, lanes].astype(jnp.float32)


def stencil(wide, params, group, b, rows, tile_cols, used, first, flipped):
    lanes = slice(group * lane_count, (group + 1) * lane_count)
    rows = list(rows)
    for q in range(kernel_side):
        for r in used:
            shifted = wide[group, b, r - first, q : q + tile_cols, :]
            for i in range(max(0, r - kernel_side + 1), min(len(rows), r + 1)):
                p = r - i
                tap = (kernel_side - 1 - p, kernel_side - 1 - q) if flipped else (p, q)
                term = params[pl.ds(tap[0] * kernel_side + tap[1], 1), lanes] * shifted
                rows[i] = term if rows[i] is None else rows[i] + term
    return rows


def conv_own_kernel(block_ref, params_ref, _w_in_ref, _w_out_ref, out_ref, wide):
    batch_size, tile_rows, pad_cols, _ = block_ref.shape
    tile_cols = pad_cols - kernel_side + 1
    first = kernel_side // 2
    spread(block_ref, wide)
    for group in range(wide.shape[0]):
        for b in range(batch_size):
            rows = stencil(
                wide, params_ref, group, b, [None] * tile_rows, tile_cols,
                range(first, first + tile_rows), first, False,
            )
            for i, row in enumerate(rows):
                at = (b * tile_rows + i) * tile_cols
                out_ref[group, at : at + tile_cols, :] = row


def conv_own(block, params, w_in, w_out):
    batch_size, tile_rows, pad_cols, channel_count = block.shape
    cells = batch_size * tile_rows * (pad_cols - kernel_side + 1)
    groups = channel_count // lane_count
    return pl.pallas_call(
        conv_own_kernel,
        out_shape=jax.ShapeDtypeStruct((groups, cells, lane_count), jnp.float32),
        in_specs=vmem_specs(4),
        out_specs=pl.BlockSpec(memory_space=pltpu.VMEM),
        scratch_shapes=[
            pltpu.VMEM((groups, batch_size, tile_rows, round_up(pad_cols, 8), lane_count), jnp.float32)
        ],
        compiler_params=pltpu.CompilerParams(vmem_limit_bytes=6 << 20),
        cost_estimate=pl.CostEstimate(flops=64 * cells * channel_count, bytes_accessed=1 << 20, transcendentals=0),
        name="conv_own",
    )(block, params, w_in, w_out)


def conv_norm_kernel(own_ref, padded_ref, params_ref, normed_ref, unit_ref, inv_ref, wide, smooth):
    batch_size, pad_rows, pad_cols, channel_count = padded_ref.shape
    cells = smooth.shape[1]
    tile_rows = pad_rows - kernel_side + 1
    tile_cols = pad_cols - kernel_side + 1
    spread(padded_ref, wide)
    first = kernel_side // 2
    used = [r for r in range(pad_rows) if r < first or r >= first + tile_rows]
    for group in range(wide.shape[0]):
        for b in range(batch_size):
            places = [
                slice(at, at + tile_cols)
                for at in range(b * tile_rows * tile_cols, (b + 1) * tile_rows * tile_cols, tile_cols)
            ]
            rows = [own_ref[group, at, :] for at in places]
            rows = stencil(wide, params_ref, group, b, rows, tile_cols, used, 0, False)
            for at, row in zip(places, rows):
                smooth[group, at, :] = row
    gain = params_ref[gain_row : gain_row + 1, :]
    block = 32

    def norm(step, _):
        at = pl.ds(pl.multiple_of(step * block, block), block)
        values = jnp.concatenate([smooth[g, at, :] for g in range(wide.shape[0])], axis=1)
        average = jnp.mean(values, axis=-1, keepdims=True)
        centred = values - average
        variance = jnp.mean(centred * centred, axis=-1, keepdims=True)
        inv_std = lax.rsqrt(variance + norm_eps)
        unit = centred * inv_std
        unit_ref[at, :] = unit
        inv_ref[at, :] = inv_std
        normed_ref[at, :] = (unit * gain).astype(jnp.bfloat16)
        return 0

    lax.fori_loop(0, cells // block, norm, 0, unroll=True)


def round_up(value, unit):
    return -(-value // unit) * unit


def conv_norm(own, padded, params):
    batch_size, pad_rows, pad_cols, channel_count = padded.shape
    cells = batch_size * (pad_rows - kernel_side + 1) * (pad_cols - kernel_side + 1)
    groups = channel_count // lane_count
    return pl.pallas_call(
        conv_norm_kernel,
        out_shape=(
            jax.ShapeDtypeStruct((cells, channel_count), jnp.bfloat16),
            jax.ShapeDtypeStruct((cells, channel_count), jnp.float32),
            jax.ShapeDtypeStruct((cells, 1), jnp.float32),
        ),
        scratch_shapes=[
            pltpu.VMEM((groups, batch_size, pad_rows, round_up(pad_cols, 8), lane_count), jnp.float32),
            pltpu.VMEM((groups, cells, lane_count), jnp.float32),
        ],
        compiler_params=pltpu.CompilerParams(vmem_limit_bytes=6 << 20),
        cost_estimate=pl.CostEstimate(flops=2 * 49 * cells * channel_count, bytes_accessed=1 << 20, transcendentals=0),
        name="conv_norm",
    )(own, padded, params)


def conv_back_kernel(padded_ref, params_ref, misfit_ref, _, out_ref, mark_ref, wide):
    mark_ref[...] = jnp.zeros_like(mark_ref)
    batch_size, tile_rows, tile_cols, channel_count = out_ref.shape
    spread(padded_ref, wide)
    for group in range(wide.shape[0]):
        lanes = slice(group * lane_count, (group + 1) * lane_count)

        def one(b, _):
            rows = stencil(
                wide, params_ref, group, b, [None] * tile_rows, tile_cols,
                range(wide.shape[2]), 0, True,
            )
            for i, row in enumerate(rows):
                out_ref[b, i, :, lanes] = (misfit_ref[b, i, :, lanes] + row).astype(out_ref.dtype)
            return 0

        for b in range(batch_size):
            one(b, 0)


def conv_back(padded, params, misfit, earlier):
    batch_size, pad_rows, pad_cols, channel_count = padded.shape
    groups = channel_count // lane_count
    return pl.pallas_call(
        conv_back_kernel,
        out_shape=(jax.ShapeDtypeStruct(misfit.shape, jnp.bfloat16), mark_shape),
        in_specs=vmem_specs(3) + [pl.BlockSpec(memory_space=pl.ANY)],
        out_specs=vmem_specs(2),
        scratch_shapes=[
            pltpu.VMEM((groups, batch_size, pad_rows, round_up(pad_cols, 8), lane_count), jnp.float32),
        ],
        compiler_params=pltpu.CompilerParams(vmem_limit_bytes=6 << 20),
        cost_estimate=pl.CostEstimate(flops=2 * 49 * misfit.size, bytes_accessed=1 << 20, transcendentals=0),
        name="conv_back",
    )(padded, params, misfit, earlier)


def tap_sums_kernel(padded_ref, grad_ref, out_ref, wide, partial):
    batch_size, tile_rows, tile_cols, channel_count = grad_ref.shape
    kernel_size = padded_ref.shape[1] - tile_rows + 1
    spread(padded_ref, wide)
    out_ref[...] = jnp.zeros_like(out_ref)
    for group in range(wide.shape[0]):
        lanes = slice(group * lane_count, (group + 1) * lane_count)

        def one(b, _):
            grads = [grad_ref[b, i, :, lanes].astype(jnp.float32) for i in range(tile_rows)]
            for q in range(kernel_size):
                sums = [None] * kernel_size
                for r in range(tile_rows + kernel_size - 1):
                    shifted = wide[group, b, r, q : q + tile_cols, :]
                    for i in range(max(0, r - kernel_size + 1), min(tile_rows, r + 1)):
                        product = shifted * grads[i]
                        term = product.reshape(tile_cols // 8, 8, lane_count).sum(axis=0)
                        p = r - i
                        sums[p] = term if sums[p] is None else sums[p] + term
                for p in range(kernel_size):
                    at = pl.ds((p * kernel_size + q) * 8, 8)
                    partial[group, b, at, :] = sums[p]
            return 0

        for b in range(batch_size):
            one(b, 0)
        taps = kernel_size * kernel_size
        total = partial[group, 0]
        for b in range(1, batch_size):
            total = total + partial[group, b]
        out_ref[:taps, lanes] = total.reshape(taps, 8, lane_count).sum(axis=1)


def tap_sums(padded, grads, row_count):
    batch_size, pad_rows, pad_cols, channel_count = padded.shape
    kernel_size = pad_rows - grads.shape[1] + 1
    groups = channel_count // lane_count
    return pl.pallas_call(
        tap_sums_kernel,
        out_shape=jax.ShapeDtypeStruct((row_count, channel_count), jnp.float32),
        scratch_shapes=[
            pltpu.VMEM((groups, batch_size, pad_rows, round_up(pad_cols, 8), lane_count), jnp.float32),
            pltpu.VMEM((groups, batch_size, kernel_size * kernel_size * 8, lane_count), jnp.float32),
        ],
        compiler_params=pltpu.CompilerParams(vmem_limit_bytes=6 << 20),
        cost_estimate=pl.CostEstimate(flops=2 * 49 * grads.size, bytes_accessed=1 << 20, transcendentals=0),
        name="tap_sums",
    )(padded, grads)


def assemble_rows_kernel(side_ref, mine, got, _, out_ref, mark_ref):
    mark_ref[...] = jnp.zeros_like(mark_ref)
    own = pl.program_id(0) == side_ref[0]
    count, rows, _ = mine.shape
    for k in range(count):
        chunk = jnp.where(own, mine[k].astype(jnp.float32), got[k].astype(jnp.float32))
        out_ref[k * rows : (k + 1) * rows, :] = chunk


def assemble_columns_kernel(side_ref, mine, got, out_ref, taps_ref):
    half = pl.program_id(0)
    own = half == side_ref[0]
    count, _, cols = mine.shape
    channel_count = out_ref.shape[0]
    for k in range(count):
        chunk = jnp.where(
            own,
            mine[k, :channel_count].astype(jnp.float32),
            got[k, :channel_count].astype(jnp.float32),
        )
        out_ref[:, k * cols : (k + 1) * cols] = chunk

    @pl.when(half == 0)
    def _():
        tail = slice(channel_count, mine.shape[1])
        chunks = mine[:, tail].astype(jnp.float32) + got[:, tail].astype(jnp.float32)
        groups = channel_count // cols
        step = chunks.shape[1] // groups
        pieces = [
            jnp.concatenate([chunks[k, n * step : (n + 1) * step] for n in range(groups)], axis=1)
            for k in range(count)
        ]
        taps = jnp.concatenate(pieces, axis=0)
        width = taps_ref.shape[1]
        for p in range(taps_ref.shape[0]):
            taps_ref[p] = taps[p * width : (p + 1) * width]


mark_shape = jax.ShapeDtypeStruct((8, 128), jnp.float32)


def whole_block(value):
    return pl.BlockSpec(value.shape, lambda i: (0,) * len(value.shape))


def assemble_rows(side, mine, got, earlier):
    count, rows, cols = mine.shape
    return pl.pallas_call(
        assemble_rows_kernel,
        grid=(2,),
        in_specs=[pl.BlockSpec(memory_space=pltpu.SMEM), whole_block(mine), whole_block(got)]
        + [pl.BlockSpec(memory_space=pl.ANY)],
        out_specs=(pl.BlockSpec((count * rows, cols), lambda i: (i, 0)), whole_block(mark_shape)),
        out_shape=(jax.ShapeDtypeStruct((2 * count * rows, cols), jnp.float32), mark_shape),
        compiler_params=pltpu.CompilerParams(vmem_limit_bytes=6 << 20),
        cost_estimate=pl.CostEstimate(flops=0, bytes_accessed=3 << 19, transcendentals=0),
        name="assemble_rows",
    )(side, mine, got, earlier)


def assemble_columns(side, mine, got, channel_count):
    count, _, cols = mine.shape
    return pl.pallas_call(
        assemble_columns_kernel,
        grid=(2,),
        in_specs=[pl.BlockSpec(memory_space=pltpu.SMEM), whole_block(mine), whole_block(got)],
        out_specs=(
            pl.BlockSpec((channel_count, count * cols), lambda i: (0, i)),
            pl.BlockSpec((kernel_side, kernel_side, channel_count), lambda i: (0, 0, 0)),
        ),
        out_shape=(
            jax.ShapeDtypeStruct((channel_count, 2 * count * cols), jnp.float32),
            jax.ShapeDtypeStruct((kernel_side, kernel_side, channel_count), jnp.float32),
        ),
        compiler_params=pltpu.CompilerParams(vmem_limit_bytes=6 << 20),
        cost_estimate=pl.CostEstimate(flops=0, bytes_accessed=3 << 19, transcendentals=0),
        name="assemble_columns",
    )(side, mine, got)


block_cols = 256


def product(left, right, left_dim, right_dim):
    return lax.dot_general(
        left, right, (((left_dim,), (right_dim,)), ((), ())), preferred_element_type=jnp.float32
    )


def half_columns(ref, half):
    count = ref.shape[1] // 2
    return ref[:, pl.ds(pl.multiple_of(half * count, count), count)]


def forward_kernel(
    side_ref, normed_ref, student_ref, target_ref, w_in_ref, w_out_ref, params_ref,
    slope_ref, misfit_ref, out_grad_ref, sent_ref, kept_ref, hidden,
):
    cells, hidden_size = slope_ref.shape
    scale = params_ref[scale_row : scale_row + 1, :]
    rows = 16
    mlp_out = None
    for k in range(0, hidden_size, block_cols):
        cols = slice(k, k + block_cols)
        slope_ref[:, cols] = product(normed_ref[...], w_in_ref[:, cols], 1, 0)
        for r in range(0, cells, rows):
            at = slice(r, r + rows)
            values = slope_ref[at, cols]
            squares = values * values
            tangent = jnp.tanh(values * (slope_coef + slope_coef * cubic_coef * squares))
            gate = 0.5 + 0.5 * tangent
            bend = (0.5 - 0.5 * (tangent * tangent)) * (
                slope_coef + 3.0 * slope_coef * cubic_coef * squares
            )
            hidden[at, cols] = (values * gate).astype(jnp.bfloat16)
            slope_ref[at, cols] = gate + values * bend
        part = product(hidden[:, cols], w_out_ref[cols, :], 1, 0)
        mlp_out = part if mlp_out is None else mlp_out + part
    misfit = student_ref[...].astype(jnp.float32) + scale * mlp_out
    misfit = misfit - target_ref[...].astype(jnp.float32)
    misfit_ref[...] = misfit
    out_grad_ref[...] = (scale * misfit).astype(jnp.bfloat16)
    side = side_ref[0]
    sent_ref[...] = product(half_columns(hidden, 1 - side), out_grad_ref[...], 0, 0).astype(
        jnp.bfloat16
    )
    kept_ref[...] = product(half_columns(hidden, side), out_grad_ref[...], 0, 0)


def vmem_specs(count):
    return [pl.BlockSpec(memory_space=pltpu.VMEM)] * count


def forward(side, normed, student, target, w_in, w_out, params):
    cells, channel_count = normed.shape
    hidden_size = w_in.shape[1]
    shape = jax.ShapeDtypeStruct
    return pl.pallas_call(
        forward_kernel,
        in_specs=[pl.BlockSpec(memory_space=pltpu.SMEM)] + vmem_specs(6),
        out_specs=vmem_specs(5),
        out_shape=(
            shape((cells, hidden_size), jnp.float32),
            shape((cells, channel_count), jnp.float32),
            shape((cells, channel_count), jnp.bfloat16),
            shape((hidden_size // 2, channel_count), jnp.bfloat16),
            shape((hidden_size // 2, channel_count), jnp.float32),
        ),
        scratch_shapes=[pltpu.VMEM((cells, hidden_size), jnp.bfloat16)],
        compiler_params=pltpu.CompilerParams(vmem_limit_bytes=6 << 20),
        cost_estimate=pl.CostEstimate(
            flops=6 * cells * channel_count * hidden_size,
            bytes_accessed=4 << 20,
            transcendentals=cells * hidden_size,
        ),
        name="forward",
    )(side, normed, student, target, w_in, w_out, params)


def backward_kernel(
    side_ref, slope_ref, out_grad_ref, normed_ref, unit_ref, inv_ref, w_in_ref, w_out_ref, params_ref,
    conv_grad_ref, sent_ref, kept_ref, preact_grad,
):
    cells, hidden_size = slope_ref.shape
    normed_grad = None
    for k in range(0, hidden_size, block_cols):
        cols = slice(k, k + block_cols)
        hidden_grad = product(out_grad_ref[...], w_out_ref[cols, :], 1, 1)
        preact_grad[:, cols] = (hidden_grad * slope_ref[:, cols]).astype(jnp.bfloat16)
        part = product(preact_grad[:, cols], w_in_ref[:, cols], 1, 1)
        normed_grad = part if normed_grad is None else normed_grad + part
    unit_grad = normed_grad * params_ref[gain_row : gain_row + 1, :]
    unit = unit_ref[...]
    first_mean = jnp.mean(unit_grad, axis=-1, keepdims=True)
    second_mean = jnp.mean(unit_grad * unit, axis=-1, keepdims=True)
    conv_grad_ref[...] = (inv_ref[...] * (unit_grad - first_mean - unit * second_mean)).astype(
        jnp.bfloat16
    )
    side = side_ref[0]
    sent_ref[...] = product(half_columns(preact_grad, 1 - side), normed_ref[...], 0, 0).astype(
        jnp.bfloat16
    )
    kept_ref[...] = product(half_columns(preact_grad, side), normed_ref[...], 0, 0)


def backward(side, slope, out_grad, normed, unit_norm, inv_std, w_in, w_out, params):
    cells, channel_count = normed.shape
    hidden_size = w_in.shape[1]
    shape = jax.ShapeDtypeStruct
    return pl.pallas_call(
        backward_kernel,
        in_specs=[pl.BlockSpec(memory_space=pltpu.SMEM)] + vmem_specs(8),
        out_specs=vmem_specs(3),
        out_shape=(
            shape((cells, channel_count), jnp.bfloat16),
            shape((hidden_size // 2, channel_count), jnp.bfloat16),
            shape((hidden_size // 2, channel_count), jnp.float32),
        ),
        scratch_shapes=[pltpu.VMEM((cells, hidden_size), jnp.bfloat16)],
        compiler_params=pltpu.CompilerParams(vmem_limit_bytes=6 << 20),
        cost_estimate=pl.CostEstimate(
            flops=6 * cells * channel_count * hidden_size, bytes_accessed=4 << 20, transcendentals=0
        ),
        name="backward",
    )(side, slope, out_grad, normed, unit_norm, inv_std, w_in, w_out, params)


def local(student, teacher, dw_weight, norm_gain, w_in, w_out, layer_scale):
    batch_size, tile_rows, tile_cols, channel_count = student.shape
    half_kernel = kernel_side // 2
    cell_total = batch_size * tile_rows * lax.axis_size("lat") * tile_cols * lax.axis_size("lon")
    tap_count = kernel_side * kernel_side
    params = jnp.concatenate(
        [dw_weight.reshape(tap_count, channel_count), norm_gain[None], layer_scale[None]]
    )
    to_inner, to_outer = edges(student, "lon", 2, half_kernel)
    from_outer = swap_outer(to_outer, "lon", True)
    from_inner = swap(to_inner, "lon", 1)
    teacher, params = after((teacher, params), (to_inner, to_outer))
    lon_padded = with_edges(student, from_inner, from_outer, "lon", 2)
    lon_padded = after(lon_padded, params)
    padded_bf = with_halo(lon_padded, "lat", 1, half_kernel, False)
    normed, unit_norm, inv_std = conv_norm(conv_own(lon_padded, params, w_in, w_out), padded_bf, params)
    target = to_bands(teacher, "lat")
    upper = lax.axis_index("lat") % 2
    side = upper.astype(jnp.int32).reshape(1)
    rows = lambda block: block.reshape(-1, channel_count)
    slope, misfit, out_grad, sent, kept_out = forward(
        side, normed, rows(student), rows(target), w_in, w_out, params
    )
    got_out = swap(sent, "lat", 1)
    conv_grad, sent, kept_in = backward(
        side, slope, out_grad, normed, unit_norm, inv_std, w_in, w_out, params
    )
    got_in = swap(sent, "lat", 1)
    conv_grid = conv_grad.reshape(student.shape)
    inner, outer = [swap(edge, "lat", 1) for edge in edges(conv_grid, "lat", 1, half_kernel)]
    part_dw = tap_sums(padded_bf, conv_grid, round_up(tap_count, 64))
    (out_chunk,), in_chunk, padded_grad = sum_over_mesh(
        [[kept_out, got_out]],
        [[kept_in, got_in], [part_dw]],
        cell_total,
        conv_grid,
        inner,
        outer,
        half_kernel,
    )
    out_chunks, in_chunks = out_chunk[None], in_chunk
    (_, out_halved), (_, in_halved) = sum_stages()
    for out_stage, in_stage in zip(out_halved[::-1], in_halved[::-1]):
        out_chunks = gather_halves(out_chunks, *out_stage)
        in_mine, in_got = in_chunks, swap(in_chunks, *in_stage)
        if in_stage != in_halved[0]:
            in_chunks = in_order(in_mine, in_got, *in_stage)
    grad_student, mark = conv_back(padded_grad, params, misfit.reshape(student.shape), in_chunk)
    sum_out, mark = assemble_rows(side, out_chunks, swap(out_chunks, "lat", 1), mark)
    axis, bit = in_halved[0]
    place = ((lax.axis_index(axis) // bit) % 2).astype(jnp.int32).reshape(1)
    in_chunks = join(place, in_mine, in_got, mark)
    sum_in, sum_dw = assemble_columns(side, in_chunks, swap(in_chunks, "lat", 1), channel_count)
    return (grad_student, sum_in, sum_out, sum_dw)


def solution(mesh):
    placed = (
        P(None, "lat", "lon", None),
        P(None, None, ("lon", "lat"), None),
        P(),
        P(),
        P(),
        P(),
        P(),
    )
    return jax.shard_map(
        local,
        mesh=mesh,
        in_specs=placed,
        out_specs=(P(None, "lat", "lon", None), P(), P(), P()),
        check_vma=False,
    )
```

```python
import functools

import jax
import jax.numpy as jnp
from jax import lax
from jax.experimental import pallas as pl
from jax.experimental.pallas import tpu as pltpu
from jax.sharding import PartitionSpec as P

slope_coef = 0.7978845608028654
cubic_coef = 0.044715
norm_eps = 1e-06


def bits_of(axis):
    return [1 << k for k in range((lax.axis_size(axis) - 1).bit_length())]


def swap(value, axis, bit):
    return lax.ppermute(value, axis, [(i, i ^ bit) for i in range(lax.axis_size(axis))])


def edges(block, axis, dim, width):
    low = lax.slice_in_dim(block, 0, width, axis=dim)
    high = lax.slice_in_dim(block, block.shape[dim] - width, None, axis=dim)
    odd = lax.axis_index(axis) % 2 == 1
    return jnp.where(odd, low, high), jnp.where(odd, high, low)


def swap_outer(edge, axis, periodic):
    count = lax.axis_size(axis)
    pairs = [(i, (i + 1) % count) for i in range(1, count, 2)]
    got = lax.ppermute(edge, axis, pairs + [(j, i) for i, j in pairs])
    return got if periodic else inside(got, axis)


def inside(edge, axis):
    index = lax.axis_index(axis)
    at_end = (index == 0) | (index == lax.axis_size(axis) - 1)
    return jnp.where(at_end, jnp.zeros_like(edge), edge)


def with_edges(block, from_inner, from_outer, axis, dim):
    odd = lax.axis_index(axis) % 2 == 1
    before = jnp.where(odd, from_inner, from_outer)
    after = jnp.where(odd, from_outer, from_inner)
    return jnp.concatenate([before, block, after], axis=dim)


def with_halo(block, axis, dim, width, periodic):
    to_inner, to_outer = edges(block, axis, dim, width)
    from_outer = swap_outer(to_outer, axis, periodic)
    from_inner = swap(to_inner, axis, 1)
    return with_edges(block, from_inner, from_outer, axis, dim)


def to_bands(teacher, axis):
    batch_size, rows, cols, channel_count = teacher.shape
    band = rows // lax.axis_size(axis)
    state = teacher.reshape(batch_size, -1, band, 1, cols, channel_count)
    for bit in bits_of(axis)[::-1]:
        upper = (lax.axis_index(axis) // bit) % 2
        state = state.reshape(batch_size, 2, -1, *state.shape[2:])
        mine = lax.dynamic_index_in_dim(state, upper, axis=1, keepdims=False)
        got = swap(lax.dynamic_index_in_dim(state, 1 - upper, axis=1, keepdims=False), axis, bit)
        state = jnp.where(
            upper == 1, jnp.stack([got, mine], axis=4), jnp.stack([mine, got], axis=4)
        )
        state = state.reshape(batch_size, -1, band, 2 * state.shape[3], cols, channel_count)
    return state.reshape(batch_size, band, -1, channel_count)


def half_of(value, upper):
    count = value.shape[0] // 2
    return lax.dynamic_slice_in_dim(value, upper * count, count, axis=0)


def total_of(terms):
    total = terms[0].astype(jnp.float32)
    for term in terms[1:]:
        total = total + term.astype(jnp.float32)
    return total


def flat_rows(block):
    return block.reshape(-1, block.shape[-1])


def after(value, other):
    return lax.optimization_barrier((value, other))[0]


def exchange(parts, axis, bit, halved, sent_as, rider=None):
    upper = (lax.axis_index(axis) // bit) % 2
    if halved:
        give = [total_of([half_of(t, 1 - upper) for t in terms]) for terms in parts]
        keep = [total_of([half_of(t, upper) for t in terms]) for terms in parts]
    else:
        give = keep = [total_of(terms) for terms in parts]
    give = [value.astype(sent_as) for value in give]
    if not halved:
        keep = [value.astype(jnp.float32) for value in give]
    counts = [value.shape[0] for value in give]
    if rider is not None:
        give = give + [flat_rows(rider).astype(sent_as)]
        counts = counts + [give[-1].shape[0]]
    sent = jnp.concatenate(give, axis=0) if len(give) > 1 else give[0]
    raw = swap(sent, axis, bit)
    got = split_rows(raw, counts) if len(give) > 1 else [raw]
    parts = [[k, g] for k, g in zip(keep, got)]
    ridden = None if rider is None else got[-1].astype(rider.dtype).reshape(rider.shape)
    return parts, ridden, sent, raw


def split_rows(value, counts):
    pieces, start = [], 0
    for count in counts:
        pieces.append(lax.slice_in_dim(value, start, start + count, axis=0))
        start += count
    return pieces


def in_order(chunks, got, axis, bit):
    upper = (lax.axis_index(axis) // bit) % 2
    return jnp.where(
        upper == 1, jnp.concatenate([got, chunks]), jnp.concatenate([chunks, got])
    )


def gather_halves(chunks, axis, bit):
    return in_order(chunks, swap(chunks, axis, bit), axis, bit)


def join_kernel(place_ref, mine, got, _, out_ref):
    count = mine.shape[0]
    place = place_ref[0]
    out_ref[pl.ds(place * count, count)] = mine[...]
    out_ref[pl.ds((1 - place) * count, count)] = got[...]


def join(place, mine, got, earlier):
    shape = (2 * mine.shape[0],) + mine.shape[1:]
    return pl.pallas_call(
        join_kernel,
        in_specs=[pl.BlockSpec(memory_space=pltpu.SMEM)]
        + vmem_specs(2)
        + [pl.BlockSpec(memory_space=pl.ANY)],
        out_specs=pl.BlockSpec(memory_space=pltpu.VMEM),
        out_shape=jax.ShapeDtypeStruct(shape, mine.dtype),
        compiler_params=pltpu.CompilerParams(vmem_limit_bytes=4 << 20),
        cost_estimate=pl.CostEstimate(flops=0, bytes_accessed=1 << 18, transcendentals=0),
        name="join",
    )(place, mine, got, earlier)


def carried(axis, bit):
    index = lax.axis_index(axis)
    lower = index % bit // 2
    return lower == jnp.where(index % 2 == 0, 0, bit // 2 - 1)


def sum_stages():
    lat_stages = [("lat", bit) for bit in bits_of("lat")[1:]]
    lon_stages = [("lon", bit) for bit in bits_of("lon")]
    trail = lat_stages + lon_stages
    lead = lon_stages[1:3] + lat_stages + lon_stages[:1] + lon_stages[3:]
    return (lead, lead[:2]), (trail, [lat_stages[0], lon_stages[0]])


def sent_type(stage, stages, halved):
    return jnp.bfloat16 if stage in halved or stage == stages[-1] else jnp.float32


def finish_columns_kernel(divisor, main_ref, taps_ref, got_ref, out_ref):
    rows, channel_count = main_ref.shape
    tap_rows = taps_ref.shape[0]
    main = main_ref[...] + got_ref[:rows].astype(jnp.float32)
    out_ref[0, :channel_count] = (main / divisor).T.astype(jnp.bfloat16)
    taps = taps_ref[...] + got_ref[rows : rows + tap_rows].astype(jnp.float32)
    taps = (taps / divisor).astype(jnp.bfloat16)
    for k in range(channel_count // rows):
        at = channel_count + k * tap_rows
        out_ref[0, at : at + tap_rows] = taps[:, k * rows : (k + 1) * rows]


def finish_columns(main, taps, got, divisor):
    rows, channel_count = main.shape
    height = channel_count + channel_count // rows * taps.shape[0]
    return pl.pallas_call(
        functools.partial(finish_columns_kernel, float(divisor)),
        out_shape=jax.ShapeDtypeStruct((1, height, rows), jnp.bfloat16),
        in_specs=vmem_specs(3),
        out_specs=pl.BlockSpec(memory_space=pltpu.VMEM),
        compiler_params=pltpu.CompilerParams(vmem_limit_bytes=4 << 20),
        cost_estimate=pl.CostEstimate(flops=main.size, bytes_accessed=1 << 18, transcendentals=0),
        name="finish_columns",
    )(main, taps, got)


def sum_over_mesh(lead, trail, divisor, block, inner, outer, width):
    (lead_stages, lead_halved), (stages, halved) = sum_stages()
    dim_of = {"lat": 1, "lon": 2}
    for k, (axis, bit) in enumerate(stages):
        dim = dim_of[axis]
        stage = lead_stages[k]
        lead, _, _, _ = exchange(
            lead, *stage, stage in lead_halved, sent_type(stage, lead_stages, lead_halved)
        )
        rider = jnp.stack(edges(block, axis, dim, width)) if bit == 1 else outer
        trail, got, sent, raw = exchange(
            trail, axis, bit, (axis, bit) in halved, sent_type((axis, bit), stages, halved), rider
        )
        lead = after(lead, sent)
        if bit == 1:
            inner, outer = got[0], got[1]
        else:
            outer = jnp.where(carried(axis, bit), got, outer)
        if k + 1 == len(stages) or stages[k + 1][0] != axis:
            if axis == "lat":
                outer = inside(outer, axis)
            block = with_edges(block, inner, outer, axis, dim)
    lead = [(total_of(terms) / divisor).astype(jnp.bfloat16) for terms in lead]
    return lead, finish_columns(trail[0][0], trail[1][0], raw, divisor), block


lane_count = 128
kernel_side = 7
gain_row = kernel_side * kernel_side
scale_row = gain_row + 1


def spread(padded_ref, wide):
    batch_size, rows, cols, channel_count = padded_ref.shape
    for group in range(channel_count // lane_count):
        lanes = slice(group * lane_count, (group + 1) * lane_count)
        for b in range(batch_size):
            wide[group, b, :, :cols, :] = padded_ref[b, :, :, lanes].astype(jnp.float32)


def stencil(wide, params, group, b, rows, tile_cols, used, first, flipped):
    lanes = slice(group * lane_count, (group + 1) * lane_count)
    rows = list(rows)
    for q in range(kernel_side):
        for r in used:
            shifted = wide[group, b, r - first, q : q + tile_cols, :]
            for i in range(max(0, r - kernel_side + 1), min(len(rows), r + 1)):
                p = r - i
                tap = (kernel_side - 1 - p, kernel_side - 1 - q) if flipped else (p, q)
                term = params[pl.ds(tap[0] * kernel_side + tap[1], 1), lanes] * shifted
                rows[i] = term if rows[i] is None else rows[i] + term
    return rows


def conv_own_kernel(block_ref, params_ref, _w_in_ref, _w_out_ref, out_ref, wide):
    batch_size, tile_rows, pad_cols, _ = block_ref.shape
    tile_cols = pad_cols - kernel_side + 1
    first = kernel_side // 2
    spread(block_ref, wide)
    for group in range(wide.shape[0]):
        for b in range(batch_size):
            rows = stencil(
                wide, params_ref, group, b, [None] * tile_rows, tile_cols,
                range(first, first + tile_rows), first, False,
            )
            for i, row in enumerate(rows):
                at = (b * tile_rows + i) * tile_cols
                out_ref[group, at : at + tile_cols, :] = row


def conv_own(block, params, w_in, w_out):
    batch_size, tile_rows, pad_cols, channel_count = block.shape
    cells = batch_size * tile_rows * (pad_cols - kernel_side + 1)
    groups = channel_count // lane_count
    return pl.pallas_call(
        conv_own_kernel,
        out_shape=jax.ShapeDtypeStruct((groups, cells, lane_count), jnp.float32),
        in_specs=vmem_specs(4),
        out_specs=pl.BlockSpec(memory_space=pltpu.VMEM),
        scratch_shapes=[
            pltpu.VMEM((groups, batch_size, tile_rows, round_up(pad_cols, 8), lane_count), jnp.float32)
        ],
        compiler_params=pltpu.CompilerParams(vmem_limit_bytes=6 << 20),
        cost_estimate=pl.CostEstimate(flops=64 * cells * channel_count, bytes_accessed=1 << 20, transcendentals=0),
        name="conv_own",
    )(block, params, w_in, w_out)


def conv_norm_kernel(own_ref, padded_ref, params_ref, normed_ref, unit_ref, inv_ref, wide, smooth):
    batch_size, pad_rows, pad_cols, channel_count = padded_ref.shape
    cells = smooth.shape[1]
    tile_rows = pad_rows - kernel_side + 1
    tile_cols = pad_cols - kernel_side + 1
    spread(padded_ref, wide)
    first = kernel_side // 2
    used = [r for r in range(pad_rows) if r < first or r >= first + tile_rows]
    for group in range(wide.shape[0]):
        for b in range(batch_size):
            places = [
                slice(at, at + tile_cols)
                for at in range(b * tile_rows * tile_cols, (b + 1) * tile_rows * tile_cols, tile_cols)
            ]
            rows = [own_ref[group, at, :] for at in places]
            rows = stencil(wide, params_ref, group, b, rows, tile_cols, used, 0, False)
            for at, row in zip(places, rows):
                smooth[group, at, :] = row
    gain = params_ref[gain_row : gain_row + 1, :]
    block = 32

    def norm(step, _):
        at = pl.ds(pl.multiple_of(step * block, block), block)
        values = jnp.concatenate([smooth[g, at, :] for g in range(wide.shape[0])], axis=1)
        average = jnp.mean(values, axis=-1, keepdims=True)
        centred = values - average
        variance = jnp.mean(centred * centred, axis=-1, keepdims=True)
        inv_std = lax.rsqrt(variance + norm_eps)
        unit = centred * inv_std
        unit_ref[at, :] = unit
        inv_ref[at, :] = inv_std
        normed_ref[at, :] = (unit * gain).astype(jnp.bfloat16)
        return 0

    lax.fori_loop(0, cells // block, norm, 0, unroll=True)


def round_up(value, unit):
    return -(-value // unit) * unit


def conv_norm(own, padded, params):
    batch_size, pad_rows, pad_cols, channel_count = padded.shape
    cells = batch_size * (pad_rows - kernel_side + 1) * (pad_cols - kernel_side + 1)
    groups = channel_count // lane_count
    return pl.pallas_call(
        conv_norm_kernel,
        out_shape=(
            jax.ShapeDtypeStruct((cells, channel_count), jnp.bfloat16),
            jax.ShapeDtypeStruct((cells, channel_count), jnp.float32),
            jax.ShapeDtypeStruct((cells, 1), jnp.float32),
        ),
        scratch_shapes=[
            pltpu.VMEM((groups, batch_size, pad_rows, round_up(pad_cols, 8), lane_count), jnp.float32),
            pltpu.VMEM((groups, cells, lane_count), jnp.float32),
        ],
        compiler_params=pltpu.CompilerParams(vmem_limit_bytes=6 << 20),
        cost_estimate=pl.CostEstimate(flops=2 * 49 * cells * channel_count, bytes_accessed=1 << 20, transcendentals=0),
        name="conv_norm",
    )(own, padded, params)


def conv_back_kernel(padded_ref, params_ref, misfit_ref, _, out_ref, mark_ref, wide):
    mark_ref[...] = jnp.zeros_like(mark_ref)
    batch_size, tile_rows, tile_cols, channel_count = out_ref.shape
    spread(padded_ref, wide)
    for group in range(wide.shape[0]):
        lanes = slice(group * lane_count, (group + 1) * lane_count)

        def one(b, _):
            rows = stencil(
                wide, params_ref, group, b, [None] * tile_rows, tile_cols,
                range(wide.shape[2]), 0, True,
            )
            for i, row in enumerate(rows):
                out_ref[b, i, :, lanes] = (misfit_ref[b, i, :, lanes] + row).astype(out_ref.dtype)
            return 0

        for b in range(batch_size):
            one(b, 0)


def conv_back(padded, params, misfit, earlier):
    batch_size, pad_rows, pad_cols, channel_count = padded.shape
    groups = channel_count // lane_count
    return pl.pallas_call(
        conv_back_kernel,
        out_shape=(jax.ShapeDtypeStruct(misfit.shape, jnp.bfloat16), mark_shape),
        in_specs=vmem_specs(3) + [pl.BlockSpec(memory_space=pl.ANY)],
        out_specs=vmem_specs(2),
        scratch_shapes=[
            pltpu.VMEM((groups, batch_size, pad_rows, round_up(pad_cols, 8), lane_count), jnp.float32),
        ],
        compiler_params=pltpu.CompilerParams(vmem_limit_bytes=6 << 20),
        cost_estimate=pl.CostEstimate(flops=2 * 49 * misfit.size, bytes_accessed=1 << 20, transcendentals=0),
        name="conv_back",
    )(padded, params, misfit, earlier)


def tap_sums_kernel(padded_ref, grad_ref, out_ref, wide, partial):
    batch_size, tile_rows, tile_cols, channel_count = grad_ref.shape
    kernel_size = padded_ref.shape[1] - tile_rows + 1
    spread(padded_ref, wide)
    out_ref[...] = jnp.zeros_like(out_ref)
    for group in range(wide.shape[0]):
        lanes = slice(group * lane_count, (group + 1) * lane_count)

        def one(b, _):
            grads = [grad_ref[b, i, :, lanes].astype(jnp.float32) for i in range(tile_rows)]
            for q in range(kernel_size):
                sums = [None] * kernel_size
                for r in range(tile_rows + kernel_size - 1):
                    shifted = wide[group, b, r, q : q + tile_cols, :]
                    for i in range(max(0, r - kernel_size + 1), min(tile_rows, r + 1)):
                        product = shifted * grads[i]
                        term = product.reshape(tile_cols // 8, 8, lane_count).sum(axis=0)
                        p = r - i
                        sums[p] = term if sums[p] is None else sums[p] + term
                for p in range(kernel_size):
                    at = pl.ds((p * kernel_size + q) * 8, 8)
                    partial[group, b, at, :] = sums[p]
            return 0

        for b in range(batch_size):
            one(b, 0)
        taps = kernel_size * kernel_size
        total = partial[group, 0]
        for b in range(1, batch_size):
            total = total + partial[group, b]
        out_ref[:taps, lanes] = total.reshape(taps, 8, lane_count).sum(axis=1)


def tap_sums(padded, grads, row_count):
    batch_size, pad_rows, pad_cols, channel_count = padded.shape
    kernel_size = pad_rows - grads.shape[1] + 1
    groups = channel_count // lane_count
    return pl.pallas_call(
        tap_sums_kernel,
        out_shape=jax.ShapeDtypeStruct((row_count, channel_count), jnp.float32),
        scratch_shapes=[
            pltpu.VMEM((groups, batch_size, pad_rows, round_up(pad_cols, 8), lane_count), jnp.float32),
            pltpu.VMEM((groups, batch_size, kernel_size * kernel_size * 8, lane_count), jnp.float32),
        ],
        compiler_params=pltpu.CompilerParams(vmem_limit_bytes=6 << 20),
        cost_estimate=pl.CostEstimate(flops=2 * 49 * grads.size, bytes_accessed=1 << 20, transcendentals=0),
        name="tap_sums",
    )(padded, grads)


def assemble_rows_kernel(side_ref, mine, got, _, out_ref, mark_ref):
    mark_ref[...] = jnp.zeros_like(mark_ref)
    own = pl.program_id(0) == side_ref[0]
    count, rows, _ = mine.shape
    for k in range(count):
        chunk = jnp.where(own, mine[k].astype(jnp.float32), got[k].astype(jnp.float32))
        out_ref[k * rows : (k + 1) * rows, :] = chunk


def assemble_columns_kernel(side_ref, mine, got, out_ref, taps_ref):
    half = pl.program_id(0)
    own = half == side_ref[0]
    count, _, cols = mine.shape
    channel_count = out_ref.shape[0]
    for k in range(count):
        chunk = jnp.where(
            own,
            mine[k, :channel_count].astype(jnp.float32),
            got[k, :channel_count].astype(jnp.float32),
        )
        out_ref[:, k * cols : (k + 1) * cols] = chunk

    @pl.when(half == 0)
    def _():
        tail = slice(channel_count, mine.shape[1])
        chunks = mine[:, tail].astype(jnp.float32) + got[:, tail].astype(jnp.float32)
        groups = channel_count // cols
        step = chunks.shape[1] // groups
        pieces = [
            jnp.concatenate([chunks[k, n * step : (n + 1) * step] for n in range(groups)], axis=1)
            for k in range(count)
        ]
        taps = jnp.concatenate(pieces, axis=0)
        width = taps_ref.shape[1]
        for p in range(taps_ref.shape[0]):
            taps_ref[p] = taps[p * width : (p + 1) * width]


mark_shape = jax.ShapeDtypeStruct((8, 128), jnp.float32)


def whole_block(value):
    return pl.BlockSpec(value.shape, lambda i: (0,) * len(value.shape))


def assemble_rows(side, mine, got, earlier):
    count, rows, cols = mine.shape
    return pl.pallas_call(
        assemble_rows_kernel,
        grid=(2,),
        in_specs=[pl.BlockSpec(memory_space=pltpu.SMEM), whole_block(mine), whole_block(got)]
        + [pl.BlockSpec(memory_space=pl.ANY)],
        out_specs=(pl.BlockSpec((count * rows, cols), lambda i: (i, 0)), whole_block(mark_shape)),
        out_shape=(jax.ShapeDtypeStruct((2 * count * rows, cols), jnp.float32), mark_shape),
        compiler_params=pltpu.CompilerParams(vmem_limit_bytes=6 << 20),
        cost_estimate=pl.CostEstimate(flops=0, bytes_accessed=3 << 19, transcendentals=0),
        name="assemble_rows",
    )(side, mine, got, earlier)


def assemble_columns(side, mine, got, channel_count):
    count, _, cols = mine.shape
    return pl.pallas_call(
        assemble_columns_kernel,
        grid=(2,),
        in_specs=[pl.BlockSpec(memory_space=pltpu.SMEM), whole_block(mine), whole_block(got)],
        out_specs=(
            pl.BlockSpec((channel_count, count * cols), lambda i: (0, i)),
            pl.BlockSpec((kernel_side, kernel_side, channel_count), lambda i: (0, 0, 0)),
        ),
        out_shape=(
            jax.ShapeDtypeStruct((channel_count, 2 * count * cols), jnp.float32),
            jax.ShapeDtypeStruct((kernel_side, kernel_side, channel_count), jnp.float32),
        ),
        compiler_params=pltpu.CompilerParams(vmem_limit_bytes=6 << 20),
        cost_estimate=pl.CostEstimate(flops=0, bytes_accessed=3 << 19, transcendentals=0),
        name="assemble_columns",
    )(side, mine, got)


block_cols = 256


def product(left, right, left_dim, right_dim):
    return lax.dot_general(
        left, right, (((left_dim,), (right_dim,)), ((), ())), preferred_element_type=jnp.float32
    )


def half_columns(ref, half):
    count = ref.shape[1] // 2
    return ref[:, pl.ds(pl.multiple_of(half * count, count), count)]


def forward_kernel(
    side_ref, normed_ref, student_ref, target_ref, w_in_ref, w_out_ref, params_ref,
    slope_ref, misfit_ref, out_grad_ref, sent_ref, kept_ref, hidden,
):
    cells, hidden_size = slope_ref.shape
    scale = params_ref[scale_row : scale_row + 1, :]
    rows = 16
    mlp_out = None
    for k in range(0, hidden_size, block_cols):
        cols = slice(k, k + block_cols)
        slope_ref[:, cols] = product(normed_ref[...], w_in_ref[:, cols], 1, 0)
        for r in range(0, cells, rows):
            at = slice(r, r + rows)
            values = slope_ref[at, cols]
            squares = values * values
            tangent = jnp.tanh(values * (slope_coef + slope_coef * cubic_coef * squares))
            gate = 0.5 + 0.5 * tangent
            bend = (0.5 - 0.5 * (tangent * tangent)) * (
                slope_coef + 3.0 * slope_coef * cubic_coef * squares
            )
            hidden[at, cols] = (values * gate).astype(jnp.bfloat16)
            slope_ref[at, cols] = gate + values * bend
        part = product(hidden[:, cols], w_out_ref[cols, :], 1, 0)
        mlp_out = part if mlp_out is None else mlp_out + part
    misfit = student_ref[...].astype(jnp.float32) + scale * mlp_out
    misfit = misfit - target_ref[...].astype(jnp.float32)
    misfit_ref[...] = misfit
    out_grad_ref[...] = (scale * misfit).astype(jnp.bfloat16)
    side = side_ref[0]
    sent_ref[...] = product(half_columns(hidden, 1 - side), out_grad_ref[...], 0, 0).astype(
        jnp.bfloat16
    )
    kept_ref[...] = product(half_columns(hidden, side), out_grad_ref[...], 0, 0)


def vmem_specs(count):
    return [pl.BlockSpec(memory_space=pltpu.VMEM)] * count


def backward_kernel(
    side_ref, slope_ref, out_grad_ref, normed_ref, unit_ref, inv_ref, w_in_ref, w_out_ref, params_ref,
    conv_grad_ref, sent_ref, kept_ref, preact_grad,
):
    cells, hidden_size = slope_ref.shape
    normed_grad = None
    for k in range(0, hidden_size, block_cols):
        cols = slice(k, k + block_cols)
        hidden_grad = product(out_grad_ref[...], w_out_ref[cols, :], 1, 1)
        preact_grad[:, cols] = (hidden_grad * slope_ref[:, cols]).astype(jnp.bfloat16)
        part = product(preact_grad[:, cols], w_in_ref[:, cols], 1, 1)
        normed_grad = part if normed_grad is None else normed_grad + part
    unit_grad = normed_grad * params_ref[gain_row : gain_row + 1, :]
    unit = unit_ref[...]
    first_mean = jnp.mean(unit_grad, axis=-1, keepdims=True)
    second_mean = jnp.mean(unit_grad * unit, axis=-1, keepdims=True)
    conv_grad_ref[...] = (inv_ref[...] * (unit_grad - first_mean - unit * second_mean)).astype(
        jnp.bfloat16
    )
    side = side_ref[0]
    sent_ref[...] = product(half_columns(preact_grad, 1 - side), normed_ref[...], 0, 0).astype(
        jnp.bfloat16
    )
    kept_ref[...] = product(half_columns(preact_grad, side), normed_ref[...], 0, 0)


def mlp_kernel(
    side_ref, normed_ref, unit_ref, inv_ref, student_ref, target_ref, w_in_ref, w_out_ref, params_ref,
    misfit_ref, conv_grad_ref, out_sent, out_kept, in_sent, in_kept,
    slope, out_grad, hidden, preact_grad,
):
    forward_kernel(
        side_ref, normed_ref, student_ref, target_ref, w_in_ref, w_out_ref, params_ref,
        slope, misfit_ref, out_grad, out_sent, out_kept, hidden,
    )
    backward_kernel(
        side_ref, slope, out_grad, normed_ref, unit_ref, inv_ref, w_in_ref, w_out_ref, params_ref,
        conv_grad_ref, in_sent, in_kept, preact_grad,
    )


def mlp(side, normed, unit_norm, inv_std, student, target, w_in, w_out, params):
    cells, channel_count = normed.shape
    hidden_size = w_in.shape[1]
    shape = jax.ShapeDtypeStruct
    halves = [
        shape((hidden_size // 2, channel_count), jnp.bfloat16),
        shape((hidden_size // 2, channel_count), jnp.float32),
    ]
    return pl.pallas_call(
        mlp_kernel,
        in_specs=[pl.BlockSpec(memory_space=pltpu.SMEM)] + vmem_specs(8),
        out_specs=vmem_specs(6),
        out_shape=[
            shape((cells, channel_count), jnp.float32),
            shape((cells, channel_count), jnp.bfloat16),
        ]
        + halves
        + halves,
        scratch_shapes=[
            pltpu.VMEM((cells, hidden_size), jnp.float32),
            pltpu.VMEM((cells, channel_count), jnp.bfloat16),
            pltpu.VMEM((cells, hidden_size), jnp.bfloat16),
            pltpu.VMEM((cells, hidden_size), jnp.bfloat16),
        ],
        compiler_params=pltpu.CompilerParams(vmem_limit_bytes=10 << 20),
        cost_estimate=pl.CostEstimate(
            flops=12 * cells * channel_count * hidden_size,
            bytes_accessed=4 << 20,
            transcendentals=cells * hidden_size,
        ),
        name="mlp",
    )(side, normed, unit_norm, inv_std, student, target, w_in, w_out, params)


def local(student, teacher, dw_weight, norm_gain, w_in, w_out, layer_scale):
    batch_size, tile_rows, tile_cols, channel_count = student.shape
    half_kernel = kernel_side // 2
    cell_total = batch_size * tile_rows * lax.axis_size("lat") * tile_cols * lax.axis_size("lon")
    tap_count = kernel_side * kernel_side
    params = jnp.concatenate(
        [dw_weight.reshape(tap_count, channel_count), norm_gain[None], layer_scale[None]]
    )
    to_inner, to_outer = edges(student, "lon", 2, half_kernel)
    from_outer = swap_outer(to_outer, "lon", True)
    from_inner = swap(to_inner, "lon", 1)
    teacher, params = after((teacher, params), (to_inner, to_outer))
    lon_padded = with_edges(student, from_inner, from_outer, "lon", 2)
    lon_padded = after(lon_padded, params)
    padded_bf = with_halo(lon_padded, "lat", 1, half_kernel, False)
    normed, unit_norm, inv_std = conv_norm(conv_own(lon_padded, params, w_in, w_out), padded_bf, params)
    target = to_bands(teacher, "lat")
    upper = lax.axis_index("lat") % 2
    side = upper.astype(jnp.int32).reshape(1)
    rows = lambda block: block.reshape(-1, channel_count)
    misfit, conv_grad, out_sent, kept_out, in_sent, kept_in = mlp(
        side, normed, unit_norm, inv_std, rows(student), rows(target), w_in, w_out, params
    )
    got_out, got_in = swap(out_sent, "lat", 1), swap(in_sent, "lat", 1)
    conv_grid = conv_grad.reshape(student.shape)
    inner, outer = [swap(edge, "lat", 1) for edge in edges(conv_grid, "lat", 1, half_kernel)]
    part_dw = tap_sums(padded_bf, conv_grid, round_up(tap_count, 64))
    (out_chunk,), in_chunk, padded_grad = sum_over_mesh(
        [[kept_out, got_out]],
        [[kept_in, got_in], [part_dw]],
        cell_total,
        conv_grid,
        inner,
        outer,
        half_kernel,
    )
    out_chunks, in_chunks = out_chunk[None], in_chunk
    (_, out_halved), (_, in_halved) = sum_stages()
    for out_stage, in_stage in zip(out_halved[::-1], in_halved[::-1]):
        out_chunks = gather_halves(out_chunks, *out_stage)
        in_mine, in_got = in_chunks, swap(in_chunks, *in_stage)
        if in_stage != in_halved[0]:
            in_chunks = in_order(in_mine, in_got, *in_stage)
    grad_student, mark = conv_back(padded_grad, params, misfit.reshape(student.shape), in_chunk)
    sum_out, mark = assemble_rows(side, out_chunks, swap(out_chunks, "lat", 1), mark)
    axis, bit = in_halved[0]
    place = ((lax.axis_index(axis) // bit) % 2).astype(jnp.int32).reshape(1)
    in_chunks = join(place, in_mine, in_got, mark)
    sum_in, sum_dw = assemble_columns(side, in_chunks, swap(in_chunks, "lat", 1), channel_count)
    return (grad_student, sum_in, sum_out, sum_dw)


def solution(mesh):
    placed = (
        P(None, "lat", "lon", None),
        P(None, None, ("lon", "lat"), None),
        P(),
        P(),
        P(),
        P(),
        P(),
    )
    return jax.shard_map(
        local,
        mesh=mesh,
        in_specs=placed,
        out_specs=(P(None, "lat", "lon", None), P(), P(), P()),
        check_vma=False,
    )
```

```python
import functools

import jax
import jax.numpy as jnp
from jax import lax
from jax.experimental import pallas as pl
from jax.experimental.pallas import tpu as pltpu
from jax.sharding import PartitionSpec as P

slope_coef = 0.7978845608028654
cubic_coef = 0.044715
norm_eps = 1e-06


def bits_of(axis):
    return [1 << k for k in range((lax.axis_size(axis) - 1).bit_length())]


def swap(value, axis, bit):
    return lax.ppermute(value, axis, [(i, i ^ bit) for i in range(lax.axis_size(axis))])


def edges(block, axis, dim, width):
    low = lax.slice_in_dim(block, 0, width, axis=dim)
    high = lax.slice_in_dim(block, block.shape[dim] - width, None, axis=dim)
    odd = lax.axis_index(axis) % 2 == 1
    return jnp.where(odd, low, high), jnp.where(odd, high, low)


def swap_outer(edge, axis, periodic):
    count = lax.axis_size(axis)
    pairs = [(i, (i + 1) % count) for i in range(1, count, 2)]
    got = lax.ppermute(edge, axis, pairs + [(j, i) for i, j in pairs])
    return got if periodic else inside(got, axis)


def inside(edge, axis):
    index = lax.axis_index(axis)
    at_end = (index == 0) | (index == lax.axis_size(axis) - 1)
    return jnp.where(at_end, jnp.zeros_like(edge), edge)


def with_edges(block, from_inner, from_outer, axis, dim):
    odd = lax.axis_index(axis) % 2 == 1
    before = jnp.where(odd, from_inner, from_outer)
    after = jnp.where(odd, from_outer, from_inner)
    return jnp.concatenate([before, block, after], axis=dim)


def with_halo(block, axis, dim, width, periodic):
    to_inner, to_outer = edges(block, axis, dim, width)
    from_outer = swap_outer(to_outer, axis, periodic)
    from_inner = swap(to_inner, axis, 1)
    return with_edges(block, from_inner, from_outer, axis, dim)


def to_bands(teacher, axis):
    batch_size, rows, cols, channel_count = teacher.shape
    band = rows // lax.axis_size(axis)
    state = teacher.reshape(batch_size, -1, band, 1, cols, channel_count)
    for bit in bits_of(axis)[::-1]:
        upper = (lax.axis_index(axis) // bit) % 2
        state = state.reshape(batch_size, 2, -1, *state.shape[2:])
        mine = lax.dynamic_index_in_dim(state, upper, axis=1, keepdims=False)
        got = swap(lax.dynamic_index_in_dim(state, 1 - upper, axis=1, keepdims=False), axis, bit)
        state = jnp.where(
            upper == 1, jnp.stack([got, mine], axis=4), jnp.stack([mine, got], axis=4)
        )
        state = state.reshape(batch_size, -1, band, 2 * state.shape[3], cols, channel_count)
    return state.reshape(batch_size, band, -1, channel_count)


def half_of(value, upper):
    count = value.shape[0] // 2
    return lax.dynamic_slice_in_dim(value, upper * count, count, axis=0)


def total_of(terms):
    total = terms[0].astype(jnp.float32)
    for term in terms[1:]:
        total = total + term.astype(jnp.float32)
    return total


def flat_rows(block):
    return block.reshape(-1, block.shape[-1])


def after(value, other):
    return lax.optimization_barrier((value, other))[0]


def exchange(parts, axis, bit, halved, sent_as, rider=None):
    upper = (lax.axis_index(axis) // bit) % 2
    if halved:
        give = [total_of([half_of(t, 1 - upper) for t in terms]) for terms in parts]
        keep = [total_of([half_of(t, upper) for t in terms]) for terms in parts]
    else:
        give = keep = [total_of(terms) for terms in parts]
    give = [value.astype(sent_as) for value in give]
    if not halved:
        keep = [value.astype(jnp.float32) for value in give]
    counts = [value.shape[0] for value in give]
    if rider is not None:
        give = give + [flat_rows(rider).astype(sent_as)]
        counts = counts + [give[-1].shape[0]]
    sent = jnp.concatenate(give, axis=0) if len(give) > 1 else give[0]
    raw = swap(sent, axis, bit)
    got = split_rows(raw, counts) if len(give) > 1 else [raw]
    parts = [[k, g] for k, g in zip(keep, got)]
    ridden = None if rider is None else got[-1].astype(rider.dtype).reshape(rider.shape)
    return parts, ridden, sent, raw


def split_rows(value, counts):
    pieces, start = [], 0
    for count in counts:
        pieces.append(lax.slice_in_dim(value, start, start + count, axis=0))
        start += count
    return pieces


def in_order(chunks, got, axis, bit):
    upper = (lax.axis_index(axis) // bit) % 2
    return jnp.where(
        upper == 1, jnp.concatenate([got, chunks]), jnp.concatenate([chunks, got])
    )


def gather_halves(chunks, axis, bit):
    return in_order(chunks, swap(chunks, axis, bit), axis, bit)


def join_kernel(place_ref, mine, got, _, out_ref):
    count = mine.shape[0]
    place = place_ref[0]
    out_ref[pl.ds(place * count, count)] = mine[...]
    out_ref[pl.ds((1 - place) * count, count)] = got[...]


def join(place, mine, got, earlier):
    shape = (2 * mine.shape[0],) + mine.shape[1:]
    return pl.pallas_call(
        join_kernel,
        in_specs=[pl.BlockSpec(memory_space=pltpu.SMEM)]
        + vmem_specs(2)
        + [pl.BlockSpec(memory_space=pl.ANY)],
        out_specs=pl.BlockSpec(memory_space=pltpu.VMEM),
        out_shape=jax.ShapeDtypeStruct(shape, mine.dtype),
        compiler_params=pltpu.CompilerParams(vmem_limit_bytes=4 << 20),
        cost_estimate=pl.CostEstimate(flops=0, bytes_accessed=1 << 18, transcendentals=0),
        name="join",
    )(place, mine, got, earlier)


def carried(axis, bit):
    index = lax.axis_index(axis)
    lower = index % bit // 2
    return lower == jnp.where(index % 2 == 0, 0, bit // 2 - 1)


def sum_stages():
    lat_stages = [("lat", bit) for bit in bits_of("lat")[1:]]
    lon_stages = [("lon", bit) for bit in bits_of("lon")]
    trail = lat_stages + lon_stages
    lead = lon_stages[1:3] + lat_stages + lon_stages[:1] + lon_stages[3:]
    return (lead, lead[:2]), (trail, [lat_stages[0], lon_stages[0]])


def sent_type(stage, stages, halved):
    return jnp.bfloat16 if stage in halved or stage == stages[-1] else jnp.float32


def finish_columns_kernel(divisor, main_ref, taps_ref, got_ref, out_ref):
    rows, channel_count = main_ref.shape
    tap_rows = taps_ref.shape[0]
    main = main_ref[...] + got_ref[:rows].astype(jnp.float32)
    out_ref[0, :channel_count] = (main / divisor).T.astype(jnp.bfloat16)
    taps = taps_ref[...] + got_ref[rows : rows + tap_rows].astype(jnp.float32)
    taps = (taps / divisor).astype(jnp.bfloat16)
    for k in range(channel_count // rows):
        at = channel_count + k * tap_rows
        out_ref[0, at : at + tap_rows] = taps[:, k * rows : (k + 1) * rows]


def finish_columns(main, taps, got, divisor):
    rows, channel_count = main.shape
    height = channel_count + channel_count // rows * taps.shape[0]
    return pl.pallas_call(
        functools.partial(finish_columns_kernel, float(divisor)),
        out_shape=jax.ShapeDtypeStruct((1, height, rows), jnp.bfloat16),
        in_specs=vmem_specs(3),
        out_specs=pl.BlockSpec(memory_space=pltpu.VMEM),
        compiler_params=pltpu.CompilerParams(vmem_limit_bytes=4 << 20),
        cost_estimate=pl.CostEstimate(flops=main.size, bytes_accessed=1 << 18, transcendentals=0),
        name="finish_columns",
    )(main, taps, got)


def sum_over_mesh(lead, trail, divisor, block, inner, outer, width):
    (lead_stages, lead_halved), (stages, halved) = sum_stages()
    dim_of = {"lat": 1, "lon": 2}
    for k, (axis, bit) in enumerate(stages):
        dim = dim_of[axis]
        stage = lead_stages[k]
        lead, _, _, _ = exchange(
            lead, *stage, stage in lead_halved, sent_type(stage, lead_stages, lead_halved)
        )
        rider = jnp.stack(edges(block, axis, dim, width)) if bit == 1 else outer
        trail, got, sent, raw = exchange(
            trail, axis, bit, (axis, bit) in halved, sent_type((axis, bit), stages, halved), rider
        )
        lead = after(lead, sent)
        if bit == 1:
            inner, outer = got[0], got[1]
        else:
            outer = jnp.where(carried(axis, bit), got, outer)
        if k + 1 == len(stages) or stages[k + 1][0] != axis:
            if axis == "lat":
                outer = inside(outer, axis)
            block = with_edges(block, inner, outer, axis, dim)
    lead = [(total_of(terms) / divisor).astype(jnp.bfloat16) for terms in lead]
    return lead, finish_columns(trail[0][0], trail[1][0], raw, divisor), block


lane_count = 128
kernel_side = 7
gain_row = kernel_side * kernel_side
scale_row = gain_row + 1


def spread(padded_ref, wide, used=None):
    batch_size, rows, cols, channel_count = padded_ref.shape
    for group in range(channel_count // lane_count):
        lanes = slice(group * lane_count, (group + 1) * lane_count)
        for b in range(batch_size):
            for r in range(rows) if used is None else used:
                wide[group, b, r, :cols, :] = padded_ref[b, r, :, lanes].astype(jnp.float32)


def stencil(wide, params, group, b, rows, tile_cols, used, first, flipped):
    lanes = slice(group * lane_count, (group + 1) * lane_count)
    rows = list(rows)
    for q in range(kernel_side):
        for r in used:
            shifted = wide[group, b, r - first, q : q + tile_cols, :]
            for i in range(max(0, r - kernel_side + 1), min(len(rows), r + 1)):
                p = r - i
                tap = (kernel_side - 1 - p, kernel_side - 1 - q) if flipped else (p, q)
                term = params[pl.ds(tap[0] * kernel_side + tap[1], 1), lanes] * shifted
                rows[i] = term if rows[i] is None else rows[i] + term
    return rows


def conv_own_kernel(block_ref, params_ref, _w_in_ref, _w_out_ref, out_ref, wide):
    batch_size, tile_rows, pad_cols, _ = block_ref.shape
    tile_cols = pad_cols - kernel_side + 1
    first = kernel_side // 2
    spread(block_ref, wide)
    for group in range(wide.shape[0]):
        for b in range(batch_size):
            rows = stencil(
                wide, params_ref, group, b, [None] * tile_rows, tile_cols,
                range(first, first + tile_rows), first, False,
            )
            for i, row in enumerate(rows):
                at = (b * tile_rows + i) * tile_cols
                out_ref[group, at : at + tile_cols, :] = row


def conv_own(block, params, w_in, w_out):
    batch_size, tile_rows, pad_cols, channel_count = block.shape
    cells = batch_size * tile_rows * (pad_cols - kernel_side + 1)
    groups = channel_count // lane_count
    return pl.pallas_call(
        conv_own_kernel,
        out_shape=jax.ShapeDtypeStruct((groups, cells, lane_count), jnp.float32),
        in_specs=vmem_specs(4),
        out_specs=pl.BlockSpec(memory_space=pltpu.VMEM),
        scratch_shapes=[
            pltpu.VMEM((groups, batch_size, tile_rows, round_up(pad_cols, 8), lane_count), jnp.float32)
        ],
        compiler_params=pltpu.CompilerParams(vmem_limit_bytes=6 << 20),
        cost_estimate=pl.CostEstimate(flops=64 * cells * channel_count, bytes_accessed=1 << 20, transcendentals=0),
        name="conv_own",
    )(block, params, w_in, w_out)


def conv_norm_kernel(own_ref, padded_ref, params_ref, normed_ref, unit_ref, inv_ref, wide, smooth):
    batch_size, pad_rows, pad_cols, channel_count = padded_ref.shape
    cells = smooth.shape[1]
    tile_rows = pad_rows - kernel_side + 1
    tile_cols = pad_cols - kernel_side + 1
    first = kernel_side // 2
    used = [r for r in range(pad_rows) if r < first or r >= first + tile_rows]
    spread(padded_ref, wide, used)
    for group in range(wide.shape[0]):
        for b in range(batch_size):
            places = [
                slice(at, at + tile_cols)
                for at in range(b * tile_rows * tile_cols, (b + 1) * tile_rows * tile_cols, tile_cols)
            ]
            rows = [own_ref[group, at, :] for at in places]
            rows = stencil(wide, params_ref, group, b, rows, tile_cols, used, 0, False)
            for at, row in zip(places, rows):
                smooth[group, at, :] = row
    gain = params_ref[gain_row : gain_row + 1, :]
    block = 32

    def norm(step, _):
        at = pl.ds(pl.multiple_of(step * block, block), block)
        values = jnp.concatenate([smooth[g, at, :] for g in range(wide.shape[0])], axis=1)
        average = jnp.mean(values, axis=-1, keepdims=True)
        centred = values - average
        variance = jnp.mean(centred * centred, axis=-1, keepdims=True)
        inv_std = lax.rsqrt(variance + norm_eps)
        unit = centred * inv_std
        unit_ref[at, :] = unit
        inv_ref[at, :] = inv_std
        normed_ref[at, :] = (unit * gain).astype(jnp.bfloat16)
        return 0

    lax.fori_loop(0, cells // block, norm, 0, unroll=True)


def round_up(value, unit):
    return -(-value // unit) * unit


def conv_norm(own, padded, params):
    batch_size, pad_rows, pad_cols, channel_count = padded.shape
    cells = batch_size * (pad_rows - kernel_side + 1) * (pad_cols - kernel_side + 1)
    groups = channel_count // lane_count
    return pl.pallas_call(
        conv_norm_kernel,
        out_shape=(
            jax.ShapeDtypeStruct((cells, channel_count), jnp.bfloat16),
            jax.ShapeDtypeStruct((cells, channel_count), jnp.float32),
            jax.ShapeDtypeStruct((cells, 1), jnp.float32),
        ),
        scratch_shapes=[
            pltpu.VMEM((groups, batch_size, pad_rows, round_up(pad_cols, 8), lane_count), jnp.float32),
            pltpu.VMEM((groups, cells, lane_count), jnp.float32),
        ],
        compiler_params=pltpu.CompilerParams(vmem_limit_bytes=6 << 20),
        cost_estimate=pl.CostEstimate(flops=2 * 49 * cells * channel_count, bytes_accessed=1 << 20, transcendentals=0),
        name="conv_norm",
    )(own, padded, params)


def conv_back_kernel(padded_ref, params_ref, misfit_ref, _, out_ref, mark_ref, wide):
    mark_ref[...] = jnp.zeros_like(mark_ref)
    batch_size, tile_rows, tile_cols, channel_count = out_ref.shape
    spread(padded_ref, wide)
    for group in range(wide.shape[0]):
        lanes = slice(group * lane_count, (group + 1) * lane_count)

        def one(b, _):
            rows = stencil(
                wide, params_ref, group, b, [None] * tile_rows, tile_cols,
                range(wide.shape[2]), 0, True,
            )
            for i, row in enumerate(rows):
                out_ref[b, i, :, lanes] = (misfit_ref[b, i, :, lanes] + row).astype(out_ref.dtype)
            return 0

        for b in range(batch_size):
            one(b, 0)


def conv_back(padded, params, misfit, earlier):
    batch_size, pad_rows, pad_cols, channel_count = padded.shape
    groups = channel_count // lane_count
    return pl.pallas_call(
        conv_back_kernel,
        out_shape=(jax.ShapeDtypeStruct(misfit.shape, jnp.bfloat16), mark_shape),
        in_specs=vmem_specs(3) + [pl.BlockSpec(memory_space=pl.ANY)],
        out_specs=vmem_specs(2),
        scratch_shapes=[
            pltpu.VMEM((groups, batch_size, pad_rows, round_up(pad_cols, 8), lane_count), jnp.float32),
        ],
        compiler_params=pltpu.CompilerParams(vmem_limit_bytes=6 << 20),
        cost_estimate=pl.CostEstimate(flops=2 * 49 * misfit.size, bytes_accessed=1 << 20, transcendentals=0),
        name="conv_back",
    )(padded, params, misfit, earlier)


def tap_sums_kernel(padded_ref, grad_ref, out_ref, wide, partial):
    batch_size, tile_rows, tile_cols, channel_count = grad_ref.shape
    kernel_size = padded_ref.shape[1] - tile_rows + 1
    spread(padded_ref, wide)
    out_ref[...] = jnp.zeros_like(out_ref)
    for group in range(wide.shape[0]):
        lanes = slice(group * lane_count, (group + 1) * lane_count)

        def one(b, _):
            grads = [grad_ref[b, i, :, lanes].astype(jnp.float32) for i in range(tile_rows)]
            for q in range(kernel_size):
                sums = [None] * kernel_size
                for r in range(tile_rows + kernel_size - 1):
                    shifted = wide[group, b, r, q : q + tile_cols, :]
                    for i in range(max(0, r - kernel_size + 1), min(tile_rows, r + 1)):
                        product = shifted * grads[i]
                        term = product.reshape(tile_cols // 8, 8, lane_count).sum(axis=0)
                        p = r - i
                        sums[p] = term if sums[p] is None else sums[p] + term
                for p in range(kernel_size):
                    at = pl.ds((p * kernel_size + q) * 8, 8)
                    partial[group, b, at, :] = sums[p]
            return 0

        for b in range(batch_size):
            one(b, 0)
        taps = kernel_size * kernel_size
        total = partial[group, 0]
        for b in range(1, batch_size):
            total = total + partial[group, b]
        out_ref[:taps, lanes] = total.reshape(taps, 8, lane_count).sum(axis=1)


def tap_sums(padded, grads, row_count):
    batch_size, pad_rows, pad_cols, channel_count = padded.shape
    kernel_size = pad_rows - grads.shape[1] + 1
    groups = channel_count // lane_count
    return pl.pallas_call(
        tap_sums_kernel,
        out_shape=jax.ShapeDtypeStruct((row_count, channel_count), jnp.float32),
        scratch_shapes=[
            pltpu.VMEM((groups, batch_size, pad_rows, round_up(pad_cols, 8), lane_count), jnp.float32),
            pltpu.VMEM((groups, batch_size, kernel_size * kernel_size * 8, lane_count), jnp.float32),
        ],
        compiler_params=pltpu.CompilerParams(vmem_limit_bytes=6 << 20),
        cost_estimate=pl.CostEstimate(flops=2 * 49 * grads.size, bytes_accessed=1 << 20, transcendentals=0),
        name="tap_sums",
    )(padded, grads)


def assemble_rows_kernel(side_ref, mine, got, _, out_ref, mark_ref):
    mark_ref[...] = jnp.zeros_like(mark_ref)
    own = pl.program_id(0) == side_ref[0]
    count, rows, _ = mine.shape
    for k in range(count):
        chunk = jnp.where(own, mine[k].astype(jnp.float32), got[k].astype(jnp.float32))
        out_ref[k * rows : (k + 1) * rows, :] = chunk


def assemble_columns_kernel(side_ref, mine, got, out_ref, taps_ref):
    half = pl.program_id(0)
    own = half == side_ref[0]
    count, _, cols = mine.shape
    channel_count = out_ref.shape[0]
    for k in range(count):
        chunk = jnp.where(
            own,
            mine[k, :channel_count].astype(jnp.float32),
            got[k, :channel_count].astype(jnp.float32),
        )
        out_ref[:, k * cols : (k + 1) * cols] = chunk

    @pl.when(half == 0)
    def _():
        tail = slice(channel_count, mine.shape[1])
        chunks = mine[:, tail].astype(jnp.float32) + got[:, tail].astype(jnp.float32)
        groups = channel_count // cols
        step = chunks.shape[1] // groups
        pieces = [
            jnp.concatenate([chunks[k, n * step : (n + 1) * step] for n in range(groups)], axis=1)
            for k in range(count)
        ]
        taps = jnp.concatenate(pieces, axis=0)
        width = taps_ref.shape[1]
        for p in range(taps_ref.shape[0]):
            taps_ref[p] = taps[p * width : (p + 1) * width]


mark_shape = jax.ShapeDtypeStruct((8, 128), jnp.float32)


def whole_block(value):
    return pl.BlockSpec(value.shape, lambda i: (0,) * len(value.shape))


def assemble_rows(side, mine, got, earlier):
    count, rows, cols = mine.shape
    return pl.pallas_call(
        assemble_rows_kernel,
        grid=(2,),
        in_specs=[pl.BlockSpec(memory_space=pltpu.SMEM), whole_block(mine), whole_block(got)]
        + [pl.BlockSpec(memory_space=pl.ANY)],
        out_specs=(pl.BlockSpec((count * rows, cols), lambda i: (i, 0)), whole_block(mark_shape)),
        out_shape=(jax.ShapeDtypeStruct((2 * count * rows, cols), jnp.float32), mark_shape),
        compiler_params=pltpu.CompilerParams(vmem_limit_bytes=6 << 20),
        cost_estimate=pl.CostEstimate(flops=0, bytes_accessed=3 << 19, transcendentals=0),
        name="assemble_rows",
    )(side, mine, got, earlier)


def assemble_columns(side, mine, got, channel_count):
    count, _, cols = mine.shape
    return pl.pallas_call(
        assemble_columns_kernel,
        grid=(2,),
        in_specs=[pl.BlockSpec(memory_space=pltpu.SMEM), whole_block(mine), whole_block(got)],
        out_specs=(
            pl.BlockSpec((channel_count, count * cols), lambda i: (0, i)),
            pl.BlockSpec((kernel_side, kernel_side, channel_count), lambda i: (0, 0, 0)),
        ),
        out_shape=(
            jax.ShapeDtypeStruct((channel_count, 2 * count * cols), jnp.float32),
            jax.ShapeDtypeStruct((kernel_side, kernel_side, channel_count), jnp.float32),
        ),
        compiler_params=pltpu.CompilerParams(vmem_limit_bytes=6 << 20),
        cost_estimate=pl.CostEstimate(flops=0, bytes_accessed=3 << 19, transcendentals=0),
        name="assemble_columns",
    )(side, mine, got)


block_cols = 256


def product(left, right, left_dim, right_dim):
    return lax.dot_general(
        left, right, (((left_dim,), (right_dim,)), ((), ())), preferred_element_type=jnp.float32
    )


def half_columns(ref, half):
    count = ref.shape[1] // 2
    return ref[:, pl.ds(pl.multiple_of(half * count, count), count)]


def forward_kernel(
    side_ref, normed_ref, student_ref, target_ref, w_in_ref, w_out_ref, params_ref,
    slope_ref, misfit_ref, out_grad_ref, sent_ref, kept_ref, hidden,
):
    cells, hidden_size = slope_ref.shape
    scale = params_ref[scale_row : scale_row + 1, :]
    rows = 16
    mlp_out = None
    for k in range(0, hidden_size, block_cols):
        cols = slice(k, k + block_cols)
        slope_ref[:, cols] = product(normed_ref[...], w_in_ref[:, cols], 1, 0)
        for r in range(0, cells, rows):
            at = slice(r, r + rows)
            values = slope_ref[at, cols]
            squares = values * values
            tangent = jnp.tanh(values * (slope_coef + slope_coef * cubic_coef * squares))
            gate = 0.5 + 0.5 * tangent
            bend = (0.5 - 0.5 * (tangent * tangent)) * (
                slope_coef + 3.0 * slope_coef * cubic_coef * squares
            )
            hidden[at, cols] = (values * gate).astype(jnp.bfloat16)
            slope_ref[at, cols] = gate + values * bend
        part = product(hidden[:, cols], w_out_ref[cols, :], 1, 0)
        mlp_out = part if mlp_out is None else mlp_out + part
    misfit = student_ref[...].astype(jnp.float32) + scale * mlp_out
    misfit = misfit - target_ref[...].astype(jnp.float32)
    misfit_ref[...] = misfit
    out_grad_ref[...] = (scale * misfit).astype(jnp.bfloat16)
    side = side_ref[0]
    sent_ref[...] = product(half_columns(hidden, 1 - side), out_grad_ref[...], 0, 0).astype(
        jnp.bfloat16
    )
    kept_ref[...] = product(half_columns(hidden, side), out_grad_ref[...], 0, 0)


def vmem_specs(count):
    return [pl.BlockSpec(memory_space=pltpu.VMEM)] * count


def backward_kernel(
    side_ref, slope_ref, out_grad_ref, normed_ref, unit_ref, inv_ref, w_in_ref, w_out_ref, params_ref,
    conv_grad_ref, sent_ref, kept_ref, preact_grad,
):
    cells, hidden_size = slope_ref.shape
    normed_grad = None
    for k in range(0, hidden_size, block_cols):
        cols = slice(k, k + block_cols)
        hidden_grad = product(out_grad_ref[...], w_out_ref[cols, :], 1, 1)
        preact_grad[:, cols] = (hidden_grad * slope_ref[:, cols]).astype(jnp.bfloat16)
        part = product(preact_grad[:, cols], w_in_ref[:, cols], 1, 1)
        normed_grad = part if normed_grad is None else normed_grad + part
    unit_grad = normed_grad * params_ref[gain_row : gain_row + 1, :]
    unit = unit_ref[...]
    first_mean = jnp.mean(unit_grad, axis=-1, keepdims=True)
    second_mean = jnp.mean(unit_grad * unit, axis=-1, keepdims=True)
    conv_grad_ref[...] = (inv_ref[...] * (unit_grad - first_mean - unit * second_mean)).astype(
        jnp.bfloat16
    )
    side = side_ref[0]
    sent_ref[...] = product(half_columns(preact_grad, 1 - side), normed_ref[...], 0, 0).astype(
        jnp.bfloat16
    )
    kept_ref[...] = product(half_columns(preact_grad, side), normed_ref[...], 0, 0)


def mlp_kernel(
    side_ref, normed_ref, unit_ref, inv_ref, student_ref, target_ref, w_in_ref, w_out_ref, params_ref,
    misfit_ref, conv_grad_ref, out_sent, out_kept, in_sent, in_kept,
    slope, out_grad, hidden, preact_grad,
):
    forward_kernel(
        side_ref, normed_ref, student_ref, target_ref, w_in_ref, w_out_ref, params_ref,
        slope, misfit_ref, out_grad, out_sent, out_kept, hidden,
    )
    backward_kernel(
        side_ref, slope, out_grad, normed_ref, unit_ref, inv_ref, w_in_ref, w_out_ref, params_ref,
        conv_grad_ref, in_sent, in_kept, preact_grad,
    )


def mlp(side, normed, unit_norm, inv_std, student, target, w_in, w_out, params):
    cells, channel_count = normed.shape
    hidden_size = w_in.shape[1]
    shape = jax.ShapeDtypeStruct
    halves = [
        shape((hidden_size // 2, channel_count), jnp.bfloat16),
        shape((hidden_size // 2, channel_count), jnp.float32),
    ]
    return pl.pallas_call(
        mlp_kernel,
        in_specs=[pl.BlockSpec(memory_space=pltpu.SMEM)] + vmem_specs(8),
        out_specs=vmem_specs(6),
        out_shape=[
            shape((cells, channel_count), jnp.float32),
            shape((cells, channel_count), jnp.bfloat16),
        ]
        + halves
        + halves,
        scratch_shapes=[
            pltpu.VMEM((cells, hidden_size), jnp.float32),
            pltpu.VMEM((cells, channel_count), jnp.bfloat16),
            pltpu.VMEM((cells, hidden_size), jnp.bfloat16),
            pltpu.VMEM((cells, hidden_size), jnp.bfloat16),
        ],
        compiler_params=pltpu.CompilerParams(vmem_limit_bytes=10 << 20),
        cost_estimate=pl.CostEstimate(
            flops=12 * cells * channel_count * hidden_size,
            bytes_accessed=4 << 20,
            transcendentals=cells * hidden_size,
        ),
        name="mlp",
    )(side, normed, unit_norm, inv_std, student, target, w_in, w_out, params)


def local(student, teacher, dw_weight, norm_gain, w_in, w_out, layer_scale):
    batch_size, tile_rows, tile_cols, channel_count = student.shape
    half_kernel = kernel_side // 2
    cell_total = batch_size * tile_rows * lax.axis_size("lat") * tile_cols * lax.axis_size("lon")
    tap_count = kernel_side * kernel_side
    params = jnp.concatenate(
        [dw_weight.reshape(tap_count, channel_count), norm_gain[None], layer_scale[None]]
    )
    to_inner, to_outer = edges(student, "lon", 2, half_kernel)
    from_outer = swap_outer(to_outer, "lon", True)
    from_inner = swap(to_inner, "lon", 1)
    teacher, params = after((teacher, params), (to_inner, to_outer))
    lon_padded = with_edges(student, from_inner, from_outer, "lon", 2)
    lon_padded = after(lon_padded, params)
    padded_bf = with_halo(lon_padded, "lat", 1, half_kernel, False)
    normed, unit_norm, inv_std = conv_norm(conv_own(lon_padded, params, w_in, w_out), padded_bf, params)
    target = to_bands(teacher, "lat")
    upper = lax.axis_index("lat") % 2
    side = upper.astype(jnp.int32).reshape(1)
    rows = lambda block: block.reshape(-1, channel_count)
    misfit, conv_grad, out_sent, kept_out, in_sent, kept_in = mlp(
        side, normed, unit_norm, inv_std, rows(student), rows(target), w_in, w_out, params
    )
    got_out, got_in = swap(out_sent, "lat", 1), swap(in_sent, "lat", 1)
    conv_grid = conv_grad.reshape(student.shape)
    inner, outer = [swap(edge, "lat", 1) for edge in edges(conv_grid, "lat", 1, half_kernel)]
    part_dw = tap_sums(padded_bf, conv_grid, round_up(tap_count, 64))
    (out_chunk,), in_chunk, padded_grad = sum_over_mesh(
        [[kept_out, got_out]],
        [[kept_in, got_in], [part_dw]],
        cell_total,
        conv_grid,
        inner,
        outer,
        half_kernel,
    )
    out_chunks, in_chunks = out_chunk[None], in_chunk
    (_, out_halved), (_, in_halved) = sum_stages()
    for out_stage, in_stage in zip(out_halved[::-1], in_halved[::-1]):
        out_chunks = gather_halves(out_chunks, *out_stage)
        in_mine, in_got = in_chunks, swap(in_chunks, *in_stage)
        if in_stage != in_halved[0]:
            in_chunks = in_order(in_mine, in_got, *in_stage)
    grad_student, mark = conv_back(padded_grad, params, misfit.reshape(student.shape), in_chunk)
    sum_out, mark = assemble_rows(side, out_chunks, swap(out_chunks, "lat", 1), mark)
    axis, bit = in_halved[0]
    place = ((lax.axis_index(axis) // bit) % 2).astype(jnp.int32).reshape(1)
    in_chunks = join(place, in_mine, in_got, mark)
    sum_in, sum_dw = assemble_columns(side, in_chunks, swap(in_chunks, "lat", 1), channel_count)
    return (grad_student, sum_in, sum_out, sum_dw)


def solution(mesh):
    placed = (
        P(None, "lat", "lon", None),
        P(None, None, ("lon", "lat"), None),
        P(),
        P(),
        P(),
        P(),
        P(),
    )
    return jax.shard_map(
        local,
        mesh=mesh,
        in_specs=placed,
        out_specs=(P(None, "lat", "lon", None), P(), P(), P()),
        check_vma=False,
    )
```
